32 devices in a mesh: gx: 4 (over z), gy: 8 (over y, x, core).
Axes of the slice: x: 2, y: 2, z: 4, core: 2. Of those that a mesh axis runs over, the one named last changes fastest.
Arguments:
- speed_factor: float32 [64, 128, 256], P('gx', 'gy'), may hold values from 0.05 to 0.17
- wave_before: float32 [64, 128, 256], P('gx', 'gy'), may hold values from -6 to 6
- wave_now: float32 [64, 128, 256], P('gx', 'gy'), may hold values from -6 to 6
- source_accel: float32 [2, 64, 128, 256], P(None, 'gx', 'gy'), may hold values from -4 to 4
- prior_image: float32 [64, 128, 256], P('gx', 'gy'), may hold values from -40 to 40
- conv_first: bfloat16 [27, 1, 8], replicated, may hold values from -1.25 to 1.25
- bias_first: float32 [8], replicated, may hold values from -3 to 3
- conv_middle: bfloat16 [27, 8, 8], replicated, may hold values from -0.4375 to 0.4375
- bias_middle: float32 [8], replicated, may hold values from -3 to 3
- conv_last: bfloat16 [27, 8, 1], replicated, may hold values from -0.4375 to 0.4375
Outputs:
- wave_next: float32 [64, 128, 256], P('gx', 'gy')
- wave_after: float32 [64, 128, 256], P('gx', 'gy')
- gradient: float32 [64, 128, 256], P('gx', 'gy')
- model_step: float32 [64, 128, 256], P('gx', 'gy')
The draws below stay inside these ranges and needn't reach their ends.
All inputs are finite; a program needn't handle non-finite values.
Results may differ from the reference program's by a relative error of at most 0.0059.
Values may be sent and summed in bfloat16 or wider, within the bound.
A program may use at most 192 MiB of HBM per device.

```python
import jax
import jax.numpy as jnp
from jax import lax

NZ = 256
CH = 8
NX = 64
NY = 128


def draw_prior_image(key, part):
    along_x = 1.0 + 2.0 * jnp.arange(NX, dtype=jnp.float32) / NX
    along_y = 1.0 + 2.0 * jnp.arange(NY, dtype=jnp.float32) / NY
    scale = along_x[:, None, None] * along_y[None, :, None]
    return scale * jnp.clip(jax.random.normal(key, (NX, NY, NZ), jnp.float32), -4.0, 4.0)


def block_scale(own_key, extent, pieces, smallest, top_value):
    gain = 1.0
    for position, parts in pieces:
        steps = jax.random.uniform(jax.random.fold_in(jax.random.fold_in(own_key, 6), position), (parts,), jnp.float32, smallest / len(pieces), top_value / len(pieces))
        gain = gain * jnp.repeat(jnp.exp(steps), extent[position] // parts).reshape((-1,) + (1,) * (len(extent) - 1 - position))
    return gain


def gaussian(stream_key, shape, width, limit, shards=(), held_as=jnp.bfloat16):
    loudness = block_scale(stream_key, shape, shards, -0.22, 0.18) if shards else 1.0
    array = jax.random.normal(stream_key, shape, jnp.float32) * width * loudness
    return jnp.minimum(jnp.maximum(array, -limit), limit).astype(held_as)


def setup_inputs(seed: int = 0) -> dict:
    keys = jax.random.split(jax.random.key(seed), 11)
    speed_factor = jnp.clip(0.05 + 0.12000000104308128 * jax.random.uniform(keys[0], (NX, NY, NZ), jnp.float32) ** block_scale(keys[0], (NX, NY, NZ), ((0, 4), (1, 8)), -0.2, 0.2), 0.05, 0.17)
    wave_before = gaussian(keys[1], (NX, NY, NZ), 1.0, 6.0, ((0, 4), (1, 8)), jnp.float32)
    wave_now = gaussian(keys[2], (NX, NY, NZ), 1.0, 6.0, ((0, 4), (1, 8)), jnp.float32)
    source_accel = gaussian(keys[3], (2, NX, NY, NZ), 0.5, 4.0, ((1, 4), (2, 8)), jnp.float32)
    prior_image = draw_prior_image(jax.random.fold_in(keys[10], 71), 0)
    conv_first = gaussian(keys[5], (27, 1, CH), 27 ** -0.5, 1.25)
    bias_first = gaussian(keys[6], (CH,), 0.5, 3.0, (), jnp.float32)
    conv_middle = gaussian(keys[7], (27, CH, CH), (27 * CH) ** -0.5, 0.4375)
    bias_middle = gaussian(keys[8], (CH,), 0.5, 3.0, (), jnp.float32)
    conv_last = gaussian(keys[9], (27, CH, 1), (27 * CH) ** -0.5, 0.4375)
    return dict(speed_factor=speed_factor, wave_before=wave_before, wave_now=wave_now, source_accel=source_accel, prior_image=prior_image, conv_first=conv_first, bias_first=bias_first, conv_middle=conv_middle, bias_middle=bias_middle, conv_last=conv_last)


COEFS = (-205.0 / 72.0, 8.0 / 5.0, -1.0 / 5.0, 8.0 / 315.0, -1.0 / 560.0)


def laplace(field):
    padded = jnp.pad(field, 4)
    size_x, size_y, size_z = field.shape
    total = 3.0 * COEFS[0] * field
    for reach in range(1, 5):
        cycle = padded[4 + reach:4 + reach + size_x, 4:4 + size_y, 4:4 + size_z]
        cycle = cycle + padded[4 - reach:4 - reach + size_x, 4:4 + size_y, 4:4 + size_z]
        cycle = cycle + padded[4:4 + size_x, 4 + reach:4 + reach + size_y, 4:4 + size_z]
        cycle = cycle + padded[4:4 + size_x, 4 - reach:4 - reach + size_y, 4:4 + size_z]
        cycle = cycle + padded[4:4 + size_x, 4:4 + size_y, 4 + reach:4 + reach + size_z]
        cycle = cycle + padded[4:4 + size_x, 4:4 + size_y, 4 - reach:4 - reach + size_z]
        total = total + COEFS[reach] * cycle
    return total


def conv_layer(inputs, weight):
    kernel = weight.astype(jnp.float32).reshape(3, 3, 3, weight.shape[1], weight.shape[2])
    kernel = kernel.transpose(4, 3, 0, 1, 2)
    result = lax.conv_general_dilated(inputs.astype(jnp.float32)[None], kernel, (1, 1, 1), "SAME",
                                      dimension_numbers=("NCDHW", "OIDHW", "NCDHW"),
                                      precision=lax.Precision.HIGHEST)
    return result[0]


def reference(speed_factor, wave_before, wave_now, source_accel, prior_image, conv_first, bias_first, conv_middle, bias_middle, conv_last):
    wave_next = 2.0 * wave_now - wave_before + speed_factor * laplace(wave_now)
    wave_after = 2.0 * wave_next - wave_now + speed_factor * laplace(wave_next)
    gradient = prior_image + source_accel[0] * wave_next + source_accel[1] * wave_after
    layer_in = gradient.astype(jnp.bfloat16)[None]
    hidden_one = jnp.maximum(conv_layer(layer_in, conv_first) + bias_first[:, None, None, None], 0.0).astype(jnp.bfloat16)
    hidden_two = jnp.maximum(conv_layer(hidden_one, conv_middle) + bias_middle[:, None, None, None], 0.0).astype(jnp.bfloat16)
    direction = conv_layer(hidden_two, conv_last)[0] + gradient
    sum_gg = jnp.sum(gradient * gradient)
    sum_gd = jnp.sum(gradient * direction)
    sum_dd = jnp.sum(direction * direction)
    damping = 8.0 * float(NX * NY * NZ)
    model_step = (sum_gd / (sum_gg + sum_dd + damping)) * direction
    return wave_next, wave_after, gradient, model_step
```

```python
import functools

import jax
import jax.numpy as jnp
from jax import lax
from jax.experimental import pallas as pl
from jax.experimental.pallas import tpu as pltpu
from jax.sharding import PartitionSpec as P

COEFS = (-205.0 / 72.0, 8.0 / 5.0, -1.0 / 5.0, 8.0 / 315.0, -1.0 / 560.0)
MESH = pl.DeviceIdType.MESH
F32 = jnp.float32
BF16 = jnp.bfloat16
UNROLL = True
WAVE_UNROLL = 8


def shift_z(v, k):
    depth = v.shape[-1]
    lane = lax.broadcasted_iota(jnp.int32, v.shape, v.ndim - 1)
    rolled = pltpu.roll(v, (-k) % depth, v.ndim - 1)
    return jnp.where((lane + k >= 0) & (lane + k < depth), rolled, 0.0)


def iota(shape, dim):
    return lax.broadcasted_iota(jnp.int32, shape, dim)


def one_hot(hit):
    return jnp.where(hit, 1.0, 0.0).astype(BF16)


def third(index, size):
    return jnp.where(index >= size, 1, 0) + jnp.where(index >= 2 * size, 1, 0)


def laplace_z(center):
    total = 3.0 * COEFS[0] * center
    for k in range(1, 5):
        total = total + COEFS[k] * (shift_z(center, k) + shift_z(center, -k))
    return total


def laplace_xy(ext, x, ny):
    total = None
    for k in range(1, 5):
        cycle = ext[x + 4 + k, 8 : 8 + ny, :] + ext[x + 4 - k, 8 : 8 + ny, :]
        cycle = cycle + ext[x + 4, 8 + k : 8 + k + ny, :]
        cycle = cycle + ext[x + 4, 8 - k : 8 - k + ny, :]
        total = COEFS[k] * cycle if total is None else total + COEFS[k] * cycle
    return total


def kernel(
    n_gx,
    n_gy,
    speed_hbm,
    before_hbm,
    now_hbm,
    src_hbm,
    prior_hbm,
    first_hbm,
    mid_hbm,
    last_hbm,
    bias1_hbm,
    bias2_hbm,
    out_next,
    out_after,
    out_grad,
    out_dir,
    out_sums,
    speed,
    before,
    src,
    prior,
    raw1,
    raw2,
    raw3,
    bias1,
    bias2,
    load_sem,
    ext_a,
    ext_b,
    pack_a,
    pack_b,
    recv_a,
    recv_b,
    grad,
    pack_g,
    recv_gx,
    recv_g,
    h1,
    h2,
    w1,
    w2,
    w3,
    part,
    red,
    send_sem,
    recv_sem,
    red_send,
    red_recv,
):
    nx, ny, depth = now_hbm.shape
    gx, gy = lax.axis_index("gx"), lax.axis_index("gy")
    barrier = pltpu.get_barrier_semaphore()
    own = pl.ds(8, ny)
    loads = [
        pltpu.make_async_copy(source, target, load_sem.at[i])
        for i, (source, target) in enumerate(
            (
                (now_hbm, ext_a.at[pl.ds(4, nx), own, :]),
                (before_hbm, before),
                (speed_hbm, speed),
                (src_hbm, src),
                (prior_hbm, prior),
                (first_hbm, raw1),
                (mid_hbm, raw2),
                (last_hbm, raw3),
                (bias1_hbm, bias1),
                (bias2_hbm, bias2),
            )
        )
    ]
    for load in loads:
        load.start()

    def there(dx, dy):
        ok = None
        for pos, d, n in ((gx, dx, n_gx), (gy, dy, n_gy)):
            if d:
                one = (pos + d >= 0) & (pos + d < n)
                ok = one if ok is None else ok & one
        return ok

    count = n_gx * n_gy
    me = gx * n_gy + gy

    def peer(i):
        flat = lax.rem(me + i, count)
        return (lax.div(flat, n_gy), lax.rem(flat, n_gy))

    for i in range(1, count):
        pl.semaphore_signal(barrier, inc=1, device_id=peer(i), device_id_type=MESH)

    class Copy:
        def __init__(self, ident, source, target, dx, dy):
            self.make = lambda: pltpu.make_async_remote_copy(
                src_ref=source,
                dst_ref=target,
                send_sem=send_sem.at[ident],
                recv_sem=recv_sem.at[ident],
                device_id=(gx + dx, gy + dy),
                device_id_type=MESH,
            )
            self.to = there(dx, dy)
            self.origin = there(-dx, -dy)
            self.target = target

        def start(self):
            @pl.when(self.to)
            def _():
                self.make().start()

        def clear(self):
            @pl.when(jnp.logical_not(self.origin))
            def _():
                self.target[...] = jnp.zeros(self.target.shape, self.target.dtype)

        def arrive(self):
            @pl.when(self.origin)
            def _():
                self.make().wait_recv()

        def sent(self):
            @pl.when(self.to)
            def _():
                self.make().wait_send()

    def wave_copies(base, ext, pack, recv):
        return (
            Copy(base, ext.at[pl.ds(nx, 4), own, :], ext.at[pl.ds(0, 4), own, :], 1, 0),
            Copy(base + 1, ext.at[pl.ds(4, 4), own, :], ext.at[pl.ds(nx + 4, 4), own, :], -1, 0),
            Copy(base + 2, pack.at[1], recv.at[0], 0, 1),
            Copy(base + 3, pack.at[0], recv.at[1], 0, -1),
        )

    copies_a = wave_copies(0, ext_a, pack_a, recv_a)
    copies_b = wave_copies(4, ext_b, pack_b, recv_b)
    groups = nx // 4
    mid = pl.ds(1, groups)
    same_z = pl.ds(ny, ny)
    copies_g = (
        Copy(12, pack_g.at[1, groups - 1], recv_g.at[0, 0], 1, 1),
        Copy(13, pack_g.at[1, 0], recv_g.at[0, groups + 1], -1, 1),
        Copy(14, pack_g.at[0, groups - 1], recv_g.at[1, 0], 1, -1),
        Copy(15, pack_g.at[0, 0], recv_g.at[1, groups + 1], -1, -1),
        Copy(10, pack_g.at[1], recv_g.at[0, mid], 0, 1),
        Copy(11, pack_g.at[0], recv_g.at[1, mid], 0, -1),
        Copy(8, grad.at[pl.ds(nx, 3), same_z, :], recv_gx.at[0], 1, 0),
        Copy(9, grad.at[pl.ds(3, 3), same_z, :], recv_gx.at[1], -1, 0),
    )

    def pack_wave(ext, pack):
        half = nx // 2
        for i in range(half):
            for side, at in ((0, 8), (1, 8 + ny - 4)):
                pack[side, i] = jnp.concatenate(
                    [ext[4 + i, at : at + 4, :], ext[4 + half + i, at : at + 4, :]], axis=0
                )

    def unpack_wave(ext, recv):
        half = nx // 2
        for i in range(half):
            for side, at in ((0, 4), (1, 8 + ny)):
                tile = recv[side, i]
                ext[4 + i, at : at + 4, :] = tile[0:4]
                ext[4 + half + i, at : at + 4, :] = tile[4:8]

    loads[0].wait()
    pack_wave(ext_a, pack_a)
    for group in (copies_a, copies_b, copies_g):
        for c in group:
            c.clear()

    pl.semaphore_wait(barrier, count - 1)
    for c in copies_a:
        c.start()

    for load in loads[1:]:
        load.wait()

    r1, r2 = ny + 4, ny + 2
    m1, m2 = 8 * r1, 8 * r2
    slots = 3 * ny + 32
    blk = 6

    def column(bias):
        wide = jnp.broadcast_to(bias[...], (8, 8))
        return jnp.sum(jnp.where(iota((8, 8), 0) == iota((8, 8), 1), wide, 0.0), axis=1, keepdims=True)

    b1, b2 = column(bias1), column(bias2)

    def place_first(shape, dim):
        col = iota(shape, dim)
        a = third(col, slots)
        slot = col - slots * a
        side = slot - 3 * ny
        q = side & 7
        e = jnp.where(slot < 3 * ny, third(slot, ny), side >> 3)
        y = jnp.where(slot < 3 * ny, slot - ny * e, jnp.where(q < 4, q - 4, q + ny - 4))
        y = jnp.where(side >= 24, 999, y)
        return a, e, y, col

    a_in, e_in, _, _ = place_first((27, 3 * slots), 0 + 1)
    taps = [
        jnp.dot(
            raw1[...],
            one_hot(iota((27, 3 * slots), 0) == 9 * a_in + 3 * b + e_in),
            preferred_element_type=F32,
        )
        for b in range(3)
    ]
    _, _, y_in, col = place_first((8, 3 * slots), 1)
    top = b1.astype(BF16).astype(F32)
    rest = b1 - top
    middle = rest.astype(BF16).astype(F32)
    base = slots + 3 * ny + 24
    biases = jnp.where(col == base, top, jnp.where(col == base + 1, middle, jnp.where(col == base + 2, rest - middle, 0.0)))

    def rows_first(y):
        total = biases
        for b in range(3):
            total = jnp.where(y_in - y == b - 1, taps[b], total)
        return total

    for y in range(0, r1, 2):
        w1[8 * y : 8 * y + 16, :] = jnp.concatenate(
            [rows_first(y - 2), rows_first(y - 1)], axis=0
        ).astype(BF16)

    k2 = 8 * (blk + 2)
    same_c = (iota((64, 3 * k2), 0) >> 3) == (iota((64, 3 * k2), 1) & 7)
    a_in = third(iota((27, 3 * k2), 1), k2)
    col = iota((8, 3 * k2), 1)
    y_in = (col - k2 * third(col, k2)) >> 3
    table = []
    for t in range(9):
        full = jnp.dot(
            raw2[...], one_hot(iota((27, 3 * k2), 0) == 9 * a_in + t), preferred_element_type=F32
        )
        full = jnp.where(same_c, full, 0.0)
        total = full[0:8]
        for c in range(1, 8):
            total = total + full[8 * c : 8 * c + 8]
        table.append(total)

    def rows_mid(i):
        e, y = i // blk, i % blk
        total = jnp.zeros((8, 3 * k2), F32)
        for b in range(3):
            total = jnp.where(y_in - y == b, table[3 * b + e], total)
        return total

    for i in range(0, 3 * blk, 2):
        w2[8 * i : 8 * i + 16, :] = jnp.concatenate([rows_mid(i), rows_mid(i + 1)], axis=0).astype(BF16)

    same_c = iota((8, 3 * m2), 0) == (iota((8, 3 * m2), 1) & 7)
    a_in = third(iota((27, 3 * m2), 1), m2)
    col = iota((ny, 3 * m2), 1)
    gap = ((col - m2 * third(col, m2)) >> 3) - iota((ny, 3 * m2), 0)
    for e in range(3):
        total = jnp.zeros((ny, 3 * m2), F32)
        for b in range(3):
            full = jnp.dot(
                raw3[...],
                one_hot(iota((27, 3 * m2), 0) == 9 * a_in + 3 * b + e),
                preferred_element_type=F32,
            )
            line = jnp.sum(jnp.where(same_c, full, 0.0), axis=0, keepdims=True)
            total = jnp.where(gap == b, jnp.broadcast_to(line, total.shape), total)
        w3[ny * e : ny * e + ny, :] = total.astype(BF16)

    def inner_one(x, carry):
        center = ext_a[x + 4, 8 : 8 + ny, :]
        out_next[x] = 2.0 * center - before[x] + speed[x] * laplace_z(center)
        return carry

    lax.fori_loop(0, nx, inner_one, 0, unroll=WAVE_UNROLL)
    for c in copies_a:
        c.arrive()
    unpack_wave(ext_a, recv_a)

    def step_one(x, carry):
        value = out_next[x] + speed[x] * laplace_xy(ext_a, x, ny)
        out_next[x] = value
        ext_b[x + 4, 8 : 8 + ny, :] = value
        return carry

    lax.fori_loop(0, nx, step_one, 0, unroll=WAVE_UNROLL)
    for c in copies_b[:2]:
        c.start()
    pack_wave(ext_b, pack_b)
    for c in copies_b[2:]:
        c.start()

    def inner_two(x, carry):
        center = out_next[x]
        out_after[x] = 2.0 * center - ext_a[x + 4, 8 : 8 + ny, :] + speed[x] * laplace_z(center)
        return carry

    lax.fori_loop(0, nx, inner_two, 0, unroll=WAVE_UNROLL)
    for c in copies_b:
        c.arrive()
    unpack_wave(ext_b, recv_b)

    def store_own(plane, value):
        for e in range(3):
            rows = value if e == 1 else shift_z(value, e - 1)
            grad[plane, ny * e : ny * e + ny, :] = rows.astype(BF16)

    def step_two(x, carry):
        center = out_next[x]
        value = out_after[x] + speed[x] * laplace_xy(ext_b, x, ny)
        out_after[x] = value
        gradient = prior[x] + src[0, x] * center + src[1, x] * value
        out_grad[x] = gradient
        store_own(x + 3, gradient)
        return carry

    lax.fori_loop(0, nx, step_two, 0, unroll=WAVE_UNROLL)
    for t in range(groups):
        for side, at in ((0, 0), (1, ny - 4)):
            pack_g[side, t] = jnp.concatenate(
                [out_grad[4 * t + j, at : at + 4, :] for j in range(4)], axis=0
            ).astype(BF16)
    for c in copies_g:
        c.start()
    for c in copies_g:
        c.arrive()
    ones = jnp.where(iota((8, depth), 0) < 3, 1.0, 0.0)
    for plane in range(nx + 6):
        t, j = (plane + 1) // 4, (plane + 1) % 4
        low = recv_g[0, t].astype(F32)[4 * j : 4 * j + 4]
        high = recv_g[1, t].astype(F32)[4 * j : 4 * j + 4]
        side = jnp.concatenate([low, high], axis=0)
        grad[plane, 3 * ny : 3 * ny + 32, :] = jnp.concatenate(
            [shift_z(side, -1), side, shift_z(side, 1), ones], axis=0
        ).astype(BF16)
    for i in range(3):
        store_own(i, recv_gx[0, i].astype(F32))
        store_own(nx + 3 + i, recv_gx[1, i].astype(F32))

    big = 3.0e38
    x_low = jnp.where(gx == 0, 0.0, big)
    x_high = jnp.where(gx == n_gx - 1, 0.0, big)
    y_low = jnp.where(gy == 0, 0.0, big)
    y_high = jnp.where(gy == n_gy - 1, 0.0, big)

    def conv_plane(weight, rhs, rows):
        res = jnp.dot(weight[...], rhs, preferred_element_type=F32)
        return (
            res[rows : 2 * rows] + shift_z(res[:rows], -1) + shift_z(res[2 * rows :], 1)
        )

    def limit(value, cap):
        return value if cap is None else jnp.minimum(value, cap)

    for p in range(nx + 4):
        res = jnp.maximum(
            jnp.dot(w1[...], grad[p : p + 3].reshape(3 * slots, depth), preferred_element_type=F32), 0.0
        )
        cap = x_low if p < 2 else x_high if p >= nx + 2 else None
        res = limit(res, cap)
        h1[p, 0:16] = jnp.minimum(res[0:16], y_low).astype(BF16)
        h1[p, 16 : m1 - 16] = res[16 : m1 - 16].astype(BF16)
        h1[p, m1 - 16 : m1] = jnp.minimum(res[m1 - 16 : m1], y_high).astype(BF16)

    full2 = jnp.concatenate([jnp.broadcast_to(b2, (8, depth))] * blk, axis=0)
    for p in range(nx + 2):
        cap = x_low if p < 1 else x_high if p >= nx + 1 else None
        for y in range(0, r2, blk):
            rhs = h1[p : p + 3, 8 * y : 8 * y + k2, :].reshape(3 * k2, depth)
            res = limit(jnp.maximum(conv_plane(w2, rhs, 8 * blk) + full2, 0.0), cap)
            if y == 0:
                res = jnp.concatenate([jnp.minimum(res[0:8], y_low), res[8:]], axis=0)
            if y + blk == r2:
                res = jnp.concatenate([res[: 8 * blk - 8], jnp.minimum(res[8 * blk - 8 :], y_high)], axis=0)
            h2[p, 8 * y : 8 * y + 8 * blk] = res.astype(BF16)

    zero = jnp.zeros((ny, depth), F32)

    def layer_three(p, carry):
        gg, gd, dd = carry
        rhs = h2[pl.ds(p, 3)].reshape(3 * m2, depth)
        g = out_grad[p]
        d = conv_plane(w3, rhs, ny) + g
        out_dir[p] = d
        return gg + g * g, gd + g * d, dd + d * d

    sums = lax.fori_loop(0, nx, layer_three, (zero, zero, zero), unroll=UNROLL)
    row, lane = iota((8, 128), 0), iota((8, 128), 1)
    tile = jnp.zeros((8, 128), F32)
    for i, s in enumerate(sums):
        line = jnp.sum(s, axis=0, keepdims=True)
        folded = line[:, 0:128]
        for j in range(1, depth // 128):
            folded = folded + line[:, 128 * j : 128 * j + 128]
        tile = jnp.where(row == i, folded, tile)
    wide = jnp.broadcast_to(jnp.sum(tile, axis=1, keepdims=True), (8, 128))
    mine = jnp.sum(jnp.where(row == lane, wide, 0.0), axis=0, keepdims=True)
    part[...] = mine
    for i in range(1, count):
        pltpu.make_async_remote_copy(
            src_ref=part,
            dst_ref=red.at[i - 1],
            send_sem=red_send.at[i - 1],
            recv_sem=red_recv.at[i - 1],
            device_id=peer(i),
            device_id_type=MESH,
        ).start()
    waits = [
        pltpu.make_async_remote_copy(
            src_ref=part,
            dst_ref=red.at[i - 1],
            send_sem=red_send.at[i - 1],
            recv_sem=red_recv.at[i - 1],
            device_id=peer(i),
            device_id_type=MESH,
        )
        for i in range(1, count)
    ]
    for c in waits:
        c.wait_recv()
    total = mine
    for i in range(count - 1):
        total = total + red[i]
    spread = jnp.where(row == lane, jnp.broadcast_to(total, (8, 128)), 0.0)
    out_sums[...] = jnp.broadcast_to(jnp.sum(spread, axis=1, keepdims=True), (8, 128))
    for group in (copies_a, copies_b, copies_g):
        for c in group:
            c.sent()
    for c in waits:
        c.wait_send()


def hand_on(damping, sums, v_next, v_after, v_grad, v_dir, o_next, o_after, o_grad, o_step, scaled, sem):
    moves = [
        pltpu.make_async_copy(source, target, sem.at[i])
        for i, (source, target) in enumerate(((v_next, o_next), (v_after, o_after), (v_grad, o_grad)))
    ]
    for move in moves:
        move.start()
    scale = sums[1:2, 0:1] / (sums[0:1, 0:1] + sums[2:3, 0:1] + damping)
    nx = v_dir.shape[0]
    step = nx // 4
    for i in range(4):
        at = pl.ds(i * step, step)
        scaled[at] = scale.reshape(1, 1, 1) * v_dir[at]
        move = pltpu.make_async_copy(scaled.at[at], o_step.at[at], sem.at[3 + i])
        move.start()
        moves.append(move)
    for move in moves:
        move.wait()


def shards(n_gx, n_gy, speed, before, now, src, prior, w_first, b_first, w_mid, b_mid, w_last):
    nx, ny, depth = now.shape
    out = jax.ShapeDtypeStruct(now.shape, F32)
    vmem = pl.BlockSpec(memory_space=pltpu.VMEM)
    hbm = pl.BlockSpec(memory_space=pltpu.HBM)
    half, groups = nx // 2, nx // 4
    r1, r2 = ny + 4, ny + 2
    ch = b_first.shape[0]
    slots, blk = 3 * ny + 32, 6
    count = n_gx * n_gy
    held = pltpu.VMEM(now.shape, F32)
    *outs, sums = pl.pallas_call(
        functools.partial(kernel, n_gx, n_gy),
        out_shape=(held,) * 4 + (pltpu.VMEM((8, 128), F32),),
        in_specs=[hbm] * 10,
        out_specs=(vmem,) * 5,
        scratch_shapes=[
            pltpu.VMEM(now.shape, F32),
            pltpu.VMEM(now.shape, F32),
            pltpu.VMEM(src.shape, F32),
            pltpu.VMEM(now.shape, F32),
            pltpu.VMEM((ch, 27), BF16),
            pltpu.VMEM((ch * ch, 27), BF16),
            pltpu.VMEM((ch, 27), BF16),
            pltpu.VMEM((1, ch), F32),
            pltpu.VMEM((1, ch), F32),
            pltpu.SemaphoreType.DMA((10,)),
            pltpu.VMEM((nx + 8, ny + 16, depth), F32),
            pltpu.VMEM((nx + 8, ny + 16, depth), F32),
            pltpu.VMEM((2, half, 8, depth), F32),
            pltpu.VMEM((2, half, 8, depth), F32),
            pltpu.VMEM((2, half, 8, depth), F32),
            pltpu.VMEM((2, half, 8, depth), F32),
            pltpu.VMEM((nx + 6, slots, depth), BF16),
            pltpu.VMEM((2, groups, 16, depth), BF16),
            pltpu.VMEM((2, 3, ny, depth), BF16),
            pltpu.VMEM((2, groups + 2, 16, depth), BF16),
            pltpu.VMEM((nx + 4, r1 * ch, depth), BF16),
            pltpu.VMEM((nx + 2, r2 * ch, depth), BF16),
            pltpu.VMEM((r1 * ch, 3 * slots), BF16),
            pltpu.VMEM((3 * blk * ch, 3 * (blk + 2) * ch), BF16),
            pltpu.VMEM((3 * ny, 3 * r2 * ch), BF16),
            pltpu.VMEM((1, 128), F32),
            pltpu.VMEM((count - 1, 1, 128), F32),
            pltpu.SemaphoreType.DMA((16,)),
            pltpu.SemaphoreType.DMA((16,)),
            pltpu.SemaphoreType.DMA((count - 1,)),
            pltpu.SemaphoreType.DMA((count - 1,)),
        ],
        compiler_params=pltpu.CompilerParams(
            collective_id=0, has_side_effects=True, vmem_limit_bytes=40 * 1024 * 1024
        ),
    )(
        *(
            pltpu.with_memory_space_constraint(v, pltpu.HBM)
            for v in (
                speed,
                before,
                now,
                src,
                prior,
                w_first.transpose(1, 2, 0).reshape(ch, 27),
                w_mid.transpose(1, 2, 0).reshape(ch * ch, 27),
                w_last.transpose(2, 1, 0).reshape(ch, 27),
                b_first.reshape(1, ch),
                b_mid.reshape(1, ch),
            )
        )
    )
    return pl.pallas_call(
        functools.partial(hand_on, 8.0 * float(nx * n_gx * ny * n_gy * depth)),
        out_shape=(out,) * 4,
        in_specs=[vmem] * 5,
        out_specs=(hbm,) * 4,
        scratch_shapes=[pltpu.VMEM(now.shape, F32), pltpu.SemaphoreType.DMA((7,))],
    )(*(pltpu.with_memory_space_constraint(v, pltpu.VMEM) for v in (sums, *outs)))


def solution(mesh):
    brick = P("gx", "gy", None)
    return jax.shard_map(
        functools.partial(shards, mesh.shape["gx"], mesh.shape["gy"]),
        mesh=mesh,
        in_specs=(brick, brick, brick, P(None, "gx", "gy", None), brick, P(), P(), P(), P(), P()),
        out_specs=(brick,) * 4,
        check_vma=False,
    )
```

```python
import functools

import jax
import jax.numpy as jnp
from jax import lax
from jax.experimental import pallas as pl
from jax.experimental.pallas import tpu as pltpu
from jax.sharding import PartitionSpec as P

COEFS = (-205.0 / 72.0, 8.0 / 5.0, -1.0 / 5.0, 8.0 / 315.0, -1.0 / 560.0)
MESH = pl.DeviceIdType.MESH
F32 = jnp.float32
BF16 = jnp.bfloat16
UNROLL = True
WAVE_UNROLL = 8


def shift_z(v, k):
    depth = v.shape[-1]
    lane = lax.broadcasted_iota(jnp.int32, v.shape, v.ndim - 1)
    rolled = pltpu.roll(v, (-k) % depth, v.ndim - 1)
    return jnp.where((lane + k >= 0) & (lane + k < depth), rolled, 0.0)


def iota(shape, dim):
    return lax.broadcasted_iota(jnp.int32, shape, dim)


def one_hot(hit):
    return jnp.where(hit, 1.0, 0.0).astype(BF16)


def third(index, size):
    return jnp.where(index >= size, 1, 0) + jnp.where(index >= 2 * size, 1, 0)


def laplace_z(center):
    total = 3.0 * COEFS[0] * center
    for k in range(1, 5):
        total = total + COEFS[k] * (shift_z(center, k) + shift_z(center, -k))
    return total


def laplace_xy(ext, x, ny):
    total = None
    for k in range(1, 5):
        cycle = ext[x + 4 + k, 8 : 8 + ny, :] + ext[x + 4 - k, 8 : 8 + ny, :]
        cycle = cycle + ext[x + 4, 8 + k : 8 + k + ny, :]
        cycle = cycle + ext[x + 4, 8 - k : 8 - k + ny, :]
        total = COEFS[k] * cycle if total is None else total + COEFS[k] * cycle
    return total


def kernel(
    n_gx,
    n_gy,
    speed_hbm,
    before_hbm,
    now_hbm,
    src_hbm,
    prior_hbm,
    first_hbm,
    mid_hbm,
    last_hbm,
    bias1_hbm,
    bias2_hbm,
    out_next,
    out_after,
    out_grad,
    out_dir,
    out_sums,
    speed,
    before,
    src,
    prior,
    raw1,
    raw2,
    raw3,
    bias1,
    bias2,
    load_sem,
    ext_a,
    ext_b,
    pack_x,
    pack_y,
    recv_x,
    recv_y,
    recv_c,
    from_own_x,
    from_own_y,
    grad,
    pack_g,
    recv_gx,
    recv_g,
    h1,
    h2,
    w1,
    w2,
    w3,
    part,
    red,
    send_sem,
    recv_sem,
    red_send,
    red_recv,
):
    nx, ny, depth = now_hbm.shape
    gx, gy = lax.axis_index("gx"), lax.axis_index("gy")
    barrier = pltpu.get_barrier_semaphore()
    brick = pl.ds(8, ny)
    loads = [
        pltpu.make_async_copy(source, target, load_sem.at[i])
        for i, (source, target) in enumerate(
            (
                (now_hbm, ext_a.at[pl.ds(4, nx), brick, :]),
                (before_hbm, before),
                (speed_hbm, speed),
                (first_hbm, raw1),
                (mid_hbm, raw2),
                (last_hbm, raw3),
                (bias1_hbm, bias1),
                (bias2_hbm, bias2),
                (src_hbm, src),
                (prior_hbm, prior),
            )
        )
    ]
    for load in loads:
        load.start()

    def there(dx, dy):
        ok = None
        for pos, d, n in ((gx, dx, n_gx), (gy, dy, n_gy)):
            if d:
                one = (pos + d >= 0) & (pos + d < n)
                ok = one if ok is None else ok & one
        return ok

    count = n_gx * n_gy
    me = gx * n_gy + gy

    def peer(i):
        flat = lax.rem(me + i, count)
        return (lax.div(flat, n_gy), lax.rem(flat, n_gy))

    for i in range(1, count):
        pl.semaphore_signal(barrier, inc=1, device_id=peer(i), device_id_type=MESH)

    class Copy:
        def __init__(self, ident, source, target, dx, dy):
            self.make = lambda: pltpu.make_async_remote_copy(
                src_ref=source,
                dst_ref=target,
                send_sem=send_sem.at[ident],
                recv_sem=recv_sem.at[ident],
                device_id=(gx + dx, gy + dy),
                device_id_type=MESH,
            )
            self.to = there(dx, dy)
            self.origin = there(-dx, -dy)
            self.target = target

        def start(self):
            @pl.when(self.to)
            def _():
                self.make().start()

        def clear(self):
            @pl.when(jnp.logical_not(self.origin))
            def _():
                self.target[...] = jnp.zeros(self.target.shape, self.target.dtype)

        def arrive(self):
            @pl.when(self.origin)
            def _():
                self.make().wait_recv()

        def sent(self):
            @pl.when(self.to)
            def _():
                self.make().wait_send()

    groups = nx // 4
    mid = pl.ds(1, groups)
    same_z = pl.ds(ny, ny)
    copies_w = (
        Copy(0, pack_y.at[1, groups - 1, 0], recv_c.at[0, 0], 1, 1),
        Copy(1, pack_y.at[1, 0, 0], recv_c.at[1, 0], -1, 1),
        Copy(2, pack_y.at[0, groups - 1, 0], recv_c.at[0, 1], 1, -1),
        Copy(3, pack_y.at[0, 0, 0], recv_c.at[1, 1], -1, -1),
        Copy(4, pack_y.at[1], recv_y.at[0], 0, 1),
        Copy(5, pack_y.at[0], recv_y.at[1], 0, -1),
        Copy(6, pack_x.at[1], recv_x.at[0], 1, 0),
        Copy(7, pack_x.at[0], recv_x.at[1], -1, 0),
    )
    copies_g = (
        Copy(12, pack_g.at[1, groups - 1], recv_g.at[0, 0], 1, 1),
        Copy(13, pack_g.at[1, 0], recv_g.at[0, groups + 1], -1, 1),
        Copy(14, pack_g.at[0, groups - 1], recv_g.at[1, 0], 1, -1),
        Copy(15, pack_g.at[0, 0], recv_g.at[1, groups + 1], -1, -1),
        Copy(10, pack_g.at[1], recv_g.at[0, mid], 0, 1),
        Copy(11, pack_g.at[0], recv_g.at[1, mid], 0, -1),
        Copy(8, grad.at[pl.ds(nx, 3), same_z, :], recv_gx.at[0], 1, 0),
        Copy(9, grad.at[pl.ds(3, 3), same_z, :], recv_gx.at[1], -1, 0),
    )

    row8 = iota((8, depth), 0)

    def half_turn(v):
        return pltpu.roll(v, 4, 0)

    def edge(v):
        return jnp.where(row8 < 4, v[0:8], v[ny - 8 : ny])

    def pack_four(e):
        low = [jnp.where(row8 < 4, e[i], half_turn(e[i + 1])) for i in (0, 2)]
        high = [jnp.where(row8 < 4, half_turn(e[i]), e[i + 1]) for i in (0, 2)]
        return [jnp.concatenate(v, axis=0).astype(BF16) for v in (low, high)]

    def unpack_four(low, high):
        sides = []
        for i in (0, 8):
            a, b = low.astype(F32)[i : i + 8], high.astype(F32)[i : i + 8]
            sides.append(jnp.where(row8 < 4, b, half_turn(a)))
            sides.append(jnp.where(row8 < 4, half_turn(b), a))
        return sides

    def across(v):
        total = jnp.zeros((8, depth), F32)
        for k in range(1, 5):
            down, up = pltpu.roll(v, k, 0), pltpu.roll(v, 8 - k, 0)
            total = total + COEFS[k] * jnp.where(row8 < k, down, jnp.where(row8 >= 8 - k, up, 0.0))
        return total

    def spread(e):
        parts = [jnp.where(row8 < 4, e, 0.0), jnp.where(row8 < 4, 0.0, e)]
        if ny > 16:
            parts.insert(1, jnp.zeros((ny - 16, depth), F32))
        return jnp.concatenate(parts, axis=0)

    blank = jnp.zeros((ny + 16, depth), F32)
    for i in range(4):
        ext_a[i] = blank
        ext_a[nx + 4 + i] = blank
    for x in range(nx):
        ext_a[x + 4, 0:8] = blank[0:8]
        ext_a[x + 4, ny + 8 : ny + 16] = blank[0:8]
    for load in loads[:3]:
        load.wait()

    for t in range(groups):
        edges = [[], [], []]
        for x in range(4 * t, 4 * t + 4):
            center = ext_a[x + 4, 8 : 8 + ny, :]
            factor = speed[x]
            partial = (
                2.0 * center - before[x] + factor * (laplace_z(center) + laplace_xy(ext_a, x, ny))
            )
            out_next[x] = partial
            for i, v in enumerate((center, partial, factor)):
                edges[i].append(edge(v))
                if x < 4:
                    pack_x[0, x, i] = v.astype(BF16)
                if x >= nx - 4:
                    pack_x[1, x - nx + 4, i] = v.astype(BF16)
        for i in range(3):
            pack_y[0, t, i], pack_y[1, t, i] = pack_four(edges[i])

    for group in (copies_w, copies_g):
        for c in group:
            c.clear()
    pl.semaphore_wait(barrier, count - 1)
    for c in copies_w:
        c.start()

    for load in loads[3:8]:
        load.wait()

    r1, r2 = ny + 4, ny + 2
    m1, m2 = 8 * r1, 8 * r2
    slots = 3 * ny + 32
    blk = 6

    def column(bias):
        wide = jnp.broadcast_to(bias[...], (8, 8))
        return jnp.sum(jnp.where(iota((8, 8), 0) == iota((8, 8), 1), wide, 0.0), axis=1, keepdims=True)

    b1, b2 = column(bias1), column(bias2)

    def place_first(shape, dim):
        col = iota(shape, dim)
        a = third(col, slots)
        slot = col - slots * a
        side = slot - 3 * ny
        q = side & 7
        e = jnp.where(slot < 3 * ny, third(slot, ny), side >> 3)
        y = jnp.where(slot < 3 * ny, slot - ny * e, jnp.where(q < 4, q + ny, q - 8))
        y = jnp.where(side >= 24, 999, y)
        return a, e, y, col

    a_in, e_in, _, _ = place_first((27, 3 * slots), 0 + 1)
    taps = [
        jnp.dot(
            raw1[...],
            one_hot(iota((27, 3 * slots), 0) == 9 * a_in + 3 * b + e_in),
            preferred_element_type=F32,
        )
        for b in range(3)
    ]
    _, _, y_in, col = place_first((8, 3 * slots), 1)
    top = b1.astype(BF16).astype(F32)
    rest = b1 - top
    middle = rest.astype(BF16).astype(F32)
    base = slots + 3 * ny + 24
    biases = jnp.where(col == base, top, jnp.where(col == base + 1, middle, jnp.where(col == base + 2, rest - middle, 0.0)))

    def rows_first(y):
        total = biases
        for b in range(3):
            total = jnp.where(y_in - y == b - 1, taps[b], total)
        return total

    for y in range(0, r1, 2):
        w1[8 * y : 8 * y + 16, :] = jnp.concatenate(
            [rows_first(y - 2), rows_first(y - 1)], axis=0
        ).astype(BF16)

    k2 = 8 * (blk + 2)
    same_c = (iota((64, 3 * k2), 0) >> 3) == (iota((64, 3 * k2), 1) & 7)
    a_in = third(iota((27, 3 * k2), 1), k2)
    col = iota((8, 3 * k2), 1)
    y_in = (col - k2 * third(col, k2)) >> 3
    table = []
    for t in range(9):
        full = jnp.dot(
            raw2[...], one_hot(iota((27, 3 * k2), 0) == 9 * a_in + t), preferred_element_type=F32
        )
        full = jnp.where(same_c, full, 0.0)
        total = full[0:8]
        for c in range(1, 8):
            total = total + full[8 * c : 8 * c + 8]
        table.append(total)

    def rows_mid(i):
        e, y = i // blk, i % blk
        total = jnp.zeros((8, 3 * k2), F32)
        for b in range(3):
            total = jnp.where(y_in - y == b, table[3 * b + e], total)
        return total

    for i in range(0, 3 * blk, 2):
        w2[8 * i : 8 * i + 16, :] = jnp.concatenate([rows_mid(i), rows_mid(i + 1)], axis=0).astype(BF16)

    same_c = iota((8, 3 * m2), 0) == (iota((8, 3 * m2), 1) & 7)
    a_in = third(iota((27, 3 * m2), 1), m2)
    col = iota((ny, 3 * m2), 1)
    gap = ((col - m2 * third(col, m2)) >> 3) - iota((ny, 3 * m2), 0)
    for e in range(3):
        total = jnp.zeros((ny, 3 * m2), F32)
        for b in range(3):
            full = jnp.dot(
                raw3[...],
                one_hot(iota((27, 3 * m2), 0) == 9 * a_in + 3 * b + e),
                preferred_element_type=F32,
            )
            line = jnp.sum(jnp.where(same_c, full, 0.0), axis=0, keepdims=True)
            total = jnp.where(gap == b, jnp.broadcast_to(line, total.shape), total)
        w3[ny * e : ny * e + ny, :] = total.astype(BF16)

    own = slice(8, 8 + ny)
    outside = [x for x in range(-4, nx + 4) if x < 0 or x >= nx]

    def reach(x, inside):
        return [(k, x + d * k) for k in range(1, 5) for d in (-1, 1) if inside(x + d * k)]

    for i, x in enumerate(outside):
        total = jnp.zeros((ny, depth), F32)
        for k, at in reach(x, lambda v: 0 <= v < nx):
            total = total + COEFS[k] * ext_a[at + 4, own]
        from_own_x[i] = total
    for x in range(nx):
        from_own_y[x] = across(edge(ext_a[x + 4, own]))
    for load in loads[8:]:
        load.wait()

    for c in copies_w:
        c.arrive()
    corner = {}
    for i, first in enumerate((-4, nx)):
        for j, v in enumerate(unpack_four(recv_c[i, 0], recv_c[i, 1])):
            corner[first + j] = v
    halo_x = {x: recv_x.at[i // 4, i % 4] for i, x in enumerate(outside)}
    for i, x in enumerate(outside):
        felt = from_own_x[i] + spread(across(corner[x]))
        ext_b[x + 4, own] = halo_x[x][1].astype(F32) + halo_x[x][2].astype(F32) * felt
    for t in range(groups):
        sides = [unpack_four(recv_y[0, t, i], recv_y[1, t, i]) for i in range(3)]
        for j in range(4):
            x = 4 * t + j
            felt = from_own_y[x]
            for k, at in reach(x, lambda v: v in corner):
                felt = felt + COEFS[k] * corner[at]
            side = sides[1][j] + sides[2][j] * felt
            ext_b[x + 4, 0:8] = side
            ext_b[x + 4, ny + 8 : ny + 16] = side
            felt = spread(across(sides[0][j]))
            for k, at in reach(x, lambda v: v in corner):
                felt = felt + COEFS[k] * halo_x[at][0].astype(F32)
            value = out_next[x] + speed[x] * felt
            out_next[x] = value
            ext_b[x + 4, own] = value

    def store_own(plane, value):
        for e in range(3):
            rows = value if e == 1 else shift_z(value, e - 1)
            grad[plane, ny * e : ny * e + ny, :] = rows.astype(BF16)

    def step_two(x, carry):
        center = out_next[x]
        value = 2.0 * center - ext_a[x + 4, own] + speed[x] * (laplace_z(center) + laplace_xy(ext_b, x, ny))
        out_after[x] = value
        gradient = prior[x] + src[0, x] * center + src[1, x] * value
        out_grad[x] = gradient
        store_own(x + 3, gradient)
        return carry

    lax.fori_loop(0, nx, step_two, 0, unroll=WAVE_UNROLL)
    for t in range(groups):
        pack_g[0, t], pack_g[1, t] = pack_four([edge(out_grad[4 * t + j]) for j in range(4)])
    for c in copies_g:
        c.start()
    for c in copies_g:
        c.arrive()
    ones = jnp.where(iota((8, depth), 0) < 3, 1.0, 0.0)
    for t in range(groups + 2):
        for j, side in enumerate(unpack_four(recv_g[0, t], recv_g[1, t])):
            plane = 4 * t + j - 1
            if 0 <= plane < nx + 6:
                grad[plane, 3 * ny : 3 * ny + 32, :] = jnp.concatenate(
                    [shift_z(side, -1), side, shift_z(side, 1), ones], axis=0
                ).astype(BF16)
    for i in range(3):
        store_own(i, recv_gx[0, i].astype(F32))
        store_own(nx + 3 + i, recv_gx[1, i].astype(F32))

    big = 3.0e38
    x_low = jnp.where(gx == 0, 0.0, big)
    x_high = jnp.where(gx == n_gx - 1, 0.0, big)
    y_low = jnp.where(gy == 0, 0.0, big)
    y_high = jnp.where(gy == n_gy - 1, 0.0, big)

    def conv_plane(weight, rhs, rows):
        res = jnp.dot(weight[...], rhs, preferred_element_type=F32)
        return (
            res[rows : 2 * rows] + shift_z(res[:rows], -1) + shift_z(res[2 * rows :], 1)
        )

    def limit(value, cap):
        return value if cap is None else jnp.minimum(value, cap)

    for p in range(nx + 4):
        res = jnp.maximum(
            jnp.dot(w1[...], grad[p : p + 3].reshape(3 * slots, depth), preferred_element_type=F32), 0.0
        )
        cap = x_low if p < 2 else x_high if p >= nx + 2 else None
        res = limit(res, cap)
        h1[p, 0:16] = jnp.minimum(res[0:16], y_low).astype(BF16)
        h1[p, 16 : m1 - 16] = res[16 : m1 - 16].astype(BF16)
        h1[p, m1 - 16 : m1] = jnp.minimum(res[m1 - 16 : m1], y_high).astype(BF16)

    full2 = jnp.concatenate([jnp.broadcast_to(b2, (8, depth))] * blk, axis=0)
    for p in range(nx + 2):
        cap = x_low if p < 1 else x_high if p >= nx + 1 else None
        for y in range(0, r2, blk):
            rhs = h1[p : p + 3, 8 * y : 8 * y + k2, :].reshape(3 * k2, depth)
            res = limit(jnp.maximum(conv_plane(w2, rhs, 8 * blk) + full2, 0.0), cap)
            if y == 0:
                res = jnp.concatenate([jnp.minimum(res[0:8], y_low), res[8:]], axis=0)
            if y + blk == r2:
                res = jnp.concatenate([res[: 8 * blk - 8], jnp.minimum(res[8 * blk - 8 :], y_high)], axis=0)
            h2[p, 8 * y : 8 * y + 8 * blk] = res.astype(BF16)

    zero = jnp.zeros((ny, depth), F32)

    def layer_three(p, carry):
        gg, gd, dd = carry
        rhs = h2[pl.ds(p, 3)].reshape(3 * m2, depth)
        g = out_grad[p]
        d = conv_plane(w3, rhs, ny) + g
        out_dir[p] = d
        return gg + g * g, gd + g * d, dd + d * d

    sums = lax.fori_loop(0, nx, layer_three, (zero, zero, zero), unroll=UNROLL)
    row, lane = iota((8, 128), 0), iota((8, 128), 1)
    tile = jnp.zeros((8, 128), F32)
    for i, s in enumerate(sums):
        line = jnp.sum(s, axis=0, keepdims=True)
        folded = line[:, 0:128]
        for j in range(1, depth // 128):
            folded = folded + line[:, 128 * j : 128 * j + 128]
        tile = jnp.where(row == i, folded, tile)
    wide = jnp.broadcast_to(jnp.sum(tile, axis=1, keepdims=True), (8, 128))
    mine = jnp.sum(jnp.where(row == lane, wide, 0.0), axis=0, keepdims=True)
    part[...] = mine
    for i in range(1, count):
        pltpu.make_async_remote_copy(
            src_ref=part,
            dst_ref=red.at[i - 1],
            send_sem=red_send.at[i - 1],
            recv_sem=red_recv.at[i - 1],
            device_id=peer(i),
            device_id_type=MESH,
        ).start()
    waits = [
        pltpu.make_async_remote_copy(
            src_ref=part,
            dst_ref=red.at[i - 1],
            send_sem=red_send.at[i - 1],
            recv_sem=red_recv.at[i - 1],
            device_id=peer(i),
            device_id_type=MESH,
        )
        for i in range(1, count)
    ]
    for c in waits:
        c.wait_recv()
    total = mine
    for i in range(count - 1):
        total = total + red[i]
    spread = jnp.where(row == lane, jnp.broadcast_to(total, (8, 128)), 0.0)
    out_sums[...] = jnp.broadcast_to(jnp.sum(spread, axis=1, keepdims=True), (8, 128))
    for group in (copies_w, copies_g):
        for c in group:
            c.sent()
    for c in waits:
        c.wait_send()


def hand_on(damping, sums, v_next, v_after, v_grad, v_dir, o_next, o_after, o_grad, o_step, scaled, sem):
    moves = [
        pltpu.make_async_copy(source, target, sem.at[i])
        for i, (source, target) in enumerate(((v_next, o_next), (v_after, o_after), (v_grad, o_grad)))
    ]
    for move in moves:
        move.start()
    scale = sums[1:2, 0:1] / (sums[0:1, 0:1] + sums[2:3, 0:1] + damping)
    nx = v_dir.shape[0]
    step = nx // 4
    for i in range(4):
        at = pl.ds(i * step, step)
        scaled[at] = scale.reshape(1, 1, 1) * v_dir[at]
        move = pltpu.make_async_copy(scaled.at[at], o_step.at[at], sem.at[3 + i])
        move.start()
        moves.append(move)
    for move in moves:
        move.wait()


def shards(n_gx, n_gy, speed, before, now, src, prior, w_first, b_first, w_mid, b_mid, w_last):
    nx, ny, depth = now.shape
    out = jax.ShapeDtypeStruct(now.shape, F32)
    vmem = pl.BlockSpec(memory_space=pltpu.VMEM)
    hbm = pl.BlockSpec(memory_space=pltpu.HBM)
    groups = nx // 4
    r1, r2 = ny + 4, ny + 2
    ch = b_first.shape[0]
    slots, blk = 3 * ny + 32, 6
    count = n_gx * n_gy
    held = pltpu.VMEM(now.shape, F32)
    *outs, sums = pl.pallas_call(
        functools.partial(kernel, n_gx, n_gy),
        out_shape=(held,) * 4 + (pltpu.VMEM((8, 128), F32),),
        in_specs=[hbm] * 10,
        out_specs=(vmem,) * 5,
        scratch_shapes=[
            pltpu.VMEM(now.shape, F32),
            pltpu.VMEM(now.shape, F32),
            pltpu.VMEM(src.shape, F32),
            pltpu.VMEM(now.shape, F32),
            pltpu.VMEM((ch, 27), BF16),
            pltpu.VMEM((ch * ch, 27), BF16),
            pltpu.VMEM((ch, 27), BF16),
            pltpu.VMEM((1, ch), F32),
            pltpu.VMEM((1, ch), F32),
            pltpu.SemaphoreType.DMA((10,)),
            pltpu.VMEM((nx + 8, ny + 16, depth), F32),
            pltpu.VMEM((nx + 8, ny + 16, depth), F32),
            pltpu.VMEM((2, 4, 3, ny, depth), BF16),
            pltpu.VMEM((2, groups, 3, 16, depth), BF16),
            pltpu.VMEM((2, 4, 3, ny, depth), BF16),
            pltpu.VMEM((2, groups, 3, 16, depth), BF16),
            pltpu.VMEM((2, 2, 16, depth), BF16),
            pltpu.VMEM((8, ny, depth), F32),
            pltpu.VMEM((nx, 8, depth), F32),
            pltpu.VMEM((nx + 6, slots, depth), BF16),
            pltpu.VMEM((2, groups, 16, depth), BF16),
            pltpu.VMEM((2, 3, ny, depth), BF16),
            pltpu.VMEM((2, groups + 2, 16, depth), BF16),
            pltpu.VMEM((nx + 4, r1 * ch, depth), BF16),
            pltpu.VMEM((nx + 2, r2 * ch, depth), BF16),
            pltpu.VMEM((r1 * ch, 3 * slots), BF16),
            pltpu.VMEM((3 * blk * ch, 3 * (blk + 2) * ch), BF16),
            pltpu.VMEM((3 * ny, 3 * r2 * ch), BF16),
            pltpu.VMEM((1, 128), F32),
            pltpu.VMEM((count - 1, 1, 128), F32),
            pltpu.SemaphoreType.DMA((16,)),
            pltpu.SemaphoreType.DMA((16,)),
            pltpu.SemaphoreType.DMA((count - 1,)),
            pltpu.SemaphoreType.DMA((count - 1,)),
        ],
        compiler_params=pltpu.CompilerParams(
            collective_id=0, has_side_effects=True, vmem_limit_bytes=40 * 1024 * 1024
        ),
    )(
        *(
            pltpu.with_memory_space_constraint(v, pltpu.HBM)
            for v in (
                speed,
                before,
                now,
                src,
                prior,
                w_first.transpose(1, 2, 0).reshape(ch, 27),
                w_mid.transpose(1, 2, 0).reshape(ch * ch, 27),
                w_last.transpose(2, 1, 0).reshape(ch, 27),
                b_first.reshape(1, ch),
                b_mid.reshape(1, ch),
            )
        )
    )
    return pl.pallas_call(
        functools.partial(hand_on, 8.0 * float(nx * n_gx * ny * n_gy * depth)),
        out_shape=(out,) * 4,
        in_specs=[vmem] * 5,
        out_specs=(hbm,) * 4,
        scratch_shapes=[pltpu.VMEM(now.shape, F32), pltpu.SemaphoreType.DMA((7,))],
    )(*(pltpu.with_memory_space_constraint(v, pltpu.VMEM) for v in (sums, *outs)))


def solution(mesh):
    brick = P("gx", "gy", None)
    return jax.shard_map(
        functools.partial(shards, mesh.shape["gx"], mesh.shape["gy"]),
        mesh=mesh,
        in_specs=(brick, brick, brick, P(None, "gx", "gy", None), brick, P(), P(), P(), P(), P()),
        out_specs=(brick,) * 4,
        check_vma=False,
    )
```

```python
import functools

import jax
import jax.numpy as jnp
from jax import lax
from jax.experimental import pallas as pl
from jax.experimental.pallas import tpu as pltpu
from jax.sharding import PartitionSpec as P

COEFS = (-205.0 / 72.0, 8.0 / 5.0, -1.0 / 5.0, 8.0 / 315.0, -1.0 / 560.0)
MESH = pl.DeviceIdType.MESH
F32 = jnp.float32
BF16 = jnp.bfloat16
UNROLL = True
WAVE_UNROLL = 4
FAR = 3


def shift_z(v, k):
    depth = v.shape[-1]
    lane = lax.broadcasted_iota(jnp.int32, v.shape, v.ndim - 1)
    rolled = pltpu.roll(v, (-k) % depth, v.ndim - 1)
    return jnp.where((lane + k >= 0) & (lane + k < depth), rolled, 0.0)


def iota(shape, dim):
    return lax.broadcasted_iota(jnp.int32, shape, dim)


def one_hot(hit):
    return jnp.where(hit, 1.0, 0.0).astype(BF16)


def third(index, size):
    return jnp.where(index >= size, 1, 0) + jnp.where(index >= 2 * size, 1, 0)


def laplace_xy(ext, x, ny):
    total = None
    for k in range(1, 5):
        cycle = ext[x + 4 + k, 8 : 8 + ny, :] + ext[x + 4 - k, 8 : 8 + ny, :]
        cycle = cycle + ext[x + 4, 8 + k : 8 + k + ny, :]
        cycle = cycle + ext[x + 4, 8 - k : 8 - k + ny, :]
        total = COEFS[k] * cycle if total is None else total + COEFS[k] * cycle
    return total


def kernel(
    n_gx,
    n_gy,
    speed_hbm,
    before_hbm,
    now_hbm,
    src_hbm,
    prior_hbm,
    first_hbm,
    mid_hbm,
    last_hbm,
    bias1_hbm,
    bias2_hbm,
    out_next,
    out_after,
    out_grad,
    out_dir,
    out_sums,
    speed,
    before,
    src,
    prior,
    raw1,
    raw2,
    raw3,
    bias1,
    bias2,
    load_sem,
    ext_a,
    ext_b,
    pack_x,
    pack_y,
    recv_x,
    recv_y,
    recv_c,
    from_own_x,
    from_own_y,
    stencil,
    lap_z,
    grad,
    pack_g,
    recv_gx,
    recv_g,
    h1,
    h2,
    w1,
    w2,
    w3,
    part,
    red,
    send_sem,
    recv_sem,
    red_send,
    red_recv,
):
    nx, ny, depth = now_hbm.shape
    gx, gy = lax.axis_index("gx"), lax.axis_index("gy")
    barrier = pltpu.get_barrier_semaphore()
    brick = pl.ds(8, ny)
    loads = [
        pltpu.make_async_copy(source, target, load_sem.at[i])
        for i, (source, target) in enumerate(
            (
                (now_hbm, ext_a.at[pl.ds(4, nx), brick, :]),
                (before_hbm, before),
                (speed_hbm, speed),
                (first_hbm, raw1),
                (mid_hbm, raw2),
                (last_hbm, raw3),
                (bias1_hbm, bias1),
                (bias2_hbm, bias2),
                (src_hbm, src),
                (prior_hbm, prior),
            )
        )
    ]
    for load in loads:
        load.start()

    def there(dx, dy):
        ok = None
        for pos, d, n in ((gx, dx, n_gx), (gy, dy, n_gy)):
            if d:
                one = (pos + d >= 0) & (pos + d < n)
                ok = one if ok is None else ok & one
        return ok

    count = n_gx * n_gy
    me = gx * n_gy + gy

    def peer(i):
        flat = lax.rem(me + i, count)
        return (lax.div(flat, n_gy), lax.rem(flat, n_gy))

    def greet(x, y):
        pl.semaphore_signal(barrier, inc=1, device_id=(x, y), device_id_type=MESH)

    def within(pos, n, d):
        return jnp.minimum(pos, d) + jnp.minimum(n - 1 - pos, d) + 1

    for dx, dy in ((0, 1), (0, -1), (1, 0), (-1, 0), (1, 1), (1, -1), (-1, 1), (-1, -1)):

        @pl.when(there(dx, dy))
        def _(dx=dx, dy=dy):
            greet(gx + dx, gy + dy)

    def far(pos, j):
        return (j - pos > FAR) | (pos - j > FAR)

    for j in range(n_gy):

        @pl.when(far(gy, j))
        def _(j=j):
            for i in range(n_gx):
                greet(i, j)

        if n_gx > FAR + 1:

            @pl.when(jnp.logical_not(far(gy, j)))
            def _(j=j):
                for i in range(n_gx):

                    @pl.when(far(gx, i))
                    def _(i=i):
                        greet(i, j)

    wanted = within(gx, n_gx, 1) * within(gy, n_gy, 1) - 1
    wanted = wanted + count - within(gx, n_gx, FAR) * within(gy, n_gy, FAR)

    class Copy:
        def __init__(self, ident, source, target, dx, dy):
            self.make = lambda: pltpu.make_async_remote_copy(
                src_ref=source,
                dst_ref=target,
                send_sem=send_sem.at[ident],
                recv_sem=recv_sem.at[ident],
                device_id=(gx + dx, gy + dy),
                device_id_type=MESH,
            )
            self.to = there(dx, dy)
            self.origin = there(-dx, -dy)
            self.target = target

        def start(self):
            @pl.when(self.to)
            def _():
                self.make().start()

        def clear(self):
            @pl.when(jnp.logical_not(self.origin))
            def _():
                self.target[...] = jnp.zeros(self.target.shape, self.target.dtype)

        def arrive(self):
            @pl.when(self.origin)
            def _():
                self.make().wait_recv()

        def sent(self):
            @pl.when(self.to)
            def _():
                self.make().wait_send()

    groups = nx // 4
    mid = pl.ds(1, groups)
    same_z = pl.ds(ny, ny)
    copies_w = (
        Copy(0, pack_y.at[1, groups - 1, 0], recv_c.at[0, 0], 1, 1),
        Copy(1, pack_y.at[1, 0, 0], recv_c.at[1, 0], -1, 1),
        Copy(2, pack_y.at[0, groups - 1, 0], recv_c.at[0, 1], 1, -1),
        Copy(3, pack_y.at[0, 0, 0], recv_c.at[1, 1], -1, -1),
        Copy(4, pack_y.at[1], recv_y.at[0], 0, 1),
        Copy(5, pack_y.at[0], recv_y.at[1], 0, -1),
        Copy(6, pack_x.at[1], recv_x.at[0], 1, 0),
        Copy(7, pack_x.at[0], recv_x.at[1], -1, 0),
    )
    copies_g = (
        Copy(12, pack_g.at[1, groups - 1], recv_g.at[0, 0], 1, 1),
        Copy(13, pack_g.at[1, 0], recv_g.at[0, groups + 1], -1, 1),
        Copy(14, pack_g.at[0, groups - 1], recv_g.at[1, 0], 1, -1),
        Copy(15, pack_g.at[0, 0], recv_g.at[1, groups + 1], -1, -1),
        Copy(10, pack_g.at[1], recv_g.at[0, mid], 0, 1),
        Copy(11, pack_g.at[0], recv_g.at[1, mid], 0, -1),
        Copy(8, grad.at[pl.ds(nx, 3), same_z, :], recv_gx.at[0], 1, 0),
        Copy(9, grad.at[pl.ds(3, 3), same_z, :], recv_gx.at[1], -1, 0),
    )

    row8 = iota((8, depth), 0)

    def half_turn(v):
        return pltpu.roll(v, 4, 0)

    def edge(v):
        return jnp.where(row8 < 4, v[0:8], v[ny - 8 : ny])

    def pack_four(e):
        low = [jnp.where(row8 < 4, e[i], half_turn(e[i + 1])) for i in (0, 2)]
        high = [jnp.where(row8 < 4, half_turn(e[i]), e[i + 1]) for i in (0, 2)]
        return [jnp.concatenate(v, axis=0).astype(BF16) for v in (low, high)]

    def unpack_four(low, high):
        sides = []
        for i in (0, 8):
            a, b = low.astype(F32)[i : i + 8], high.astype(F32)[i : i + 8]
            sides.append(jnp.where(row8 < 4, b, half_turn(a)))
            sides.append(jnp.where(row8 < 4, half_turn(b), a))
        return sides

    def across(v):
        total = jnp.zeros((8, depth), F32)
        for k in range(1, 5):
            down, up = pltpu.roll(v, k, 0), pltpu.roll(v, 8 - k, 0)
            total = total + COEFS[k] * jnp.where(row8 < k, down, jnp.where(row8 >= 8 - k, up, 0.0))
        return total

    def spread(e):
        parts = [jnp.where(row8 < 4, e, 0.0), jnp.where(row8 < 4, 0.0, e)]
        if ny > 16:
            parts.insert(1, jnp.zeros((ny - 16, depth), F32))
        return jnp.concatenate(parts, axis=0)

    gap = iota((depth, depth), 0) - iota((depth, depth), 1)
    taps = jnp.zeros((depth, depth), F32)
    for k in range(5):
        taps = jnp.where((gap == k) | (gap == -k), COEFS[k] * (1.0 if k else 3.0), taps)
    stencil[0] = taps.astype(BF16)
    stencil[1] = (taps - taps.astype(BF16).astype(F32)).astype(BF16)

    def along_z(field):
        v = field.reshape(nx * ny, depth)
        high = v.astype(BF16)
        low = (v - high.astype(F32)).astype(BF16)

        def times(x, i):
            return jnp.dot(x, stencil[i], preferred_element_type=F32)

        total = times(high, 0) + times(high, 1) + times(low, 0)
        lap_z[...] = total.reshape(nx, ny, depth)

    blank = jnp.zeros((ny + 16, depth), F32)
    for i in range(4):
        ext_a[i] = blank
        ext_a[nx + 4 + i] = blank
    for x in range(nx):
        ext_a[x + 4, 0:8] = blank[0:8]
        ext_a[x + 4, ny + 8 : ny + 16] = blank[0:8]
    for load in loads[:3]:
        load.wait()

    along_z(ext_a[4 : 4 + nx, 8 : 8 + ny, :])
    for t in range(groups):
        edges = [[], [], []]
        for x in range(4 * t, 4 * t + 4):
            center = ext_a[x + 4, 8 : 8 + ny, :]
            factor = speed[x]
            partial = (
                2.0 * center - before[x] + factor * (lap_z[x] + laplace_xy(ext_a, x, ny))
            )
            out_next[x] = partial
            for i, v in enumerate((center, partial, factor)):
                edges[i].append(edge(v))
                if x < 4:
                    pack_x[0, x, i] = v.astype(BF16)
                if x >= nx - 4:
                    pack_x[1, x - nx + 4, i] = v.astype(BF16)
        for i in range(3):
            pack_y[0, t, i], pack_y[1, t, i] = pack_four(edges[i])

    for group in (copies_w, copies_g):
        for c in group:
            c.clear()
    pl.semaphore_wait(barrier, wanted)
    for c in copies_w:
        c.start()

    for load in loads[3:8]:
        load.wait()

    r1, r2 = ny + 4, ny + 2
    m1, m2 = 8 * r1, 8 * r2
    slots = 3 * ny + 32
    blk = 6

    def column(bias):
        wide = jnp.broadcast_to(bias[...], (8, 8))
        return jnp.sum(jnp.where(iota((8, 8), 0) == iota((8, 8), 1), wide, 0.0), axis=1, keepdims=True)

    b1, b2 = column(bias1), column(bias2)

    def place_first(shape, dim):
        col = iota(shape, dim)
        a = third(col, slots)
        slot = col - slots * a
        side = slot - 3 * ny
        q = side & 7
        e = jnp.where(slot < 3 * ny, third(slot, ny), side >> 3)
        y = jnp.where(slot < 3 * ny, slot - ny * e, jnp.where(q < 4, q + ny, q - 8))
        y = jnp.where(side >= 24, 999, y)
        return a, e, y, col

    a_in, e_in, _, _ = place_first((27, 3 * slots), 0 + 1)
    taps = [
        jnp.dot(
            raw1[...],
            one_hot(iota((27, 3 * slots), 0) == 9 * a_in + 3 * b + e_in),
            preferred_element_type=F32,
        )
        for b in range(3)
    ]
    _, _, y_in, col = place_first((8, 3 * slots), 1)
    top = b1.astype(BF16).astype(F32)
    rest = b1 - top
    middle = rest.astype(BF16).astype(F32)
    base = slots + 3 * ny + 24
    biases = jnp.where(col == base, top, jnp.where(col == base + 1, middle, jnp.where(col == base + 2, rest - middle, 0.0)))

    def rows_first(y):
        total = biases
        for b in range(3):
            total = jnp.where(y_in - y == b - 1, taps[b], total)
        return total

    for y in range(0, r1, 2):
        w1[8 * y : 8 * y + 16, :] = jnp.concatenate(
            [rows_first(y - 2), rows_first(y - 1)], axis=0
        ).astype(BF16)

    k2 = 8 * (blk + 2)
    same_c = (iota((64, 3 * k2), 0) >> 3) == (iota((64, 3 * k2), 1) & 7)
    a_in = third(iota((27, 3 * k2), 1), k2)
    col = iota((8, 3 * k2), 1)
    y_in = (col - k2 * third(col, k2)) >> 3
    table = []
    for t in range(9):
        full = jnp.dot(
            raw2[...], one_hot(iota((27, 3 * k2), 0) == 9 * a_in + t), preferred_element_type=F32
        )
        full = jnp.where(same_c, full, 0.0)
        total = full[0:8]
        for c in range(1, 8):
            total = total + full[8 * c : 8 * c + 8]
        table.append(total)

    def rows_mid(i):
        e, y = i // blk, i % blk
        total = jnp.zeros((8, 3 * k2), F32)
        for b in range(3):
            total = jnp.where(y_in - y == b, table[3 * b + e], total)
        return total

    for i in range(0, 3 * blk, 2):
        w2[8 * i : 8 * i + 16, :] = jnp.concatenate([rows_mid(i), rows_mid(i + 1)], axis=0).astype(BF16)

    same_c = iota((8, 3 * m2), 0) == (iota((8, 3 * m2), 1) & 7)
    a_in = third(iota((27, 3 * m2), 1), m2)
    col = iota((ny, 3 * m2), 1)
    gap = ((col - m2 * third(col, m2)) >> 3) - iota((ny, 3 * m2), 0)
    for e in range(3):
        total = jnp.zeros((ny, 3 * m2), F32)
        for b in range(3):
            full = jnp.dot(
                raw3[...],
                one_hot(iota((27, 3 * m2), 0) == 9 * a_in + 3 * b + e),
                preferred_element_type=F32,
            )
            line = jnp.sum(jnp.where(same_c, full, 0.0), axis=0, keepdims=True)
            total = jnp.where(gap == b, jnp.broadcast_to(line, total.shape), total)
        w3[ny * e : ny * e + ny, :] = total.astype(BF16)

    own = slice(8, 8 + ny)
    outside = [x for x in range(-4, nx + 4) if x < 0 or x >= nx]

    def reach(x, inside):
        return [(k, x + d * k) for k in range(1, 5) for d in (-1, 1) if inside(x + d * k)]

    for i, x in enumerate(outside):
        total = jnp.zeros((ny, depth), F32)
        for k, at in reach(x, lambda v: 0 <= v < nx):
            total = total + COEFS[k] * ext_a[at + 4, own]
        from_own_x[i] = total
    for x in range(nx):
        from_own_y[x] = across(edge(ext_a[x + 4, own]))
    for load in loads[8:]:
        load.wait()

    for c in copies_w:
        c.arrive()
    corner = {}
    for i, first in enumerate((-4, nx)):
        for j, v in enumerate(unpack_four(recv_c[i, 0], recv_c[i, 1])):
            corner[first + j] = v
    halo_x = {x: recv_x.at[i // 4, i % 4] for i, x in enumerate(outside)}
    for i, x in enumerate(outside):
        felt = from_own_x[i] + spread(across(corner[x]))
        ext_b[x + 4, own] = halo_x[x][1].astype(F32) + halo_x[x][2].astype(F32) * felt
    for t in range(groups):
        sides = [unpack_four(recv_y[0, t, i], recv_y[1, t, i]) for i in range(3)]
        for j in range(4):
            x = 4 * t + j
            felt = from_own_y[x]
            for k, at in reach(x, lambda v: v in corner):
                felt = felt + COEFS[k] * corner[at]
            side = sides[1][j] + sides[2][j] * felt
            ext_b[x + 4, 0:8] = side
            ext_b[x + 4, ny + 8 : ny + 16] = side
            felt = spread(across(sides[0][j]))
            for k, at in reach(x, lambda v: v in corner):
                felt = felt + COEFS[k] * halo_x[at][0].astype(F32)
            value = out_next[x] + speed[x] * felt
            out_next[x] = value
            ext_b[x + 4, own] = value

    def store_own(plane, value):
        for e in range(3):
            rows = value if e == 1 else shift_z(value, e - 1)
            grad[plane, ny * e : ny * e + ny, :] = rows.astype(BF16)

    along_z(out_next[...])

    def step_two(x, carry):
        center = out_next[x]
        value = 2.0 * center - ext_a[x + 4, own] + speed[x] * (lap_z[x] + laplace_xy(ext_b, x, ny))
        out_after[x] = value
        gradient = prior[x] + src[0, x] * center + src[1, x] * value
        out_grad[x] = gradient
        store_own(x + 3, gradient)
        return carry

    lax.fori_loop(0, nx, step_two, 0, unroll=WAVE_UNROLL)
    for t in range(groups):
        pack_g[0, t], pack_g[1, t] = pack_four([edge(out_grad[4 * t + j]) for j in range(4)])
    for c in copies_g:
        c.start()
    for c in copies_g:
        c.arrive()
    ones = jnp.where(iota((8, depth), 0) < 3, 1.0, 0.0)
    for t in range(groups + 2):
        for j, side in enumerate(unpack_four(recv_g[0, t], recv_g[1, t])):
            plane = 4 * t + j - 1
            if 0 <= plane < nx + 6:
                grad[plane, 3 * ny : 3 * ny + 32, :] = jnp.concatenate(
                    [shift_z(side, -1), side, shift_z(side, 1), ones], axis=0
                ).astype(BF16)
    for i in range(3):
        store_own(i, recv_gx[0, i].astype(F32))
        store_own(nx + 3 + i, recv_gx[1, i].astype(F32))

    big = 3.0e38
    x_low = jnp.where(gx == 0, 0.0, big)
    x_high = jnp.where(gx == n_gx - 1, 0.0, big)
    y_low = jnp.where(gy == 0, 0.0, big)
    y_high = jnp.where(gy == n_gy - 1, 0.0, big)

    def conv_plane(weight, rhs, rows):
        res = jnp.dot(weight[...], rhs, preferred_element_type=F32)
        return (
            res[rows : 2 * rows] + shift_z(res[:rows], -1) + shift_z(res[2 * rows :], 1)
        )

    def limit(value, cap):
        return value if cap is None else jnp.minimum(value, cap)

    for p in range(nx + 4):
        res = jnp.maximum(
            jnp.dot(w1[...], grad[p : p + 3].reshape(3 * slots, depth), preferred_element_type=F32), 0.0
        )
        cap = x_low if p < 2 else x_high if p >= nx + 2 else None
        res = limit(res, cap)
        h1[p, 0:16] = jnp.minimum(res[0:16], y_low).astype(BF16)
        h1[p, 16 : m1 - 16] = res[16 : m1 - 16].astype(BF16)
        h1[p, m1 - 16 : m1] = jnp.minimum(res[m1 - 16 : m1], y_high).astype(BF16)

    full2 = jnp.concatenate([jnp.broadcast_to(b2, (8, depth))] * blk, axis=0)
    for p in range(nx + 2):
        cap = x_low if p < 1 else x_high if p >= nx + 1 else None
        for y in range(0, r2, blk):
            rhs = h1[p : p + 3, 8 * y : 8 * y + k2, :].reshape(3 * k2, depth)
            res = limit(jnp.maximum(conv_plane(w2, rhs, 8 * blk) + full2, 0.0), cap)
            if y == 0:
                res = jnp.concatenate([jnp.minimum(res[0:8], y_low), res[8:]], axis=0)
            if y + blk == r2:
                res = jnp.concatenate([res[: 8 * blk - 8], jnp.minimum(res[8 * blk - 8 :], y_high)], axis=0)
            h2[p, 8 * y : 8 * y + 8 * blk] = res.astype(BF16)

    zero = jnp.zeros((ny, depth), F32)

    def layer_three(p, carry):
        gg, gd, dd = carry
        rhs = h2[pl.ds(p, 3)].reshape(3 * m2, depth)
        g = out_grad[p]
        d = conv_plane(w3, rhs, ny) + g
        out_dir[p] = d
        return gg + g * g, gd + g * d, dd + d * d

    sums = lax.fori_loop(0, nx, layer_three, (zero, zero, zero), unroll=UNROLL)
    row, lane = iota((8, 128), 0), iota((8, 128), 1)
    tile = jnp.zeros((8, 128), F32)
    for i, s in enumerate(sums):
        line = jnp.sum(s, axis=0, keepdims=True)
        folded = line[:, 0:128]
        for j in range(1, depth // 128):
            folded = folded + line[:, 128 * j : 128 * j + 128]
        tile = jnp.where(row == i, folded, tile)
    wide = jnp.broadcast_to(jnp.sum(tile, axis=1, keepdims=True), (8, 128))
    mine = jnp.sum(jnp.where(row == lane, wide, 0.0), axis=0, keepdims=True)
    part[...] = mine
    for i in range(1, count):
        pltpu.make_async_remote_copy(
            src_ref=part,
            dst_ref=red.at[i - 1],
            send_sem=red_send.at[i - 1],
            recv_sem=red_recv.at[i - 1],
            device_id=peer(i),
            device_id_type=MESH,
        ).start()
    waits = [
        pltpu.make_async_remote_copy(
            src_ref=part,
            dst_ref=red.at[i - 1],
            send_sem=red_send.at[i - 1],
            recv_sem=red_recv.at[i - 1],
            device_id=peer(i),
            device_id_type=MESH,
        )
        for i in range(1, count)
    ]
    for c in waits:
        c.wait_recv()
    total = mine
    for i in range(count - 1):
        total = total + red[i]
    spread = jnp.where(row == lane, jnp.broadcast_to(total, (8, 128)), 0.0)
    out_sums[...] = jnp.broadcast_to(jnp.sum(spread, axis=1, keepdims=True), (8, 128))
    for group in (copies_w, copies_g):
        for c in group:
            c.sent()
    for c in waits:
        c.wait_send()


def hand_on(damping, sums, v_next, v_after, v_grad, v_dir, o_next, o_after, o_grad, o_step, scaled, sem):
    moves = [
        pltpu.make_async_copy(source, target, sem.at[i])
        for i, (source, target) in enumerate(((v_next, o_next), (v_after, o_after), (v_grad, o_grad)))
    ]
    for move in moves:
        move.start()
    scale = sums[1:2, 0:1] / (sums[0:1, 0:1] + sums[2:3, 0:1] + damping)
    nx = v_dir.shape[0]
    step = nx // 4
    for i in range(4):
        at = pl.ds(i * step, step)
        scaled[at] = scale.reshape(1, 1, 1) * v_dir[at]
        move = pltpu.make_async_copy(scaled.at[at], o_step.at[at], sem.at[3 + i])
        move.start()
        moves.append(move)
    for move in moves:
        move.wait()


def shards(n_gx, n_gy, speed, before, now, src, prior, w_first, b_first, w_mid, b_mid, w_last):
    nx, ny, depth = now.shape
    out = jax.ShapeDtypeStruct(now.shape, F32)
    vmem = pl.BlockSpec(memory_space=pltpu.VMEM)
    hbm = pl.BlockSpec(memory_space=pltpu.HBM)
    groups = nx // 4
    r1, r2 = ny + 4, ny + 2
    ch = b_first.shape[0]
    slots, blk = 3 * ny + 32, 6
    count = n_gx * n_gy
    held = pltpu.VMEM(now.shape, F32)
    *outs, sums = pl.pallas_call(
        functools.partial(kernel, n_gx, n_gy),
        out_shape=(held,) * 4 + (pltpu.VMEM((8, 128), F32),),
        in_specs=[hbm] * 10,
        out_specs=(vmem,) * 5,
        scratch_shapes=[
            pltpu.VMEM(now.shape, F32),
            pltpu.VMEM(now.shape, F32),
            pltpu.VMEM(src.shape, F32),
            pltpu.VMEM(now.shape, F32),
            pltpu.VMEM((ch, 27), BF16),
            pltpu.VMEM((ch * ch, 27), BF16),
            pltpu.VMEM((ch, 27), BF16),
            pltpu.VMEM((1, ch), F32),
            pltpu.VMEM((1, ch), F32),
            pltpu.SemaphoreType.DMA((10,)),
            pltpu.VMEM((nx + 8, ny + 16, depth), F32),
            pltpu.VMEM((nx + 8, ny + 16, depth), F32),
            pltpu.VMEM((2, 4, 3, ny, depth), BF16),
            pltpu.VMEM((2, groups, 3, 16, depth), BF16),
            pltpu.VMEM((2, 4, 3, ny, depth), BF16),
            pltpu.VMEM((2, groups, 3, 16, depth), BF16),
            pltpu.VMEM((2, 2, 16, depth), BF16),
            pltpu.VMEM((8, ny, depth), F32),
            pltpu.VMEM((nx, 8, depth), F32),
            pltpu.VMEM((2, depth, depth), BF16),
            pltpu.VMEM(now.shape, F32),
            pltpu.VMEM((nx + 6, slots, depth), BF16),
            pltpu.VMEM((2, groups, 16, depth), BF16),
            pltpu.VMEM((2, 3, ny, depth), BF16),
            pltpu.VMEM((2, groups + 2, 16, depth), BF16),
            pltpu.VMEM((nx + 4, r1 * ch, depth), BF16),
            pltpu.VMEM((nx + 2, r2 * ch, depth), BF16),
            pltpu.VMEM((r1 * ch, 3 * slots), BF16),
            pltpu.VMEM((3 * blk * ch, 3 * (blk + 2) * ch), BF16),
            pltpu.VMEM((3 * ny, 3 * r2 * ch), BF16),
            pltpu.VMEM((1, 128), F32),
            pltpu.VMEM((count - 1, 1, 128), F32),
            pltpu.SemaphoreType.DMA((16,)),
            pltpu.SemaphoreType.DMA((16,)),
            pltpu.SemaphoreType.DMA((count - 1,)),
            pltpu.SemaphoreType.DMA((count - 1,)),
        ],
        compiler_params=pltpu.CompilerParams(
            collective_id=0, has_side_effects=True, vmem_limit_bytes=40 * 1024 * 1024
        ),
    )(
        *(
            pltpu.with_memory_space_constraint(v, pltpu.HBM)
            for v in (
                speed,
                before,
                now,
                src,
                prior,
                w_first.transpose(1, 2, 0).reshape(ch, 27),
                w_mid.transpose(1, 2, 0).reshape(ch * ch, 27),
                w_last.transpose(2, 1, 0).reshape(ch, 27),
                b_first.reshape(1, ch),
                b_mid.reshape(1, ch),
            )
        )
    )
    return pl.pallas_call(
        functools.partial(hand_on, 8.0 * float(nx * n_gx * ny * n_gy * depth)),
        out_shape=(out,) * 4,
        in_specs=[vmem] * 5,
        out_specs=(hbm,) * 4,
        scratch_shapes=[pltpu.VMEM(now.shape, F32), pltpu.SemaphoreType.DMA((7,))],
    )(*(pltpu.with_memory_space_constraint(v, pltpu.VMEM) for v in (sums, *outs)))


def solution(mesh):
    brick = P("gx", "gy", None)
    return jax.shard_map(
        functools.partial(shards, mesh.shape["gx"], mesh.shape["gy"]),
        mesh=mesh,
        in_specs=(brick, brick, brick, P(None, "gx", "gy", None), brick, P(), P(), P(), P(), P()),
        out_specs=(brick,) * 4,
        check_vma=False,
    )
```

```python
import functools

import jax
import jax.numpy as jnp
from jax import lax
from jax.experimental import pallas as pl
from jax.experimental.pallas import tpu as pltpu
from jax.sharding import PartitionSpec as P

COEFS = (-205.0 / 72.0, 8.0 / 5.0, -1.0 / 5.0, 8.0 / 315.0, -1.0 / 560.0)
MESH = pl.DeviceIdType.MESH
F32 = jnp.float32
BF16 = jnp.bfloat16
UNROLL = True
WAVE_UNROLL = 4
FAR = 3


def shift_z(v, k):
    depth = v.shape[-1]
    lane = lax.broadcasted_iota(jnp.int32, v.shape, v.ndim - 1)
    rolled = pltpu.roll(v, (-k) % depth, v.ndim - 1)
    return jnp.where((lane + k >= 0) & (lane + k < depth), rolled, 0.0)


def iota(shape, dim):
    return lax.broadcasted_iota(jnp.int32, shape, dim)


def one_hot(hit):
    return jnp.where(hit, 1.0, 0.0).astype(BF16)


def third(index, size):
    return jnp.where(index >= size, 1, 0) + jnp.where(index >= 2 * size, 1, 0)


def laplace_xy(ext, x, ny):
    total = None
    for k in range(1, 5):
        cycle = ext[x + 4 + k, 8 : 8 + ny, :] + ext[x + 4 - k, 8 : 8 + ny, :]
        cycle = cycle + ext[x + 4, 8 + k : 8 + k + ny, :]
        cycle = cycle + ext[x + 4, 8 - k : 8 - k + ny, :]
        total = COEFS[k] * cycle if total is None else total + COEFS[k] * cycle
    return total


def kernel(
    n_gx,
    n_gy,
    speed_hbm,
    before_hbm,
    now_hbm,
    src_hbm,
    prior_hbm,
    first_hbm,
    mid_hbm,
    last_hbm,
    bias1_hbm,
    bias2_hbm,
    out_next,
    out_after,
    out_grad,
    out_dir,
    out_sums,
    speed,
    before,
    src,
    prior,
    raw1,
    raw2,
    raw3,
    bias1,
    bias2,
    load_sem,
    ext_a,
    ext_b,
    pack_x,
    pack_y,
    recv_x,
    recv_y,
    recv_c,
    from_own_x,
    from_own_y,
    stencil,
    lap_z,
    grad,
    pack_g,
    recv_gx,
    recv_g,
    h1,
    h2,
    w1,
    w1_rim,
    w2,
    w2_short,
    w3,
    part,
    red,
    send_sem,
    recv_sem,
    red_send,
    red_recv,
):
    nx, ny, depth = now_hbm.shape
    gx, gy = lax.axis_index("gx"), lax.axis_index("gy")
    barrier = pltpu.get_barrier_semaphore()
    brick = pl.ds(8, ny)
    loads = [
        pltpu.make_async_copy(source, target, load_sem.at[i])
        for i, (source, target) in enumerate(
            (
                (now_hbm, ext_a.at[pl.ds(4, nx), brick, :]),
                (before_hbm, before),
                (speed_hbm, speed),
                (first_hbm, raw1),
                (mid_hbm, raw2),
                (last_hbm, raw3),
                (bias1_hbm, bias1),
                (bias2_hbm, bias2),
                (src_hbm, src),
                (prior_hbm, prior),
            )
        )
    ]
    for load in loads:
        load.start()

    def there(dx, dy):
        ok = None
        for pos, d, n in ((gx, dx, n_gx), (gy, dy, n_gy)):
            if d:
                one = (pos + d >= 0) & (pos + d < n)
                ok = one if ok is None else ok & one
        return ok

    count = n_gx * n_gy
    me = gx * n_gy + gy

    def peer(i):
        flat = lax.rem(me + i, count)
        return (lax.div(flat, n_gy), lax.rem(flat, n_gy))

    def greet(x, y):
        pl.semaphore_signal(barrier, inc=1, device_id=(x, y), device_id_type=MESH)

    def within(pos, n, d):
        return jnp.minimum(pos, d) + jnp.minimum(n - 1 - pos, d) + 1

    for dx, dy in ((0, 1), (0, -1), (1, 0), (-1, 0), (1, 1), (1, -1), (-1, 1), (-1, -1)):

        @pl.when(there(dx, dy))
        def _(dx=dx, dy=dy):
            greet(gx + dx, gy + dy)

    def far(pos, j):
        return (j - pos > FAR) | (pos - j > FAR)

    for j in range(n_gy):

        @pl.when(far(gy, j))
        def _(j=j):
            for i in range(n_gx):
                greet(i, j)

        if n_gx > FAR + 1:

            @pl.when(jnp.logical_not(far(gy, j)))
            def _(j=j):
                for i in range(n_gx):

                    @pl.when(far(gx, i))
                    def _(i=i):
                        greet(i, j)

    wanted = within(gx, n_gx, 1) * within(gy, n_gy, 1) - 1
    wanted = wanted + count - within(gx, n_gx, FAR) * within(gy, n_gy, FAR)

    class Copy:
        def __init__(self, ident, source, target, dx, dy):
            self.make = lambda: pltpu.make_async_remote_copy(
                src_ref=source,
                dst_ref=target,
                send_sem=send_sem.at[ident],
                recv_sem=recv_sem.at[ident],
                device_id=(gx + dx, gy + dy),
                device_id_type=MESH,
            )
            self.to = there(dx, dy)
            self.origin = there(-dx, -dy)
            self.target = target

        def start(self):
            @pl.when(self.to)
            def _():
                self.make().start()

        def clear(self):
            @pl.when(jnp.logical_not(self.origin))
            def _():
                self.target[...] = jnp.zeros(self.target.shape, self.target.dtype)

        def arrive(self):
            @pl.when(self.origin)
            def _():
                self.make().wait_recv()

        def sent(self):
            @pl.when(self.to)
            def _():
                self.make().wait_send()

    groups = nx // 4
    mid = pl.ds(1, groups)
    same_z = pl.ds(ny, ny)
    copies_w = (
        Copy(0, pack_y.at[1, groups - 1, 0], recv_c.at[0, 0], 1, 1),
        Copy(1, pack_y.at[1, 0, 0], recv_c.at[1, 0], -1, 1),
        Copy(2, pack_y.at[0, groups - 1, 0], recv_c.at[0, 1], 1, -1),
        Copy(3, pack_y.at[0, 0, 0], recv_c.at[1, 1], -1, -1),
        Copy(4, pack_y.at[1], recv_y.at[0], 0, 1),
        Copy(5, pack_y.at[0], recv_y.at[1], 0, -1),
        Copy(6, pack_x.at[1], recv_x.at[0], 1, 0),
        Copy(7, pack_x.at[0], recv_x.at[1], -1, 0),
    )
    copies_g = (
        Copy(12, pack_g.at[1, groups - 1], recv_g.at[0, 0], 1, 1),
        Copy(13, pack_g.at[1, 0], recv_g.at[0, groups + 1], -1, 1),
        Copy(14, pack_g.at[0, groups - 1], recv_g.at[1, 0], 1, -1),
        Copy(15, pack_g.at[0, 0], recv_g.at[1, groups + 1], -1, -1),
        Copy(10, pack_g.at[1], recv_g.at[0, mid], 0, 1),
        Copy(11, pack_g.at[0], recv_g.at[1, mid], 0, -1),
        Copy(8, grad.at[pl.ds(nx, 3), same_z, :], recv_gx.at[0], 1, 0),
        Copy(9, grad.at[pl.ds(3, 3), same_z, :], recv_gx.at[1], -1, 0),
    )

    row8 = iota((8, depth), 0)

    def half_turn(v):
        return pltpu.roll(v, 4, 0)

    def edge(v):
        return jnp.where(row8 < 4, v[0:8], v[ny - 8 : ny])

    def pack_four(e):
        low = [jnp.where(row8 < 4, e[i], half_turn(e[i + 1])) for i in (0, 2)]
        high = [jnp.where(row8 < 4, half_turn(e[i]), e[i + 1]) for i in (0, 2)]
        return [jnp.concatenate(v, axis=0).astype(BF16) for v in (low, high)]

    def unpack_four(low, high):
        sides = []
        for i in (0, 8):
            a, b = low.astype(F32)[i : i + 8], high.astype(F32)[i : i + 8]
            sides.append(jnp.where(row8 < 4, b, half_turn(a)))
            sides.append(jnp.where(row8 < 4, half_turn(b), a))
        return sides

    def across(v):
        total = jnp.zeros((8, depth), F32)
        for k in range(1, 5):
            down, up = pltpu.roll(v, k, 0), pltpu.roll(v, 8 - k, 0)
            total = total + COEFS[k] * jnp.where(row8 < k, down, jnp.where(row8 >= 8 - k, up, 0.0))
        return total

    def spread(e):
        parts = [jnp.where(row8 < 4, e, 0.0), jnp.where(row8 < 4, 0.0, e)]
        if ny > 16:
            parts.insert(1, jnp.zeros((ny - 16, depth), F32))
        return jnp.concatenate(parts, axis=0)

    gap = iota((depth, depth), 0) - iota((depth, depth), 1)
    taps = jnp.zeros((depth, depth), F32)
    for k in range(5):
        taps = jnp.where((gap == k) | (gap == -k), COEFS[k] * (1.0 if k else 3.0), taps)
    stencil[0] = taps.astype(BF16)
    stencil[1] = (taps - taps.astype(BF16).astype(F32)).astype(BF16)

    def along_z(field):
        v = field.reshape(nx * ny, depth)
        high = v.astype(BF16)
        low = (v - high.astype(F32)).astype(BF16)

        def times(x, i):
            return jnp.dot(x, stencil[i], preferred_element_type=F32)

        total = times(high, 0) + times(high, 1) + times(low, 0)
        lap_z[...] = total.reshape(nx, ny, depth)

    blank = jnp.zeros((ny + 16, depth), F32)
    for i in range(4):
        ext_a[i] = blank
        ext_a[nx + 4 + i] = blank
    for x in range(nx):
        ext_a[x + 4, 0:8] = blank[0:8]
        ext_a[x + 4, ny + 8 : ny + 16] = blank[0:8]
    for load in loads[:3]:
        load.wait()

    along_z(ext_a[4 : 4 + nx, 8 : 8 + ny, :])
    for t in range(groups):
        edges = [[], [], []]
        for x in range(4 * t, 4 * t + 4):
            center = ext_a[x + 4, 8 : 8 + ny, :]
            factor = speed[x]
            partial = (
                2.0 * center - before[x] + factor * (lap_z[x] + laplace_xy(ext_a, x, ny))
            )
            out_next[x] = partial
            for i, v in enumerate((center, partial, factor)):
                edges[i].append(edge(v))
                if x < 4:
                    pack_x[0, x, i] = v.astype(BF16)
                if x >= nx - 4:
                    pack_x[1, x - nx + 4, i] = v.astype(BF16)
        for i in range(3):
            pack_y[0, t, i], pack_y[1, t, i] = pack_four(edges[i])

    for group in (copies_w, copies_g):
        for c in group:
            c.clear()
    pl.semaphore_wait(barrier, wanted)
    for c in copies_w:
        c.start()

    for load in loads[3:8]:
        load.wait()

    r1, r2 = ny + 4, ny + 2
    m1, m2 = 8 * r1, 8 * r2
    slots = 3 * ny + 32
    blk = 6

    def column(bias):
        wide = jnp.broadcast_to(bias[...], (8, 8))
        return jnp.sum(jnp.where(iota((8, 8), 0) == iota((8, 8), 1), wide, 0.0), axis=1, keepdims=True)

    b1, b2 = column(bias1), column(bias2)

    def place_first(shape, dim):
        col = iota(shape, dim)
        a = third(col, slots)
        slot = col - slots * a
        side = slot - 3 * ny
        q = side & 7
        e = jnp.where(slot < 3 * ny, third(slot, ny), side >> 3)
        y = jnp.where(slot < 3 * ny, slot - ny * e, jnp.where(q < 4, q + ny, q - 8))
        y = jnp.where(side >= 24, 999, y)
        return a, e, y, col

    a_in, e_in, _, _ = place_first((27, 3 * slots), 0 + 1)
    taps = [
        jnp.dot(
            raw1[...],
            one_hot(iota((27, 3 * slots), 0) == 9 * a_in + 3 * b + e_in),
            preferred_element_type=F32,
        )
        for b in range(3)
    ]
    _, _, y_in, col = place_first((8, 3 * slots), 1)
    top = b1.astype(BF16).astype(F32)
    rest = b1 - top
    middle = rest.astype(BF16).astype(F32)
    base = slots + 3 * ny + 24
    biases = jnp.where(col == base, top, jnp.where(col == base + 1, middle, jnp.where(col == base + 2, rest - middle, 0.0)))

    def rows_first(y):
        total = biases
        for b in range(3):
            total = jnp.where(y_in - y == b - 1, taps[b], total)
        return total

    for y in range(0, r1, 2):
        w1[8 * y : 8 * y + 16, :] = jnp.concatenate(
            [rows_first(y - 2), rows_first(y - 1)], axis=0
        ).astype(BF16)

    w1_rim[0:32] = w1[0:32]
    w1_rim[32:64] = w1[m1 - 32 : m1]

    def fill_mid(out, size):
        wide = 8 * (size + 2)
        same_c = (iota((64, 3 * wide), 0) >> 3) == (iota((64, 3 * wide), 1) & 7)
        a_in = third(iota((27, 3 * wide), 1), wide)
        col = iota((8, 3 * wide), 1)
        y_in = (col - wide * third(col, wide)) >> 3
        table = []
        for t in range(9):
            full = jnp.dot(
                raw2[...], one_hot(iota((27, 3 * wide), 0) == 9 * a_in + t), preferred_element_type=F32
            )
            full = jnp.where(same_c, full, 0.0)
            total = full[0:8]
            for c in range(1, 8):
                total = total + full[8 * c : 8 * c + 8]
            table.append(total)

        def rows_mid(i):
            e, y = i // size, i % size
            total = jnp.zeros((8, 3 * wide), F32)
            for b in range(3):
                total = jnp.where(y_in - y == b, table[3 * b + e], total)
            return total

        for i in range(0, 3 * size, 2):
            out[8 * i : 8 * i + 16, :] = jnp.concatenate(
                [rows_mid(i), rows_mid(i + 1)], axis=0
            ).astype(BF16)

    fill_mid(w2, blk)
    fill_mid(w2_short, 4)

    same_c = iota((8, 3 * m2), 0) == (iota((8, 3 * m2), 1) & 7)
    a_in = third(iota((27, 3 * m2), 1), m2)
    col = iota((ny, 3 * m2), 1)
    gap = ((col - m2 * third(col, m2)) >> 3) - iota((ny, 3 * m2), 0)
    for e in range(3):
        total = jnp.zeros((ny, 3 * m2), F32)
        for b in range(3):
            full = jnp.dot(
                raw3[...],
                one_hot(iota((27, 3 * m2), 0) == 9 * a_in + 3 * b + e),
                preferred_element_type=F32,
            )
            line = jnp.sum(jnp.where(same_c, full, 0.0), axis=0, keepdims=True)
            total = jnp.where(gap == b, jnp.broadcast_to(line, total.shape), total)
        w3[ny * e : ny * e + ny, :] = total.astype(BF16)

    own = slice(8, 8 + ny)
    outside = [x for x in range(-4, nx + 4) if x < 0 or x >= nx]

    def reach(x, inside):
        return [(k, x + d * k) for k in range(1, 5) for d in (-1, 1) if inside(x + d * k)]

    for i, x in enumerate(outside):
        total = jnp.zeros((ny, depth), F32)
        for k, at in reach(x, lambda v: 0 <= v < nx):
            total = total + COEFS[k] * ext_a[at + 4, own]
        from_own_x[i] = total
    for x in range(nx):
        from_own_y[x] = across(edge(ext_a[x + 4, own]))
    ones = jnp.where(iota((8, depth), 0) < 3, 1.0, 0.0)
    vacant = jnp.concatenate([jnp.zeros((24, depth), F32), ones], axis=0).astype(BF16)
    for x in range(nx):
        grad[x + 3, 3 * ny : 3 * ny + 32, :] = vacant
    for load in loads[8:]:
        load.wait()

    for c in copies_w:
        c.arrive()
    corner = {}
    for i, first in enumerate((-4, nx)):
        for j, v in enumerate(unpack_four(recv_c[i, 0], recv_c[i, 1])):
            corner[first + j] = v
    halo_x = {x: recv_x.at[i // 4, i % 4] for i, x in enumerate(outside)}
    for i, x in enumerate(outside):
        felt = from_own_x[i] + spread(across(corner[x]))
        ext_b[x + 4, own] = halo_x[x][1].astype(F32) + halo_x[x][2].astype(F32) * felt
    for t in range(groups):
        sides = [unpack_four(recv_y[0, t, i], recv_y[1, t, i]) for i in range(3)]
        for j in range(4):
            x = 4 * t + j
            felt = from_own_y[x]
            for k, at in reach(x, lambda v: v in corner):
                felt = felt + COEFS[k] * corner[at]
            side = sides[1][j] + sides[2][j] * felt
            ext_b[x + 4, 0:8] = side
            ext_b[x + 4, ny + 8 : ny + 16] = side
            felt = spread(across(sides[0][j]))
            for k, at in reach(x, lambda v: v in corner):
                felt = felt + COEFS[k] * halo_x[at][0].astype(F32)
            value = out_next[x] + speed[x] * felt
            out_next[x] = value
            ext_b[x + 4, own] = value

    def store_own(plane, value):
        for e in range(3):
            rows = value if e == 1 else shift_z(value, e - 1)
            grad[plane, ny * e : ny * e + ny, :] = rows.astype(BF16)

    along_z(out_next[...])

    def step_two(x, carry):
        center = out_next[x]
        value = 2.0 * center - ext_a[x + 4, own] + speed[x] * (lap_z[x] + laplace_xy(ext_b, x, ny))
        out_after[x] = value
        gradient = prior[x] + src[0, x] * center + src[1, x] * value
        out_grad[x] = gradient
        grad[x + 3, ny : 2 * ny, :] = gradient.astype(BF16)
        return carry

    lax.fori_loop(0, nx, step_two, 0, unroll=WAVE_UNROLL)
    for t in range(groups):
        pack_g[0, t], pack_g[1, t] = pack_four([edge(out_grad[4 * t + j]) for j in range(4)])
    for c in copies_g:
        c.start()
    for x in range(nx):
        for e in (0, 2):
            grad[x + 3, ny * e : ny * e + ny, :] = shift_z(out_grad[x], e - 1).astype(BF16)

    big = 3.0e38
    x_low = jnp.where(gx == 0, 0.0, big)
    x_high = jnp.where(gx == n_gx - 1, 0.0, big)
    y_low = jnp.where(gy == 0, 0.0, big)
    y_high = jnp.where(gy == n_gy - 1, 0.0, big)

    def limit(value, cap):
        return value if cap is None else jnp.minimum(value, cap)

    def conv_plane(weight, rhs, rows):
        res = jnp.dot(weight[...], rhs, preferred_element_type=F32)
        return (
            res[rows : 2 * rows] + shift_z(res[:rows], -1) + shift_z(res[2 * rows :], 1)
        )

    def layer_one(p, weight):
        return jnp.maximum(
            jnp.dot(weight, grad[p : p + 3].reshape(3 * slots, depth), preferred_element_type=F32), 0.0
        )

    def store_rim(p, low, high):
        h1[p, 0:16] = jnp.minimum(low[0:16], y_low).astype(BF16)
        h1[p, 16:32] = low[16:32].astype(BF16)
        h1[p, m1 - 32 : m1 - 16] = high[0:16].astype(BF16)
        h1[p, m1 - 16 : m1] = jnp.minimum(high[16:32], y_high).astype(BF16)

    def layer_two(p, y, size, weight, cap):
        rhs = h1[p : p + 3, 8 * y : 8 * y + 8 * size + 16, :].reshape(24 * size + 48, depth)
        full = jnp.concatenate([jnp.broadcast_to(b2, (8, depth))] * size, axis=0)
        res = limit(jnp.maximum(conv_plane(weight, rhs, 8 * size) + full, 0.0), cap)
        if y == 0:
            res = jnp.concatenate([jnp.minimum(res[0:8], y_low), res[8:]], axis=0)
        if y + size == r2:
            res = jnp.concatenate([res[: 8 * size - 8], jnp.minimum(res[8 * size - 8 :], y_high)], axis=0)
        h2[p, 8 * y : 8 * y + 8 * size] = res.astype(BF16)

    def fill_sides(t):
        for j, side in enumerate(unpack_four(recv_g[0, t], recv_g[1, t])):
            plane = 4 * t + j - 1
            if 0 <= plane < nx + 6:
                grad[plane, 3 * ny : 3 * ny + 32, :] = jnp.concatenate(
                    [shift_z(side, -1), side, shift_z(side, 1), ones], axis=0
                ).astype(BF16)

    core_one = range(3, nx + 1)
    core_two = range(3, nx - 1)
    for p in core_one:
        h1[p, 32 : m1 - 32] = layer_one(p, w1[32 : m1 - 32]).astype(BF16)
    for p in core_two:
        layer_two(p, 4, 6, w2, None)
        layer_two(p, 10, 4, w2_short, None)
    for c in copies_g[4:6]:
        c.arrive()
    for t in range(1, groups + 1):
        fill_sides(t)
    for p in core_one:
        res = layer_one(p, w1_rim[...])
        store_rim(p, res[0:32], res[32:64])
    for p in core_two:
        layer_two(p, 0, 4, w2_short, None)
        layer_two(p, 14, 4, w2_short, None)
    for c in copies_g[:4] + copies_g[6:]:
        c.arrive()
    for t in (0, groups + 1):
        fill_sides(t)
    for i in range(3):
        store_own(i, recv_gx[0, i].astype(F32))
        store_own(nx + 3 + i, recv_gx[1, i].astype(F32))
    for p in range(nx + 4):
        if p not in core_one:
            cap = x_low if p < 2 else x_high if p >= nx + 2 else None
            res = limit(layer_one(p, w1[...]), cap)
            store_rim(p, res[0:32], res[m1 - 32 : m1])
            h1[p, 32 : m1 - 32] = res[32 : m1 - 32].astype(BF16)
    for p in range(nx + 2):
        if p not in core_two:
            cap = x_low if p < 1 else x_high if p >= nx + 1 else None
            for y in range(0, r2, blk):
                layer_two(p, y, blk, w2, cap)

    zero = jnp.zeros((ny, depth), F32)

    def layer_three(p, carry):
        gg, gd, dd = carry
        rhs = h2[pl.ds(p, 3)].reshape(3 * m2, depth)
        g = out_grad[p]
        d = conv_plane(w3, rhs, ny) + g
        out_dir[p] = d
        return gg + g * g, gd + g * d, dd + d * d

    sums = lax.fori_loop(0, nx, layer_three, (zero, zero, zero), unroll=UNROLL)
    row, lane = iota((8, 128), 0), iota((8, 128), 1)
    tile = jnp.zeros((8, 128), F32)
    for i, s in enumerate(sums):
        line = jnp.sum(s, axis=0, keepdims=True)
        folded = line[:, 0:128]
        for j in range(1, depth // 128):
            folded = folded + line[:, 128 * j : 128 * j + 128]
        tile = jnp.where(row == i, folded, tile)
    wide = jnp.broadcast_to(jnp.sum(tile, axis=1, keepdims=True), (8, 128))
    mine = jnp.sum(jnp.where(row == lane, wide, 0.0), axis=0, keepdims=True)
    part[...] = mine
    for i in range(1, count):
        pltpu.make_async_remote_copy(
            src_ref=part,
            dst_ref=red.at[i - 1],
            send_sem=red_send.at[i - 1],
            recv_sem=red_recv.at[i - 1],
            device_id=peer(i),
            device_id_type=MESH,
        ).start()
    waits = [
        pltpu.make_async_remote_copy(
            src_ref=part,
            dst_ref=red.at[i - 1],
            send_sem=red_send.at[i - 1],
            recv_sem=red_recv.at[i - 1],
            device_id=peer(i),
            device_id_type=MESH,
        )
        for i in range(1, count)
    ]
    for c in waits:
        c.wait_recv()
    total = mine
    for i in range(count - 1):
        total = total + red[i]
    spread = jnp.where(row == lane, jnp.broadcast_to(total, (8, 128)), 0.0)
    out_sums[...] = jnp.broadcast_to(jnp.sum(spread, axis=1, keepdims=True), (8, 128))
    for group in (copies_w, copies_g):
        for c in group:
            c.sent()
    for c in waits:
        c.wait_send()


def hand_on(damping, sums, v_next, v_after, v_grad, v_dir, o_next, o_after, o_grad, o_step, scaled, sem):
    moves = [
        pltpu.make_async_copy(source, target, sem.at[i])
        for i, (source, target) in enumerate(((v_next, o_next), (v_after, o_after), (v_grad, o_grad)))
    ]
    for move in moves:
        move.start()
    scale = sums[1:2, 0:1] / (sums[0:1, 0:1] + sums[2:3, 0:1] + damping)
    nx = v_dir.shape[0]
    step = nx // 4
    for i in range(4):
        at = pl.ds(i * step, step)
        scaled[at] = scale.reshape(1, 1, 1) * v_dir[at]
        move = pltpu.make_async_copy(scaled.at[at], o_step.at[at], sem.at[3 + i])
        move.start()
        moves.append(move)
    for move in moves:
        move.wait()


def shards(n_gx, n_gy, speed, before, now, src, prior, w_first, b_first, w_mid, b_mid, w_last):
    nx, ny, depth = now.shape
    out = jax.ShapeDtypeStruct(now.shape, F32)
    vmem = pl.BlockSpec(memory_space=pltpu.VMEM)
    hbm = pl.BlockSpec(memory_space=pltpu.HBM)
    groups = nx // 4
    r1, r2 = ny + 4, ny + 2
    ch = b_first.shape[0]
    slots, blk = 3 * ny + 32, 6
    count = n_gx * n_gy
    held = pltpu.VMEM(now.shape, F32)
    *outs, sums = pl.pallas_call(
        functools.partial(kernel, n_gx, n_gy),
        out_shape=(held,) * 4 + (pltpu.VMEM((8, 128), F32),),
        in_specs=[hbm] * 10,
        out_specs=(vmem,) * 5,
        scratch_shapes=[
            pltpu.VMEM(now.shape, F32),
            pltpu.VMEM(now.shape, F32),
            pltpu.VMEM(src.shape, F32),
            pltpu.VMEM(now.shape, F32),
            pltpu.VMEM((ch, 27), BF16),
            pltpu.VMEM((ch * ch, 27), BF16),
            pltpu.VMEM((ch, 27), BF16),
            pltpu.VMEM((1, ch), F32),
            pltpu.VMEM((1, ch), F32),
            pltpu.SemaphoreType.DMA((10,)),
            pltpu.VMEM((nx + 8, ny + 16, depth), F32),
            pltpu.VMEM((nx + 8, ny + 16, depth), F32),
            pltpu.VMEM((2, 4, 3, ny, depth), BF16),
            pltpu.VMEM((2, groups, 3, 16, depth), BF16),
            pltpu.VMEM((2, 4, 3, ny, depth), BF16),
            pltpu.VMEM((2, groups, 3, 16, depth), BF16),
            pltpu.VMEM((2, 2, 16, depth), BF16),
            pltpu.VMEM((8, ny, depth), F32),
            pltpu.VMEM((nx, 8, depth), F32),
            pltpu.VMEM((2, depth, depth), BF16),
            pltpu.VMEM(now.shape, F32),
            pltpu.VMEM((nx + 6, slots, depth), BF16),
            pltpu.VMEM((2, groups, 16, depth), BF16),
            pltpu.VMEM((2, 3, ny, depth), BF16),
            pltpu.VMEM((2, groups + 2, 16, depth), BF16),
            pltpu.VMEM((nx + 4, r1 * ch, depth), BF16),
            pltpu.VMEM((nx + 2, r2 * ch, depth), BF16),
            pltpu.VMEM((r1 * ch, 3 * slots), BF16),
            pltpu.VMEM((64, 3 * slots), BF16),
            pltpu.VMEM((3 * blk * ch, 3 * (blk + 2) * ch), BF16),
            pltpu.VMEM((12 * ch, 18 * ch), BF16),
            pltpu.VMEM((3 * ny, 3 * r2 * ch), BF16),
            pltpu.VMEM((1, 128), F32),
            pltpu.VMEM((count - 1, 1, 128), F32),
            pltpu.SemaphoreType.DMA((16,)),
            pltpu.SemaphoreType.DMA((16,)),
            pltpu.SemaphoreType.DMA((count - 1,)),
            pltpu.SemaphoreType.DMA((count - 1,)),
        ],
        compiler_params=pltpu.CompilerParams(
            collective_id=0, has_side_effects=True, vmem_limit_bytes=40 * 1024 * 1024
        ),
    )(
        *(
            pltpu.with_memory_space_constraint(v, pltpu.HBM)
            for v in (
                speed,
                before,
                now,
                src,
                prior,
                w_first.transpose(1, 2, 0).reshape(ch, 27),
                w_mid.transpose(1, 2, 0).reshape(ch * ch, 27),
                w_last.transpose(2, 1, 0).reshape(ch, 27),
                b_first.reshape(1, ch),
                b_mid.reshape(1, ch),
            )
        )
    )
    return pl.pallas_call(
        functools.partial(hand_on, 8.0 * float(nx * n_gx * ny * n_gy * depth)),
        out_shape=(out,) * 4,
        in_specs=[vmem] * 5,
        out_specs=(hbm,) * 4,
        scratch_shapes=[pltpu.VMEM(now.shape, F32), pltpu.SemaphoreType.DMA((7,))],
    )(*(pltpu.with_memory_space_constraint(v, pltpu.VMEM) for v in (sums, *outs)))


def solution(mesh):
    brick = P("gx", "gy", None)
    return jax.shard_map(
        functools.partial(shards, mesh.shape["gx"], mesh.shape["gy"]),
        mesh=mesh,
        in_specs=(brick, brick, brick, P(None, "gx", "gy", None), brick, P(), P(), P(), P(), P()),
        out_specs=(brick,) * 4,
        check_vma=False,
    )
```

```python
import functools

import jax
import jax.numpy as jnp
from jax import lax
from jax.experimental import pallas as pl
from jax.experimental.pallas import tpu as pltpu
from jax.sharding import PartitionSpec as P

COEFS = (-205.0 / 72.0, 8.0 / 5.0, -1.0 / 5.0, 8.0 / 315.0, -1.0 / 560.0)
MESH = pl.DeviceIdType.MESH
F32 = jnp.float32
BF16 = jnp.bfloat16
UNROLL = True
WAVE_UNROLL = 4
FAR = 3


def shift_z(v, k):
    depth = v.shape[-1]
    lane = lax.broadcasted_iota(jnp.int32, v.shape, v.ndim - 1)
    rolled = pltpu.roll(v, (-k) % depth, v.ndim - 1)
    return jnp.where((lane + k >= 0) & (lane + k < depth), rolled, 0.0)


def iota(shape, dim):
    return lax.broadcasted_iota(jnp.int32, shape, dim)


def one_hot(hit):
    return jnp.where(hit, 1.0, 0.0).astype(BF16)


def third(index, size):
    return jnp.where(index >= size, 1, 0) + jnp.where(index >= 2 * size, 1, 0)


def kernel(
    n_gx,
    n_gy,
    speed_hbm,
    before_hbm,
    now_hbm,
    src_hbm,
    prior_hbm,
    first_hbm,
    mid_hbm,
    last_hbm,
    bias1_hbm,
    bias2_hbm,
    out_next,
    out_after,
    out_grad,
    out_dir,
    out_sums,
    speed,
    before,
    src,
    prior,
    raw1,
    raw2,
    raw3,
    bias1,
    bias2,
    load_sem,
    now,
    star,
    wave,
    pack_x,
    pack_y,
    recv_x,
    recv_y,
    recv_c,
    from_own_x,
    from_own_y,
    stencil,
    lap_z,
    grad,
    pack_g,
    recv_gx,
    recv_g,
    h1,
    h2,
    w1,
    w1_rim,
    w2,
    w2_short,
    w3,
    part,
    red,
    send_sem,
    recv_sem,
    red_send,
    red_recv,
):
    nx, ny, depth = now_hbm.shape
    gx, gy = lax.axis_index("gx"), lax.axis_index("gy")
    barrier = pltpu.get_barrier_semaphore()
    loads = [
        pltpu.make_async_copy(source, target, load_sem.at[i])
        for i, (source, target) in enumerate(
            (
                (now_hbm, now),
                (before_hbm, before),
                (speed_hbm, speed),
                (first_hbm, raw1),
                (mid_hbm, raw2),
                (last_hbm, raw3),
                (bias1_hbm, bias1),
                (bias2_hbm, bias2),
                (src_hbm, src),
                (prior_hbm, prior),
            )
        )
    ]
    for load in loads[:3]:
        load.start()

    def there(dx, dy):
        ok = None
        for pos, d, n in ((gx, dx, n_gx), (gy, dy, n_gy)):
            if d:
                one = (pos + d >= 0) & (pos + d < n)
                ok = one if ok is None else ok & one
        return ok

    count = n_gx * n_gy
    me = gx * n_gy + gy

    def peer(i):
        flat = lax.rem(me + i, count)
        return (lax.div(flat, n_gy), lax.rem(flat, n_gy))

    def greet(x, y):
        pl.semaphore_signal(barrier, inc=1, device_id=(x, y), device_id_type=MESH)

    def within(pos, n, d):
        return jnp.minimum(pos, d) + jnp.minimum(n - 1 - pos, d) + 1

    for dx, dy in ((0, 1), (0, -1), (1, 0), (-1, 0), (1, 1), (1, -1), (-1, 1), (-1, -1)):

        @pl.when(there(dx, dy))
        def _(dx=dx, dy=dy):
            greet(gx + dx, gy + dy)

    for load in loads[3:]:
        load.start()

    def far(pos, j):
        return (j - pos > FAR) | (pos - j > FAR)

    for j in range(n_gy):

        @pl.when(far(gy, j))
        def _(j=j):
            for i in range(n_gx):
                greet(i, j)

        if n_gx > FAR + 1:

            @pl.when(jnp.logical_not(far(gy, j)))
            def _(j=j):
                for i in range(n_gx):

                    @pl.when(far(gx, i))
                    def _(i=i):
                        greet(i, j)

    wanted = within(gx, n_gx, 1) * within(gy, n_gy, 1) - 1
    wanted = wanted + count - within(gx, n_gx, FAR) * within(gy, n_gy, FAR)

    class Copy:
        def __init__(self, ident, source, target, dx, dy):
            self.make = lambda: pltpu.make_async_remote_copy(
                src_ref=source,
                dst_ref=target,
                send_sem=send_sem.at[ident],
                recv_sem=recv_sem.at[ident],
                device_id=(gx + dx, gy + dy),
                device_id_type=MESH,
            )
            self.to = there(dx, dy)
            self.origin = there(-dx, -dy)
            self.target = target

        def start(self):
            @pl.when(self.to)
            def _():
                self.make().start()

        def clear(self):
            @pl.when(jnp.logical_not(self.origin))
            def _():
                self.target[...] = jnp.zeros(self.target.shape, self.target.dtype)

        def arrive(self):
            @pl.when(self.origin)
            def _():
                self.make().wait_recv()

        def sent(self):
            @pl.when(self.to)
            def _():
                self.make().wait_send()

    groups = nx // 4
    mid = pl.ds(1, groups)
    same_z = pl.ds(ny, ny)
    copies_w = (
        Copy(0, pack_y.at[1, groups - 1, 0], recv_c.at[0, 0], 1, 1),
        Copy(1, pack_y.at[1, 0, 0], recv_c.at[1, 0], -1, 1),
        Copy(2, pack_y.at[0, groups - 1, 0], recv_c.at[0, 1], 1, -1),
        Copy(3, pack_y.at[0, 0, 0], recv_c.at[1, 1], -1, -1),
        Copy(4, pack_y.at[1], recv_y.at[0], 0, 1),
        Copy(5, pack_y.at[0], recv_y.at[1], 0, -1),
        Copy(6, pack_x.at[1], recv_x.at[0], 1, 0),
        Copy(7, pack_x.at[0], recv_x.at[1], -1, 0),
    )
    copies_g = (
        Copy(12, pack_g.at[1, groups - 1], recv_g.at[0, 0], 1, 1),
        Copy(13, pack_g.at[1, 0], recv_g.at[0, groups + 1], -1, 1),
        Copy(14, pack_g.at[0, groups - 1], recv_g.at[1, 0], 1, -1),
        Copy(15, pack_g.at[0, 0], recv_g.at[1, groups + 1], -1, -1),
        Copy(10, pack_g.at[1], recv_g.at[0, mid], 0, 1),
        Copy(11, pack_g.at[0], recv_g.at[1, mid], 0, -1),
        Copy(8, grad.at[pl.ds(nx, 3), same_z, :], recv_gx.at[0], 1, 0),
        Copy(9, grad.at[pl.ds(3, 3), same_z, :], recv_gx.at[1], -1, 0),
    )

    row8 = iota((8, depth), 0)

    def half_turn(v):
        return pltpu.roll(v, 4, 0)

    def edge(v):
        return jnp.where(row8 < 4, v[0:8], v[ny - 8 : ny])

    def pack_four(e):
        low = [jnp.where(row8 < 4, e[i], half_turn(e[i + 1])) for i in (0, 2)]
        high = [jnp.where(row8 < 4, half_turn(e[i]), e[i + 1]) for i in (0, 2)]
        return [jnp.concatenate(v, axis=0).astype(BF16) for v in (low, high)]

    def unpack_four(low, high):
        sides = []
        for i in (0, 8):
            a, b = low.astype(F32)[i : i + 8], high.astype(F32)[i : i + 8]
            sides.append(jnp.where(row8 < 4, b, half_turn(a)))
            sides.append(jnp.where(row8 < 4, half_turn(b), a))
        return sides

    def across(v):
        total = jnp.zeros((8, depth), F32)
        for k in range(1, 5):
            down, up = pltpu.roll(v, k, 0), pltpu.roll(v, 8 - k, 0)
            total = total + COEFS[k] * jnp.where(row8 < k, down, jnp.where(row8 >= 8 - k, up, 0.0))
        return total

    def spread(e):
        parts = [jnp.where(row8 < 4, e, 0.0), jnp.where(row8 < 4, 0.0, e)]
        if ny > 16:
            parts.insert(1, jnp.zeros((ny - 16, depth), F32))
        return jnp.concatenate(parts, axis=0)

    gap = iota((depth, depth), 0) - iota((depth, depth), 1)
    taps = jnp.zeros((depth, depth), F32)
    for k in range(5):
        taps = jnp.where((gap == k) | (gap == -k), COEFS[k] * (1.0 if k else 3.0), taps)
    stencil[0] = taps.astype(BF16)
    stencil[1] = (taps - taps.astype(BF16).astype(F32)).astype(BF16)

    cells = nx * ny
    bits = ny.bit_length() - 1

    def split(v):
        high = v.astype(BF16)
        return high, (v - high.astype(F32)).astype(BF16)

    def fill_star(start, width, place):
        row, col = iota((cells, width), 0), iota((cells, width), 1)
        x_in, y_in = place(col)
        dx, dy = x_in - (row >> bits), y_in - (row & (ny - 1))
        far = jnp.where(dx == 0, jnp.abs(dy), jnp.where(dy == 0, jnp.abs(dx), 0))
        value = jnp.zeros((cells, width), F32)
        for k in range(1, 5):
            value = jnp.where(far == k, COEFS[k], value)
        at = slice(start, start + width)
        star[0, :, at], star[1, :, at] = split(value)

    def laplace(high, low, width):
        def times(x, y):
            return jnp.dot(x, y, preferred_element_type=F32)

        total = times(high[0:cells], stencil[0]) + times(high[0:cells], stencil[1])
        total = total + times(low[0:cells], stencil[0])
        total = total + times(star[0, :, 0:width], high[0:width]) + times(star[1, :, 0:width], high[0:width])
        total = total + times(star[0, :, 0:width], low[0:width])
        lap_z[...] = total.reshape(nx, ny, depth)

    fill_star(0, cells, lambda col: (col >> bits, col & (ny - 1)))
    for load in loads[:3]:
        load.wait()

    laplace(*split(now[...].reshape(cells, depth)), cells)
    for t in range(groups):
        edges = [[], [], []]
        for x in range(4 * t, 4 * t + 4):
            center = now[x]
            factor = speed[x]
            partial = 2.0 * center - before[x] + factor * lap_z[x]
            out_next[x] = partial
            for i, v in enumerate((center, partial, factor)):
                edges[i].append(edge(v))
                if x < 4:
                    pack_x[0, x, i] = v.astype(BF16)
                if x >= nx - 4:
                    pack_x[1, x - nx + 4, i] = v.astype(BF16)
        for i in range(3):
            pack_y[0, t, i], pack_y[1, t, i] = pack_four(edges[i])

    for group in (copies_w, copies_g):
        for c in group:
            c.clear()
    pl.semaphore_wait(barrier, wanted)
    for c in copies_w:
        c.start()

    for load in loads[3:8]:
        load.wait()

    r1, r2 = ny + 4, ny + 2
    m1, m2 = 8 * r1, 8 * r2
    slots = 3 * ny + 32
    blk = 6

    def column(bias):
        wide = jnp.broadcast_to(bias[...], (8, 8))
        return jnp.sum(jnp.where(iota((8, 8), 0) == iota((8, 8), 1), wide, 0.0), axis=1, keepdims=True)

    b1, b2 = column(bias1), column(bias2)

    def place_first(shape, dim):
        col = iota(shape, dim)
        a = third(col, slots)
        slot = col - slots * a
        side = slot - 3 * ny
        q = side & 7
        e = jnp.where(slot < 3 * ny, third(slot, ny), side >> 3)
        y = jnp.where(slot < 3 * ny, slot - ny * e, jnp.where(q < 4, q + ny, q - 8))
        y = jnp.where(side >= 24, 999, y)
        return a, e, y, col

    a_in, e_in, _, _ = place_first((27, 3 * slots), 0 + 1)
    taps = [
        jnp.dot(
            raw1[...],
            one_hot(iota((27, 3 * slots), 0) == 9 * a_in + 3 * b + e_in),
            preferred_element_type=F32,
        )
        for b in range(3)
    ]
    _, _, y_in, col = place_first((8, 3 * slots), 1)
    top = b1.astype(BF16).astype(F32)
    rest = b1 - top
    middle = rest.astype(BF16).astype(F32)
    base = slots + 3 * ny + 24
    biases = jnp.where(col == base, top, jnp.where(col == base + 1, middle, jnp.where(col == base + 2, rest - middle, 0.0)))

    def rows_first(y):
        total = biases
        for b in range(3):
            total = jnp.where(y_in - y == b - 1, taps[b], total)
        return total

    for y in range(0, r1, 2):
        w1[8 * y : 8 * y + 16, :] = jnp.concatenate(
            [rows_first(y - 2), rows_first(y - 1)], axis=0
        ).astype(BF16)

    w1_rim[0:32] = w1[0:32]
    w1_rim[32:64] = w1[m1 - 32 : m1]

    def fill_mid(out, size):
        wide = 8 * (size + 2)
        same_c = (iota((64, 3 * wide), 0) >> 3) == (iota((64, 3 * wide), 1) & 7)
        a_in = third(iota((27, 3 * wide), 1), wide)
        col = iota((8, 3 * wide), 1)
        y_in = (col - wide * third(col, wide)) >> 3
        table = []
        for t in range(9):
            full = jnp.dot(
                raw2[...], one_hot(iota((27, 3 * wide), 0) == 9 * a_in + t), preferred_element_type=F32
            )
            full = jnp.where(same_c, full, 0.0)
            total = full[0:8]
            for c in range(1, 8):
                total = total + full[8 * c : 8 * c + 8]
            table.append(total)

        def rows_mid(i):
            e, y = i // size, i % size
            total = jnp.zeros((8, 3 * wide), F32)
            for b in range(3):
                total = jnp.where(y_in - y == b, table[3 * b + e], total)
            return total

        for i in range(0, 3 * size, 2):
            out[8 * i : 8 * i + 16, :] = jnp.concatenate(
                [rows_mid(i), rows_mid(i + 1)], axis=0
            ).astype(BF16)

    fill_mid(w2, blk)
    fill_mid(w2_short, 4)

    same_c = iota((8, 3 * m2), 0) == (iota((8, 3 * m2), 1) & 7)
    a_in = third(iota((27, 3 * m2), 1), m2)
    col = iota((ny, 3 * m2), 1)
    gap = ((col - m2 * third(col, m2)) >> 3) - iota((ny, 3 * m2), 0)
    for e in range(3):
        total = jnp.zeros((ny, 3 * m2), F32)
        for b in range(3):
            full = jnp.dot(
                raw3[...],
                one_hot(iota((27, 3 * m2), 0) == 9 * a_in + 3 * b + e),
                preferred_element_type=F32,
            )
            line = jnp.sum(jnp.where(same_c, full, 0.0), axis=0, keepdims=True)
            total = jnp.where(gap == b, jnp.broadcast_to(line, total.shape), total)
        w3[ny * e : ny * e + ny, :] = total.astype(BF16)

    outside = [x for x in range(-4, nx + 4) if x < 0 or x >= nx]

    def reach(x, inside):
        return [(k, x + d * k) for k in range(1, 5) for d in (-1, 1) if inside(x + d * k)]

    for i, x in enumerate(outside):
        total = jnp.zeros((ny, depth), F32)
        for k, at in reach(x, lambda v: 0 <= v < nx):
            total = total + COEFS[k] * now[at]
        from_own_x[i] = total
    for x in range(nx):
        from_own_y[x] = across(edge(now[x]))
    fill_star(
        cells,
        8 * ny,
        lambda col: ((col >> bits) + jnp.where((col >> bits) < 4, -4, nx - 4), col & (ny - 1)),
    )
    fill_star(
        cells + 8 * ny,
        8 * nx,
        lambda col: (col >> 3, (col & 7) + jnp.where((col & 7) < 4, ny, -8)),
    )
    ones = jnp.where(iota((8, depth), 0) < 3, 1.0, 0.0)
    vacant = jnp.concatenate([jnp.zeros((24, depth), F32), ones], axis=0).astype(BF16)
    for x in range(nx):
        grad[x + 3, 3 * ny : 3 * ny + 32, :] = vacant
    for load in loads[8:]:
        load.wait()

    for c in copies_w:
        c.arrive()
    def keep(start, value):
        at = slice(start, start + value.shape[0])
        wave[0, at], wave[1, at] = split(value)

    corner = {}
    for i, first in enumerate((-4, nx)):
        for j, v in enumerate(unpack_four(recv_c[i, 0], recv_c[i, 1])):
            corner[first + j] = v
    halo_x = {x: recv_x.at[i // 4, i % 4] for i, x in enumerate(outside)}
    for i, x in enumerate(outside):
        felt = from_own_x[i] + spread(across(corner[x]))
        keep(cells + ny * i, halo_x[x][1].astype(F32) + halo_x[x][2].astype(F32) * felt)
    for t in range(groups):
        sides = [unpack_four(recv_y[0, t, i], recv_y[1, t, i]) for i in range(3)]
        for j in range(4):
            x = 4 * t + j
            felt = from_own_y[x]
            for k, at in reach(x, lambda v: v in corner):
                felt = felt + COEFS[k] * corner[at]
            side = sides[1][j] + sides[2][j] * felt
            if x % 2:
                keep(cells + 8 * ny + 8 * (x - 1), jnp.concatenate([before_side, side], axis=0))
            before_side = side
            felt = spread(across(sides[0][j]))
            for k, at in reach(x, lambda v: v in corner):
                felt = felt + COEFS[k] * halo_x[at][0].astype(F32)
            value = out_next[x] + speed[x] * felt
            out_next[x] = value
            keep(ny * x, value)

    def store_own(plane, value):
        for e in range(3):
            rows = value if e == 1 else shift_z(value, e - 1)
            grad[plane, ny * e : ny * e + ny, :] = rows.astype(BF16)

    laplace(wave.at[0], wave.at[1], cells + 8 * ny + 8 * nx)

    def step_two(x, carry):
        center = out_next[x]
        value = 2.0 * center - now[x] + speed[x] * lap_z[x]
        out_after[x] = value
        gradient = prior[x] + src[0, x] * center + src[1, x] * value
        out_grad[x] = gradient
        grad[x + 3, ny : 2 * ny, :] = gradient.astype(BF16)
        return carry

    lax.fori_loop(0, nx, step_two, 0, unroll=WAVE_UNROLL)
    for t in range(groups):
        pack_g[0, t], pack_g[1, t] = pack_four([edge(out_grad[4 * t + j]) for j in range(4)])
    for c in copies_g:
        c.start()
    for x in range(nx):
        for e in (0, 2):
            grad[x + 3, ny * e : ny * e + ny, :] = shift_z(out_grad[x], e - 1).astype(BF16)

    big = 3.0e38
    x_low = jnp.where(gx == 0, 0.0, big)
    x_high = jnp.where(gx == n_gx - 1, 0.0, big)
    y_low = jnp.where(gy == 0, 0.0, big)
    y_high = jnp.where(gy == n_gy - 1, 0.0, big)

    def limit(value, cap):
        return value if cap is None else jnp.minimum(value, cap)

    def conv_plane(weight, rhs, rows):
        res = jnp.dot(weight[...], rhs, preferred_element_type=F32)
        return (
            res[rows : 2 * rows] + shift_z(res[:rows], -1) + shift_z(res[2 * rows :], 1)
        )

    def layer_one(p, weight):
        return jnp.maximum(
            jnp.dot(weight, grad[p : p + 3].reshape(3 * slots, depth), preferred_element_type=F32), 0.0
        )

    def store_rim(p, low, high):
        h1[p, 0:16] = jnp.minimum(low[0:16], y_low).astype(BF16)
        h1[p, 16:32] = low[16:32].astype(BF16)
        h1[p, m1 - 32 : m1 - 16] = high[0:16].astype(BF16)
        h1[p, m1 - 16 : m1] = jnp.minimum(high[16:32], y_high).astype(BF16)

    def layer_two(p, y, size, weight, cap):
        rhs = h1[p : p + 3, 8 * y : 8 * y + 8 * size + 16, :].reshape(24 * size + 48, depth)
        full = jnp.concatenate([jnp.broadcast_to(b2, (8, depth))] * size, axis=0)
        res = limit(jnp.maximum(conv_plane(weight, rhs, 8 * size) + full, 0.0), cap)
        if y == 0:
            res = jnp.concatenate([jnp.minimum(res[0:8], y_low), res[8:]], axis=0)
        if y + size == r2:
            res = jnp.concatenate([res[: 8 * size - 8], jnp.minimum(res[8 * size - 8 :], y_high)], axis=0)
        h2[p, 8 * y : 8 * y + 8 * size] = res.astype(BF16)

    def fill_sides(t):
        for j, side in enumerate(unpack_four(recv_g[0, t], recv_g[1, t])):
            plane = 4 * t + j - 1
            if 0 <= plane < nx + 6:
                grad[plane, 3 * ny : 3 * ny + 32, :] = jnp.concatenate(
                    [shift_z(side, -1), side, shift_z(side, 1), ones], axis=0
                ).astype(BF16)

    core_one = range(3, nx + 1)
    core_two = range(3, nx - 1)
    for p in core_one:
        h1[p, 32 : m1 - 32] = layer_one(p, w1[32 : m1 - 32]).astype(BF16)
    for p in core_two:
        layer_two(p, 4, 6, w2, None)
        layer_two(p, 10, 4, w2_short, None)
    for c in copies_g[4:6]:
        c.arrive()
    for t in range(1, groups + 1):
        fill_sides(t)
    for p in core_one:
        res = layer_one(p, w1_rim[...])
        store_rim(p, res[0:32], res[32:64])
    for p in core_two:
        layer_two(p, 0, 4, w2_short, None)
        layer_two(p, 14, 4, w2_short, None)
    zero = jnp.zeros((ny, depth), F32)

    def layer_three(p, carry):
        gg, gd, dd = carry
        rhs = h2[p : p + 3].reshape(3 * m2, depth)
        g = out_grad[p]
        d = conv_plane(w3, rhs, ny) + g
        out_dir[p] = d
        return gg + g * g, gd + g * d, dd + d * d

    sums = (zero, zero, zero)
    core_three = range(3, nx - 3)
    for p in core_three:
        sums = layer_three(p, sums)
    for c in copies_g[:4] + copies_g[6:]:
        c.arrive()
    for t in (0, groups + 1):
        fill_sides(t)
    for i in range(3):
        store_own(i, recv_gx[0, i].astype(F32))
        store_own(nx + 3 + i, recv_gx[1, i].astype(F32))
    for p in range(nx + 4):
        if p not in core_one:
            cap = x_low if p < 2 else x_high if p >= nx + 2 else None
            res = limit(layer_one(p, w1[...]), cap)
            store_rim(p, res[0:32], res[m1 - 32 : m1])
            h1[p, 32 : m1 - 32] = res[32 : m1 - 32].astype(BF16)
    for p in range(nx + 2):
        if p not in core_two:
            cap = x_low if p < 1 else x_high if p >= nx + 1 else None
            for y in range(0, r2, blk):
                layer_two(p, y, blk, w2, cap)

    for p in range(nx):
        if p not in core_three:
            sums = layer_three(p, sums)
    row, lane = iota((8, 128), 0), iota((8, 128), 1)
    tile = jnp.zeros((8, 128), F32)
    for i, s in enumerate(sums):
        line = jnp.sum(s, axis=0, keepdims=True)
        folded = line[:, 0:128]
        for j in range(1, depth // 128):
            folded = folded + line[:, 128 * j : 128 * j + 128]
        tile = jnp.where(row == i, folded, tile)
    wide = jnp.broadcast_to(jnp.sum(tile, axis=1, keepdims=True), (8, 128))
    mine = jnp.sum(jnp.where(row == lane, wide, 0.0), axis=0, keepdims=True)
    part[...] = mine
    for i in range(1, count):
        pltpu.make_async_remote_copy(
            src_ref=part,
            dst_ref=red.at[i - 1],
            send_sem=red_send,
            recv_sem=red_recv,
            device_id=peer(i),
            device_id_type=MESH,
        ).start()
    for group in (copies_w, copies_g):
        for c in group:
            c.sent()
    every = pltpu.make_async_remote_copy(
        src_ref=red,
        dst_ref=red,
        send_sem=red_send,
        recv_sem=red_recv,
        device_id=peer(1),
        device_id_type=MESH,
    )
    every.wait_recv()
    terms = [mine] + [red[i] for i in range(count - 1)]
    while len(terms) > 1:
        pairs = [terms[i] + terms[i + 1] for i in range(0, len(terms) - 1, 2)]
        terms = pairs + terms[2 * len(pairs) :]
    total = terms[0]
    spread = jnp.where(row == lane, jnp.broadcast_to(total, (8, 128)), 0.0)
    out_sums[...] = jnp.broadcast_to(jnp.sum(spread, axis=1, keepdims=True), (8, 128))
    every.wait_send()


def hand_on(damping, sums, v_next, v_after, v_grad, v_dir, o_next, o_after, o_grad, o_step, scaled, sem):
    moves = [
        pltpu.make_async_copy(source, target, sem.at[i])
        for i, (source, target) in enumerate(((v_next, o_next), (v_after, o_after), (v_grad, o_grad)))
    ]
    for move in moves:
        move.start()
    scale = sums[1:2, 0:1] / (sums[0:1, 0:1] + sums[2:3, 0:1] + damping)
    nx = v_dir.shape[0]
    step = nx // 4
    for i in range(4):
        at = pl.ds(i * step, step)
        scaled[at] = scale.reshape(1, 1, 1) * v_dir[at]
        move = pltpu.make_async_copy(scaled.at[at], o_step.at[at], sem.at[3 + i])
        move.start()
        moves.append(move)
    for move in moves:
        move.wait()


def shards(n_gx, n_gy, speed, before, now, src, prior, w_first, b_first, w_mid, b_mid, w_last):
    nx, ny, depth = now.shape
    out = jax.ShapeDtypeStruct(now.shape, F32)
    vmem = pl.BlockSpec(memory_space=pltpu.VMEM)
    hbm = pl.BlockSpec(memory_space=pltpu.HBM)
    groups = nx // 4
    r1, r2 = ny + 4, ny + 2
    ch = b_first.shape[0]
    slots, blk = 3 * ny + 32, 6
    count = n_gx * n_gy
    held = pltpu.VMEM(now.shape, F32)
    *outs, sums = pl.pallas_call(
        functools.partial(kernel, n_gx, n_gy),
        out_shape=(held,) * 4 + (pltpu.VMEM((8, 128), F32),),
        in_specs=[hbm] * 10,
        out_specs=(vmem,) * 5,
        scratch_shapes=[
            pltpu.VMEM(now.shape, F32),
            pltpu.VMEM(now.shape, F32),
            pltpu.VMEM(src.shape, F32),
            pltpu.VMEM(now.shape, F32),
            pltpu.VMEM((ch, 27), BF16),
            pltpu.VMEM((ch * ch, 27), BF16),
            pltpu.VMEM((ch, 27), BF16),
            pltpu.VMEM((1, ch), F32),
            pltpu.VMEM((1, ch), F32),
            pltpu.SemaphoreType.DMA((10,)),
            pltpu.VMEM(now.shape, F32),
            pltpu.VMEM((2, nx * ny, nx * ny + 8 * ny + 8 * nx), BF16),
            pltpu.VMEM((2, nx * ny + 8 * ny + 8 * nx, depth), BF16),
            pltpu.VMEM((2, 4, 3, ny, depth), BF16),
            pltpu.VMEM((2, groups, 3, 16, depth), BF16),
            pltpu.VMEM((2, 4, 3, ny, depth), BF16),
            pltpu.VMEM((2, groups, 3, 16, depth), BF16),
            pltpu.VMEM((2, 2, 16, depth), BF16),
            pltpu.VMEM((8, ny, depth), F32),
            pltpu.VMEM((nx, 8, depth), F32),
            pltpu.VMEM((2, depth, depth), BF16),
            pltpu.VMEM(now.shape, F32),
            pltpu.VMEM((nx + 6, slots, depth), BF16),
            pltpu.VMEM((2, groups, 16, depth), BF16),
            pltpu.VMEM((2, 3, ny, depth), BF16),
            pltpu.VMEM((2, groups + 2, 16, depth), BF16),
            pltpu.VMEM((nx + 4, r1 * ch, depth), BF16),
            pltpu.VMEM((nx + 2, r2 * ch, depth), BF16),
            pltpu.VMEM((r1 * ch, 3 * slots), BF16),
            pltpu.VMEM((64, 3 * slots), BF16),
            pltpu.VMEM((3 * blk * ch, 3 * (blk + 2) * ch), BF16),
            pltpu.VMEM((12 * ch, 18 * ch), BF16),
            pltpu.VMEM((3 * ny, 3 * r2 * ch), BF16),
            pltpu.VMEM((1, 128), F32),
            pltpu.VMEM((count - 1, 1, 128), F32),
            pltpu.SemaphoreType.DMA((16,)),
            pltpu.SemaphoreType.DMA((16,)),
            pltpu.SemaphoreType.DMA,
            pltpu.SemaphoreType.DMA,
        ],
        compiler_params=pltpu.CompilerParams(
            collective_id=0, has_side_effects=True, vmem_limit_bytes=40 * 1024 * 1024
        ),
    )(
        *(
            pltpu.with_memory_space_constraint(v, pltpu.HBM)
            for v in (
                speed,
                before,
                now,
                src,
                prior,
                w_first.transpose(1, 2, 0).reshape(ch, 27),
                w_mid.transpose(1, 2, 0).reshape(ch * ch, 27),
                w_last.transpose(2, 1, 0).reshape(ch, 27),
                b_first.reshape(1, ch),
                b_mid.reshape(1, ch),
            )
        )
    )
    return pl.pallas_call(
        functools.partial(hand_on, 8.0 * float(nx * n_gx * ny * n_gy * depth)),
        out_shape=(out,) * 4,
        in_specs=[vmem] * 5,
        out_specs=(hbm,) * 4,
        scratch_shapes=[pltpu.VMEM(now.shape, F32), pltpu.SemaphoreType.DMA((7,))],
    )(*(pltpu.with_memory_space_constraint(v, pltpu.VMEM) for v in (sums, *outs)))


def solution(mesh):
    brick = P("gx", "gy", None)
    return jax.shard_map(
        functools.partial(shards, mesh.shape["gx"], mesh.shape["gy"]),
        mesh=mesh,
        in_specs=(brick, brick, brick, P(None, "gx", "gy", None), brick, P(), P(), P(), P(), P()),
        out_specs=(brick,) * 4,
        check_vma=False,
    )
```

```python
import functools

import jax
import jax.numpy as jnp
from jax import lax
from jax.experimental import pallas as pl
from jax.experimental.pallas import tpu as pltpu
from jax.sharding import PartitionSpec as P

COEFS = (-205.0 / 72.0, 8.0 / 5.0, -1.0 / 5.0, 8.0 / 315.0, -1.0 / 560.0)
MESH = pl.DeviceIdType.MESH
F32 = jnp.float32
BF16 = jnp.bfloat16
UNROLL = True
WAVE_UNROLL = 4
FAR = 3


def shift_z(v, k):
    depth = v.shape[-1]
    lane = lax.broadcasted_iota(jnp.int32, v.shape, v.ndim - 1)
    rolled = pltpu.roll(v, (-k) % depth, v.ndim - 1)
    return jnp.where((lane + k >= 0) & (lane + k < depth), rolled, 0.0)


def iota(shape, dim):
    return lax.broadcasted_iota(jnp.int32, shape, dim)


def one_hot(hit):
    return jnp.where(hit, 1.0, 0.0).astype(BF16)


def third(index, size):
    return jnp.where(index >= size, 1, 0) + jnp.where(index >= 2 * size, 1, 0)


def kernel(
    n_gx,
    n_gy,
    speed_hbm,
    before_hbm,
    now_hbm,
    src_hbm,
    prior_hbm,
    first_hbm,
    mid_hbm,
    last_hbm,
    bias1_hbm,
    bias2_hbm,
    out_next,
    out_after,
    out_grad,
    out_dir,
    out_sums,
    speed,
    before,
    src,
    prior,
    raw1,
    raw2,
    raw3,
    bias1,
    bias2,
    load_sem,
    now,
    star,
    wave,
    pack_x,
    pack_y,
    recv_x,
    recv_y,
    recv_c,
    from_own_x,
    from_own_y,
    stencil,
    lap_z,
    grad,
    pack_g,
    recv_gx,
    recv_g,
    h1,
    h2,
    w1,
    w1_rim,
    w2,
    w2_short,
    w3,
    part,
    red,
    send_sem,
    recv_sem,
    red_send,
    red_recv,
):
    nx, ny, depth = now_hbm.shape
    gx, gy = lax.axis_index("gx"), lax.axis_index("gy")
    barrier = pltpu.get_barrier_semaphore()
    loads = [
        pltpu.make_async_copy(source, target, load_sem.at[i])
        for i, (source, target) in enumerate(
            (
                (now_hbm, now),
                (before_hbm, before),
                (speed_hbm, speed),
                (first_hbm, raw1),
                (mid_hbm, raw2),
                (last_hbm, raw3),
                (bias1_hbm, bias1),
                (bias2_hbm, bias2),
                (src_hbm, src),
                (prior_hbm, prior),
            )
        )
    ]
    for load in loads[:3]:
        load.start()

    def there(dx, dy):
        ok = None
        for pos, d, n in ((gx, dx, n_gx), (gy, dy, n_gy)):
            if d:
                one = (pos + d >= 0) & (pos + d < n)
                ok = one if ok is None else ok & one
        return ok

    count = n_gx * n_gy
    me = gx * n_gy + gy

    def peer(i):
        flat = lax.rem(me + i, count)
        return (lax.div(flat, n_gy), lax.rem(flat, n_gy))

    def greet(x, y):
        pl.semaphore_signal(barrier, inc=1, device_id=(x, y), device_id_type=MESH)

    def within(pos, n, d):
        return jnp.minimum(pos, d) + jnp.minimum(n - 1 - pos, d) + 1

    for dx, dy in ((0, 1), (0, -1), (1, 0), (-1, 0), (1, 1), (1, -1), (-1, 1), (-1, -1)):

        @pl.when(there(dx, dy))
        def _(dx=dx, dy=dy):
            greet(gx + dx, gy + dy)

    for load in loads[3:]:
        load.start()

    def far(pos, j):
        return (j - pos > FAR) | (pos - j > FAR)

    for j in range(n_gy):

        @pl.when(far(gy, j))
        def _(j=j):
            for i in range(n_gx):
                greet(i, j)

        if n_gx > FAR + 1:

            @pl.when(jnp.logical_not(far(gy, j)))
            def _(j=j):
                for i in range(n_gx):

                    @pl.when(far(gx, i))
                    def _(i=i):
                        greet(i, j)

    wanted = within(gx, n_gx, 1) * within(gy, n_gy, 1) - 1
    wanted = wanted + count - within(gx, n_gx, FAR) * within(gy, n_gy, FAR)

    class Copy:
        def __init__(self, ident, source, target, dx, dy):
            self.make = lambda: pltpu.make_async_remote_copy(
                src_ref=source,
                dst_ref=target,
                send_sem=send_sem.at[ident],
                recv_sem=recv_sem.at[ident],
                device_id=(gx + dx, gy + dy),
                device_id_type=MESH,
            )
            self.to = there(dx, dy)
            self.origin = there(-dx, -dy)
            self.target = target

        def start(self):
            @pl.when(self.to)
            def _():
                self.make().start()

        def clear(self):
            @pl.when(jnp.logical_not(self.origin))
            def _():
                self.target[...] = jnp.zeros(self.target.shape, self.target.dtype)

        def arrive(self):
            @pl.when(self.origin)
            def _():
                self.make().wait_recv()

        def sent(self):
            @pl.when(self.to)
            def _():
                self.make().wait_send()

    groups = nx // 4
    mid = pl.ds(1, groups)
    same_z = pl.ds(ny, ny)
    copies_w = (
        Copy(0, pack_y.at[1, groups - 1, 0], recv_c.at[0, 0], 1, 1),
        Copy(1, pack_y.at[1, 0, 0], recv_c.at[1, 0], -1, 1),
        Copy(2, pack_y.at[0, groups - 1, 0], recv_c.at[0, 1], 1, -1),
        Copy(3, pack_y.at[0, 0, 0], recv_c.at[1, 1], -1, -1),
        Copy(4, pack_y.at[1], recv_y.at[0], 0, 1),
        Copy(5, pack_y.at[0], recv_y.at[1], 0, -1),
        Copy(6, pack_x.at[1], recv_x.at[0], 1, 0),
        Copy(7, pack_x.at[0], recv_x.at[1], -1, 0),
    )
    copies_g = (
        Copy(12, pack_g.at[1, groups - 1], recv_g.at[0, 0], 1, 1),
        Copy(13, pack_g.at[1, 0], recv_g.at[0, groups + 1], -1, 1),
        Copy(14, pack_g.at[0, groups - 1], recv_g.at[1, 0], 1, -1),
        Copy(15, pack_g.at[0, 0], recv_g.at[1, groups + 1], -1, -1),
        Copy(10, pack_g.at[1], recv_g.at[0, mid], 0, 1),
        Copy(11, pack_g.at[0], recv_g.at[1, mid], 0, -1),
        Copy(8, grad.at[pl.ds(nx, 3), same_z, :], recv_gx.at[0], 1, 0),
        Copy(9, grad.at[pl.ds(3, 3), same_z, :], recv_gx.at[1], -1, 0),
    )

    row8 = iota((8, depth), 0)

    def half_turn(v):
        return pltpu.roll(v, 4, 0)

    def edge(v):
        return jnp.where(row8 < 4, v[0:8], v[ny - 8 : ny])

    def pack_four(e):
        low = [jnp.where(row8 < 4, e[i], half_turn(e[i + 1])) for i in (0, 2)]
        high = [jnp.where(row8 < 4, half_turn(e[i]), e[i + 1]) for i in (0, 2)]
        return [jnp.concatenate(v, axis=0).astype(BF16) for v in (low, high)]

    def unpack_four(low, high):
        sides = []
        for i in (0, 8):
            a, b = low.astype(F32)[i : i + 8], high.astype(F32)[i : i + 8]
            sides.append(jnp.where(row8 < 4, b, half_turn(a)))
            sides.append(jnp.where(row8 < 4, half_turn(b), a))
        return sides

    def across(v):
        total = jnp.zeros((8, depth), F32)
        for k in range(1, 5):
            down, up = pltpu.roll(v, k, 0), pltpu.roll(v, 8 - k, 0)
            total = total + COEFS[k] * jnp.where(row8 < k, down, jnp.where(row8 >= 8 - k, up, 0.0))
        return total

    def spread(e):
        parts = [jnp.where(row8 < 4, e, 0.0), jnp.where(row8 < 4, 0.0, e)]
        if ny > 16:
            parts.insert(1, jnp.zeros((ny - 16, depth), F32))
        return jnp.concatenate(parts, axis=0)

    gap = iota((depth, depth), 0) - iota((depth, depth), 1)
    taps = jnp.zeros((depth, depth), F32)
    for k in range(5):
        taps = jnp.where((gap == k) | (gap == -k), COEFS[k] * (1.0 if k else 3.0), taps)
    stencil[0] = taps.astype(BF16)
    stencil[1] = (taps - taps.astype(BF16).astype(F32)).astype(BF16)

    cells = nx * ny
    bits = ny.bit_length() - 1

    def split(v):
        high = v.astype(BF16)
        return high, (v - high.astype(F32)).astype(BF16)

    def fill_star(start, width, place):
        row, col = iota((cells, width), 0), iota((cells, width), 1)
        x_in, y_in = place(col)
        dx, dy = x_in - (row >> bits), y_in - (row & (ny - 1))
        far = jnp.where(dx == 0, jnp.abs(dy), jnp.where(dy == 0, jnp.abs(dx), 0))
        value = jnp.zeros((cells, width), F32)
        for k in range(1, 5):
            value = jnp.where(far == k, COEFS[k], value)
        at = slice(start, start + width)
        star[0, :, at], star[1, :, at] = split(value)

    def laplace(high, low, width):
        def times(x, y):
            return jnp.dot(x, y, preferred_element_type=F32)

        total = times(high[0:cells], stencil[0]) + times(high[0:cells], stencil[1])
        total = total + times(low[0:cells], stencil[0])
        total = total + times(star[0, :, 0:width], high[0:width]) + times(star[1, :, 0:width], high[0:width])
        total = total + times(star[0, :, 0:width], low[0:width])
        lap_z[...] = total.reshape(nx, ny, depth)

    fill_star(0, cells, lambda col: (col >> bits, col & (ny - 1)))
    for load in loads[:3]:
        load.wait()

    laplace(*split(now[...].reshape(cells, depth)), cells)
    for t in range(groups):
        edges = [[], [], []]
        for x in range(4 * t, 4 * t + 4):
            center = now[x]
            factor = speed[x]
            partial = 2.0 * center - before[x] + factor * lap_z[x]
            out_next[x] = partial
            for i, v in enumerate((center, partial, factor)):
                edges[i].append(edge(v))
                if x < 4:
                    pack_x[0, x, i] = v.astype(BF16)
                if x >= nx - 4:
                    pack_x[1, x - nx + 4, i] = v.astype(BF16)
        for i in range(3):
            pack_y[0, t, i], pack_y[1, t, i] = pack_four(edges[i])

    for group in (copies_w, copies_g):
        for c in group:
            c.clear()
    pl.semaphore_wait(barrier, wanted)
    for c in copies_w:
        c.start()

    for load in loads[3:8]:
        load.wait()

    r1, r2 = ny + 4, ny + 2
    m1, m2 = 8 * r1, 8 * r2
    slots = 3 * ny + 32
    blk = 6

    def column(bias):
        wide = jnp.broadcast_to(bias[...], (8, 8))
        return jnp.sum(jnp.where(iota((8, 8), 0) == iota((8, 8), 1), wide, 0.0), axis=1, keepdims=True)

    b1, b2 = column(bias1), column(bias2)

    def place_first(shape, dim):
        col = iota(shape, dim)
        a = third(col, slots)
        slot = col - slots * a
        side = slot - 3 * ny
        q = side & 7
        e = jnp.where(slot < 3 * ny, third(slot, ny), side >> 3)
        y = jnp.where(slot < 3 * ny, slot - ny * e, jnp.where(q < 4, q + ny, q - 8))
        y = jnp.where(side >= 24, 999, y)
        return a, e, y, col

    a_in, e_in, _, _ = place_first((27, 3 * slots), 0 + 1)
    taps = [
        jnp.dot(
            raw1[...],
            one_hot(iota((27, 3 * slots), 0) == 9 * a_in + 3 * b + e_in),
            preferred_element_type=F32,
        )
        for b in range(3)
    ]
    _, _, y_in, col = place_first((8, 3 * slots), 1)
    top = b1.astype(BF16).astype(F32)
    rest = b1 - top
    middle = rest.astype(BF16).astype(F32)
    base = slots + 3 * ny + 24
    biases = jnp.where(col == base, top, jnp.where(col == base + 1, middle, jnp.where(col == base + 2, rest - middle, 0.0)))

    def rows_first(y):
        total = biases
        for b in range(3):
            total = jnp.where(y_in - y == b - 1, taps[b], total)
        return total

    for y in range(0, r1, 2):
        w1[8 * y : 8 * y + 16, :] = jnp.concatenate(
            [rows_first(y - 2), rows_first(y - 1)], axis=0
        ).astype(BF16)

    w1_rim[0:32] = w1[0:32]
    w1_rim[32:64] = w1[m1 - 32 : m1]

    def fill_mid(out, size):
        wide = 8 * (size + 2)
        same_c = (iota((64, 3 * wide), 0) >> 3) == (iota((64, 3 * wide), 1) & 7)
        a_in = third(iota((27, 3 * wide), 1), wide)
        col = iota((8, 3 * wide), 1)
        y_in = (col - wide * third(col, wide)) >> 3
        table = []
        for t in range(9):
            full = jnp.dot(
                raw2[...], one_hot(iota((27, 3 * wide), 0) == 9 * a_in + t), preferred_element_type=F32
            )
            full = jnp.where(same_c, full, 0.0)
            total = full[0:8]
            for c in range(1, 8):
                total = total + full[8 * c : 8 * c + 8]
            table.append(total)

        def rows_mid(i):
            e, y = i // size, i % size
            total = jnp.zeros((8, 3 * wide), F32)
            for b in range(3):
                total = jnp.where(y_in - y == b, table[3 * b + e], total)
            return total

        for i in range(0, 3 * size, 2):
            out[8 * i : 8 * i + 16, :] = jnp.concatenate(
                [rows_mid(i), rows_mid(i + 1)], axis=0
            ).astype(BF16)

    fill_mid(w2, blk)
    fill_mid(w2_short, 4)

    same_c = iota((8, 3 * m2), 0) == (iota((8, 3 * m2), 1) & 7)
    a_in = third(iota((27, 3 * m2), 1), m2)
    col = iota((ny, 3 * m2), 1)
    gap = ((col - m2 * third(col, m2)) >> 3) - iota((ny, 3 * m2), 0)
    for e in range(3):
        total = jnp.zeros((ny, 3 * m2), F32)
        for b in range(3):
            full = jnp.dot(
                raw3[...],
                one_hot(iota((27, 3 * m2), 0) == 9 * a_in + 3 * b + e),
                preferred_element_type=F32,
            )
            line = jnp.sum(jnp.where(same_c, full, 0.0), axis=0, keepdims=True)
            total = jnp.where(gap == b, jnp.broadcast_to(line, total.shape), total)
        w3[ny * e : ny * e + ny, :] = total.astype(BF16)

    outside = [x for x in range(-4, nx + 4) if x < 0 or x >= nx]

    def reach(x, inside):
        return [(k, x + d * k) for k in range(1, 5) for d in (-1, 1) if inside(x + d * k)]

    for i, x in enumerate(outside):
        total = jnp.zeros((ny, depth), F32)
        for k, at in reach(x, lambda v: 0 <= v < nx):
            total = total + COEFS[k] * now[at]
        from_own_x[i] = total
    for x in range(nx):
        from_own_y[x] = across(edge(now[x]))
    fill_star(
        cells,
        8 * ny,
        lambda col: ((col >> bits) + jnp.where((col >> bits) < 4, -4, nx - 4), col & (ny - 1)),
    )
    fill_star(
        cells + 8 * ny,
        8 * nx,
        lambda col: (col >> 3, (col & 7) + jnp.where((col & 7) < 4, ny, -8)),
    )
    ones = jnp.where(iota((8, depth), 0) < 3, 1.0, 0.0)
    vacant = jnp.concatenate([jnp.zeros((24, depth), F32), ones], axis=0).astype(BF16)
    for x in range(nx):
        grad[x + 3, 3 * ny : 3 * ny + 32, :] = vacant
    for load in loads[8:]:
        load.wait()

    for c in copies_w:
        c.arrive()
    def keep(start, value):
        at = slice(start, start + value.shape[0])
        wave[0, at], wave[1, at] = split(value)

    corner = {}
    for i, first in enumerate((-4, nx)):
        for j, v in enumerate(unpack_four(recv_c[i, 0], recv_c[i, 1])):
            corner[first + j] = v
    halo_x = {x: recv_x.at[i // 4, i % 4] for i, x in enumerate(outside)}
    for i, x in enumerate(outside):
        felt = from_own_x[i] + spread(across(corner[x]))
        keep(cells + ny * i, halo_x[x][1].astype(F32) + halo_x[x][2].astype(F32) * felt)
    for t in range(groups):
        sides = [unpack_four(recv_y[0, t, i], recv_y[1, t, i]) for i in range(3)]
        for j in range(4):
            x = 4 * t + j
            felt = from_own_y[x]
            for k, at in reach(x, lambda v: v in corner):
                felt = felt + COEFS[k] * corner[at]
            side = sides[1][j] + sides[2][j] * felt
            if x % 2:
                keep(cells + 8 * ny + 8 * (x - 1), jnp.concatenate([before_side, side], axis=0))
            before_side = side
            felt = spread(across(sides[0][j]))
            for k, at in reach(x, lambda v: v in corner):
                felt = felt + COEFS[k] * halo_x[at][0].astype(F32)
            value = out_next[x] + speed[x] * felt
            out_next[x] = value
            keep(ny * x, value)

    def store_own(plane, value):
        for e in range(3):
            rows = value if e == 1 else shift_z(value, e - 1)
            grad[plane, ny * e : ny * e + ny, :] = rows.astype(BF16)

    laplace(wave.at[0], wave.at[1], cells + 8 * ny + 8 * nx)

    def step_two(t):
        edges = []
        for x in range(4 * t, 4 * t + 4):
            center = out_next[x]
            value = 2.0 * center - now[x] + speed[x] * lap_z[x]
            out_after[x] = value
            gradient = prior[x] + src[0, x] * center + src[1, x] * value
            out_grad[x] = gradient
            grad[x + 3, ny : 2 * ny, :] = gradient.astype(BF16)
            edges.append(edge(gradient))
        pack_g[0, t], pack_g[1, t] = pack_four(edges)

    step_two(0)
    step_two(groups - 1)
    for c in copies_g[:4] + copies_g[6:]:
        c.start()
    for t in range(1, groups - 1):
        step_two(t)
    for c in copies_g[4:6]:
        c.start()
    for x in range(nx):
        for e in (0, 2):
            grad[x + 3, ny * e : ny * e + ny, :] = shift_z(out_grad[x], e - 1).astype(BF16)

    big = 3.0e38
    x_low = jnp.where(gx == 0, 0.0, big)
    x_high = jnp.where(gx == n_gx - 1, 0.0, big)
    y_low = jnp.where(gy == 0, 0.0, big)
    y_high = jnp.where(gy == n_gy - 1, 0.0, big)

    def limit(value, cap):
        return value if cap is None else jnp.minimum(value, cap)

    def conv_plane(weight, rhs, rows):
        res = jnp.dot(weight[...], rhs, preferred_element_type=F32)
        return (
            res[rows : 2 * rows] + shift_z(res[:rows], -1) + shift_z(res[2 * rows :], 1)
        )

    def layer_one(p, weight):
        return jnp.maximum(
            jnp.dot(weight, grad[p : p + 3].reshape(3 * slots, depth), preferred_element_type=F32), 0.0
        )

    def store_rim(p, low, high):
        h1[p, 0:16] = jnp.minimum(low[0:16], y_low).astype(BF16)
        h1[p, 16:32] = low[16:32].astype(BF16)
        h1[p, m1 - 32 : m1 - 16] = high[0:16].astype(BF16)
        h1[p, m1 - 16 : m1] = jnp.minimum(high[16:32], y_high).astype(BF16)

    def layer_two(p, y, size, weight, cap):
        rhs = h1[p : p + 3, 8 * y : 8 * y + 8 * size + 16, :].reshape(24 * size + 48, depth)
        full = jnp.concatenate([jnp.broadcast_to(b2, (8, depth))] * size, axis=0)
        res = limit(jnp.maximum(conv_plane(weight, rhs, 8 * size) + full, 0.0), cap)
        if y == 0:
            res = jnp.concatenate([jnp.minimum(res[0:8], y_low), res[8:]], axis=0)
        if y + size == r2:
            res = jnp.concatenate([res[: 8 * size - 8], jnp.minimum(res[8 * size - 8 :], y_high)], axis=0)
        h2[p, 8 * y : 8 * y + 8 * size] = res.astype(BF16)

    def fill_sides(t):
        for j, side in enumerate(unpack_four(recv_g[0, t], recv_g[1, t])):
            plane = 4 * t + j - 1
            if 0 <= plane < nx + 6:
                grad[plane, 3 * ny : 3 * ny + 32, :] = jnp.concatenate(
                    [shift_z(side, -1), side, shift_z(side, 1), ones], axis=0
                ).astype(BF16)

    core_one = range(3, nx + 1)
    core_two = range(3, nx - 1)
    for p in core_one:
        h1[p, 32 : m1 - 32] = layer_one(p, w1[32 : m1 - 32]).astype(BF16)
    for p in core_two:
        layer_two(p, 4, 6, w2, None)
        layer_two(p, 10, 4, w2_short, None)
    for c in copies_g[4:6]:
        c.arrive()
    for t in range(1, groups + 1):
        fill_sides(t)
    for p in core_one:
        res = layer_one(p, w1_rim[...])
        store_rim(p, res[0:32], res[32:64])
    for p in core_two:
        layer_two(p, 0, 4, w2_short, None)
        layer_two(p, 14, 4, w2_short, None)
    zero = jnp.zeros((ny, depth), F32)

    def layer_three(p, carry):
        gg, gd, dd = carry
        rhs = h2[p : p + 3].reshape(3 * m2, depth)
        g = out_grad[p]
        d = conv_plane(w3, rhs, ny) + g
        out_dir[p] = d
        return gg + g * g, gd + g * d, dd + d * d

    sums = (zero, zero, zero)
    core_three = range(3, nx - 3)
    for p in core_three:
        sums = layer_three(p, sums)
    for c in copies_g[:4] + copies_g[6:]:
        c.arrive()
    for t in (0, groups + 1):
        fill_sides(t)
    for i in range(3):
        store_own(i, recv_gx[0, i].astype(F32))
        store_own(nx + 3 + i, recv_gx[1, i].astype(F32))
    for p in range(nx + 4):
        if p not in core_one:
            cap = x_low if p < 2 else x_high if p >= nx + 2 else None
            res = limit(layer_one(p, w1[...]), cap)
            store_rim(p, res[0:32], res[m1 - 32 : m1])
            h1[p, 32 : m1 - 32] = res[32 : m1 - 32].astype(BF16)
    for p in range(nx + 2):
        if p not in core_two:
            cap = x_low if p < 1 else x_high if p >= nx + 1 else None
            for y in range(0, r2, blk):
                layer_two(p, y, blk, w2, cap)

    for p in range(nx):
        if p not in core_three:
            sums = layer_three(p, sums)
    row, lane = iota((8, 128), 0), iota((8, 128), 1)
    tile = jnp.zeros((8, 128), F32)
    for i, s in enumerate(sums):
        line = jnp.sum(s, axis=0, keepdims=True)
        folded = line[:, 0:128]
        for j in range(1, depth // 128):
            folded = folded + line[:, 128 * j : 128 * j + 128]
        tile = jnp.where(row == i, folded, tile)
    wide = jnp.broadcast_to(jnp.sum(tile, axis=1, keepdims=True), (8, 128))
    mine = jnp.sum(jnp.where(row == lane, wide, 0.0), axis=0, keepdims=True)
    part[...] = mine
    for i in range(1, count):
        pltpu.make_async_remote_copy(
            src_ref=part,
            dst_ref=red.at[i - 1],
            send_sem=red_send,
            recv_sem=red_recv,
            device_id=peer(i),
            device_id_type=MESH,
        ).start()
    for group in (copies_w, copies_g):
        for c in group:
            c.sent()
    every = pltpu.make_async_remote_copy(
        src_ref=red,
        dst_ref=red,
        send_sem=red_send,
        recv_sem=red_recv,
        device_id=peer(1),
        device_id_type=MESH,
    )
    every.wait_recv()
    terms = [mine] + [red[i] for i in range(count - 1)]
    while len(terms) > 1:
        pairs = [terms[i] + terms[i + 1] for i in range(0, len(terms) - 1, 2)]
        terms = pairs + terms[2 * len(pairs) :]
    total = terms[0]
    spread = jnp.where(row == lane, jnp.broadcast_to(total, (8, 128)), 0.0)
    out_sums[...] = jnp.broadcast_to(jnp.sum(spread, axis=1, keepdims=True), (8, 128))
    every.wait_send()


def hand_on(damping, sums, v_next, v_after, v_grad, v_dir, o_next, o_after, o_grad, o_step, scaled, sem):
    moves = [
        pltpu.make_async_copy(source, target, sem.at[i])
        for i, (source, target) in enumerate(((v_next, o_next), (v_after, o_after), (v_grad, o_grad)))
    ]
    for move in moves:
        move.start()
    scale = sums[1:2, 0:1] / (sums[0:1, 0:1] + sums[2:3, 0:1] + damping)
    nx = v_dir.shape[0]
    step = nx // 4
    for i in range(4):
        at = pl.ds(i * step, step)
        scaled[at] = scale.reshape(1, 1, 1) * v_dir[at]
        move = pltpu.make_async_copy(scaled.at[at], o_step.at[at], sem.at[3 + i])
        move.start()
        moves.append(move)
    for move in moves:
        move.wait()


def shards(n_gx, n_gy, speed, before, now, src, prior, w_first, b_first, w_mid, b_mid, w_last):
    nx, ny, depth = now.shape
    out = jax.ShapeDtypeStruct(now.shape, F32)
    vmem = pl.BlockSpec(memory_space=pltpu.VMEM)
    hbm = pl.BlockSpec(memory_space=pltpu.HBM)
    groups = nx // 4
    r1, r2 = ny + 4, ny + 2
    ch = b_first.shape[0]
    slots, blk = 3 * ny + 32, 6
    count = n_gx * n_gy
    held = pltpu.VMEM(now.shape, F32)
    *outs, sums = pl.pallas_call(
        functools.partial(kernel, n_gx, n_gy),
        out_shape=(held,) * 4 + (pltpu.VMEM((8, 128), F32),),
        in_specs=[hbm] * 10,
        out_specs=(vmem,) * 5,
        scratch_shapes=[
            pltpu.VMEM(now.shape, F32),
            pltpu.VMEM(now.shape, F32),
            pltpu.VMEM(src.shape, F32),
            pltpu.VMEM(now.shape, F32),
            pltpu.VMEM((ch, 27), BF16),
            pltpu.VMEM((ch * ch, 27), BF16),
            pltpu.VMEM((ch, 27), BF16),
            pltpu.VMEM((1, ch), F32),
            pltpu.VMEM((1, ch), F32),
            pltpu.SemaphoreType.DMA((10,)),
            pltpu.VMEM(now.shape, F32),
            pltpu.VMEM((2, nx * ny, nx * ny + 8 * ny + 8 * nx), BF16),
            pltpu.VMEM((2, nx * ny + 8 * ny + 8 * nx, depth), BF16),
            pltpu.VMEM((2, 4, 3, ny, depth), BF16),
            pltpu.VMEM((2, groups, 3, 16, depth), BF16),
            pltpu.VMEM((2, 4, 3, ny, depth), BF16),
            pltpu.VMEM((2, groups, 3, 16, depth), BF16),
            pltpu.VMEM((2, 2, 16, depth), BF16),
            pltpu.VMEM((8, ny, depth), F32),
            pltpu.VMEM((nx, 8, depth), F32),
            pltpu.VMEM((2, depth, depth), BF16),
            pltpu.VMEM(now.shape, F32),
            pltpu.VMEM((nx + 6, slots, depth), BF16),
            pltpu.VMEM((2, groups, 16, depth), BF16),
            pltpu.VMEM((2, 3, ny, depth), BF16),
            pltpu.VMEM((2, groups + 2, 16, depth), BF16),
            pltpu.VMEM((nx + 4, r1 * ch, depth), BF16),
            pltpu.VMEM((nx + 2, r2 * ch, depth), BF16),
            pltpu.VMEM((r1 * ch, 3 * slots), BF16),
            pltpu.VMEM((64, 3 * slots), BF16),
            pltpu.VMEM((3 * blk * ch, 3 * (blk + 2) * ch), BF16),
            pltpu.VMEM((12 * ch, 18 * ch), BF16),
            pltpu.VMEM((3 * ny, 3 * r2 * ch), BF16),
            pltpu.VMEM((1, 128), F32),
            pltpu.VMEM((count - 1, 1, 128), F32),
            pltpu.SemaphoreType.DMA((16,)),
            pltpu.SemaphoreType.DMA((16,)),
            pltpu.SemaphoreType.DMA,
            pltpu.SemaphoreType.DMA,
        ],
        compiler_params=pltpu.CompilerParams(
            collective_id=0, has_side_effects=True, vmem_limit_bytes=40 * 1024 * 1024
        ),
    )(
        *(
            pltpu.with_memory_space_constraint(v, pltpu.HBM)
            for v in (
                speed,
                before,
                now,
                src,
                prior,
                w_first.transpose(1, 2, 0).reshape(ch, 27),
                w_mid.transpose(1, 2, 0).reshape(ch * ch, 27),
                w_last.transpose(2, 1, 0).reshape(ch, 27),
                b_first.reshape(1, ch),
                b_mid.reshape(1, ch),
            )
        )
    )
    return pl.pallas_call(
        functools.partial(hand_on, 8.0 * float(nx * n_gx * ny * n_gy * depth)),
        out_shape=(out,) * 4,
        in_specs=[vmem] * 5,
        out_specs=(hbm,) * 4,
        scratch_shapes=[pltpu.VMEM(now.shape, F32), pltpu.SemaphoreType.DMA((7,))],
    )(*(pltpu.with_memory_space_constraint(v, pltpu.VMEM) for v in (sums, *outs)))


def solution(mesh):
    brick = P("gx", "gy", None)
    return jax.shard_map(
        functools.partial(shards, mesh.shape["gx"], mesh.shape["gy"]),
        mesh=mesh,
        in_specs=(brick, brick, brick, P(None, "gx", "gy", None), brick, P(), P(), P(), P(), P()),
        out_specs=(brick,) * 4,
        check_vma=False,
    )
```

```python
import functools

import jax
import jax.numpy as jnp
from jax import lax
from jax.experimental import pallas as pl
from jax.experimental.pallas import tpu as pltpu
from jax.sharding import PartitionSpec as P

COEFS = (-205.0 / 72.0, 8.0 / 5.0, -1.0 / 5.0, 8.0 / 315.0, -1.0 / 560.0)
MESH = pl.DeviceIdType.MESH
F32 = jnp.float32
BF16 = jnp.bfloat16
UNROLL = True
WAVE_UNROLL = 4
FAR = 3


def shift_z(v, k):
    depth = v.shape[-1]
    lane = lax.broadcasted_iota(jnp.int32, v.shape, v.ndim - 1)
    rolled = pltpu.roll(v, (-k) % depth, v.ndim - 1)
    return jnp.where((lane + k >= 0) & (lane + k < depth), rolled, 0.0)


def iota(shape, dim):
    return lax.broadcasted_iota(jnp.int32, shape, dim)


def one_hot(hit):
    return jnp.where(hit, 1.0, 0.0).astype(BF16)


def third(index, size):
    return jnp.where(index >= size, 1, 0) + jnp.where(index >= 2 * size, 1, 0)


def kernel(
    n_gx,
    n_gy,
    speed_hbm,
    before_hbm,
    now_hbm,
    src_hbm,
    prior_hbm,
    first_hbm,
    mid_hbm,
    last_hbm,
    bias1_hbm,
    bias2_hbm,
    out_next,
    out_after,
    out_grad,
    out_dir,
    out_sums,
    speed,
    before,
    src,
    prior,
    raw1,
    raw2,
    raw3,
    bias1,
    bias2,
    load_sem,
    now,
    star,
    wave,
    pack_x,
    pack_y,
    recv_x,
    recv_y,
    recv_c,
    from_own_x,
    from_own_y,
    stencil,
    lap_z,
    grad,
    pack_g,
    recv_gx,
    recv_g,
    h1,
    h2,
    w1,
    w1_rim,
    w2,
    w2_short,
    w3,
    part,
    red,
    send_sem,
    recv_sem,
    red_send,
    red_recv,
):
    nx, ny, depth = now_hbm.shape
    gx, gy = lax.axis_index("gx"), lax.axis_index("gy")
    barrier = pltpu.get_barrier_semaphore()
    loads = [
        pltpu.make_async_copy(source, target, load_sem.at[i])
        for i, (source, target) in enumerate(
            (
                (now_hbm, now),
                (before_hbm, before),
                (speed_hbm, speed),
                (first_hbm, raw1),
                (mid_hbm, raw2),
                (last_hbm, raw3),
                (bias1_hbm, bias1),
                (bias2_hbm, bias2),
                (src_hbm, src),
                (prior_hbm, prior),
            )
        )
    ]
    for load in loads[:3]:
        load.start()

    def there(dx, dy):
        ok = None
        for pos, d, n in ((gx, dx, n_gx), (gy, dy, n_gy)):
            if d:
                one = (pos + d >= 0) & (pos + d < n)
                ok = one if ok is None else ok & one
        return ok

    count = n_gx * n_gy
    me = gx * n_gy + gy

    def peer(i):
        flat = lax.rem(me + i, count)
        return (lax.div(flat, n_gy), lax.rem(flat, n_gy))

    def greet(x, y):
        pl.semaphore_signal(barrier, inc=1, device_id=(x, y), device_id_type=MESH)

    def within(pos, n, d):
        return jnp.minimum(pos, d) + jnp.minimum(n - 1 - pos, d) + 1

    for dx, dy in ((0, 1), (0, -1), (1, 0), (-1, 0), (1, 1), (1, -1), (-1, 1), (-1, -1)):

        @pl.when(there(dx, dy))
        def _(dx=dx, dy=dy):
            greet(gx + dx, gy + dy)

    for load in loads[3:]:
        load.start()

    def far(pos, j):
        return (j - pos > FAR) | (pos - j > FAR)

    for j in range(n_gy):

        @pl.when(far(gy, j))
        def _(j=j):
            for i in range(n_gx):
                greet(i, j)

        if n_gx > FAR + 1:

            @pl.when(jnp.logical_not(far(gy, j)))
            def _(j=j):
                for i in range(n_gx):

                    @pl.when(far(gx, i))
                    def _(i=i):
                        greet(i, j)

    wanted = within(gx, n_gx, 1) * within(gy, n_gy, 1) - 1
    wanted = wanted + count - within(gx, n_gx, FAR) * within(gy, n_gy, FAR)

    class Copy:
        def __init__(self, ident, source, target, dx, dy):
            self.make = lambda: pltpu.make_async_remote_copy(
                src_ref=source,
                dst_ref=target,
                send_sem=send_sem.at[ident],
                recv_sem=recv_sem.at[ident],
                device_id=(gx + dx, gy + dy),
                device_id_type=MESH,
            )
            self.to = there(dx, dy)
            self.origin = there(-dx, -dy)
            self.target = target

        def start(self):
            @pl.when(self.to)
            def _():
                self.make().start()

        def clear(self):
            @pl.when(jnp.logical_not(self.origin))
            def _():
                self.target[...] = jnp.zeros(self.target.shape, self.target.dtype)

        def arrive(self):
            @pl.when(self.origin)
            def _():
                self.make().wait_recv()

        def sent(self):
            @pl.when(self.to)
            def _():
                self.make().wait_send()

    groups = nx // 4
    mid = pl.ds(1, groups)
    same_z = pl.ds(ny, ny)
    copies_w = (
        Copy(0, pack_y.at[1, groups - 1, 0], recv_c.at[0, 0], 1, 1),
        Copy(1, pack_y.at[1, 0, 0], recv_c.at[1, 0], -1, 1),
        Copy(2, pack_y.at[0, groups - 1, 0], recv_c.at[0, 1], 1, -1),
        Copy(3, pack_y.at[0, 0, 0], recv_c.at[1, 1], -1, -1),
        Copy(4, pack_y.at[1], recv_y.at[0], 0, 1),
        Copy(5, pack_y.at[0], recv_y.at[1], 0, -1),
        Copy(6, pack_x.at[1], recv_x.at[0], 1, 0),
        Copy(7, pack_x.at[0], recv_x.at[1], -1, 0),
    )
    copies_g = (
        Copy(12, pack_g.at[1, groups - 1], recv_g.at[0, 0], 1, 1),
        Copy(13, pack_g.at[1, 0], recv_g.at[0, groups + 1], -1, 1),
        Copy(14, pack_g.at[0, groups - 1], recv_g.at[1, 0], 1, -1),
        Copy(15, pack_g.at[0, 0], recv_g.at[1, groups + 1], -1, -1),
        Copy(10, pack_g.at[1], recv_g.at[0, mid], 0, 1),
        Copy(11, pack_g.at[0], recv_g.at[1, mid], 0, -1),
        Copy(8, grad.at[pl.ds(nx, 3), same_z, :], recv_gx.at[0], 1, 0),
        Copy(9, grad.at[pl.ds(3, 3), same_z, :], recv_gx.at[1], -1, 0),
    )

    row8 = iota((8, depth), 0)

    def half_turn(v):
        return pltpu.roll(v, 4, 0)

    def edge(v):
        return jnp.where(row8 < 4, v[0:8], v[ny - 8 : ny])

    def pack_four(e):
        low = [jnp.where(row8 < 4, e[i], half_turn(e[i + 1])) for i in (0, 2)]
        high = [jnp.where(row8 < 4, half_turn(e[i]), e[i + 1]) for i in (0, 2)]
        return [jnp.concatenate(v, axis=0).astype(BF16) for v in (low, high)]

    def unpack_four(low, high):
        sides = []
        for i in (0, 8):
            a, b = low.astype(F32)[i : i + 8], high.astype(F32)[i : i + 8]
            sides.append(jnp.where(row8 < 4, b, half_turn(a)))
            sides.append(jnp.where(row8 < 4, half_turn(b), a))
        return sides

    def across(v):
        total = jnp.zeros((8, depth), F32)
        for k in range(1, 5):
            down, up = pltpu.roll(v, k, 0), pltpu.roll(v, 8 - k, 0)
            total = total + COEFS[k] * jnp.where(row8 < k, down, jnp.where(row8 >= 8 - k, up, 0.0))
        return total

    def spread(e):
        parts = [jnp.where(row8 < 4, e, 0.0), jnp.where(row8 < 4, 0.0, e)]
        if ny > 16:
            parts.insert(1, jnp.zeros((ny - 16, depth), F32))
        return jnp.concatenate(parts, axis=0)

    gap = iota((depth, depth), 0) - iota((depth, depth), 1)
    taps = jnp.zeros((depth, depth), F32)
    for k in range(5):
        taps = jnp.where((gap == k) | (gap == -k), COEFS[k] * (1.0 if k else 3.0), taps)
    stencil[0] = taps.astype(BF16)
    stencil[1] = (taps - taps.astype(BF16).astype(F32)).astype(BF16)

    cells = nx * ny
    bits = ny.bit_length() - 1

    def split(v):
        high = v.astype(BF16)
        return high, (v - high.astype(F32)).astype(BF16)

    def fill_star(start, width, place):
        row, col = iota((cells, width), 0), iota((cells, width), 1)
        x_in, y_in = place(col)
        dx, dy = x_in - (row >> bits), y_in - (row & (ny - 1))
        far = jnp.where(dx == 0, jnp.abs(dy), jnp.where(dy == 0, jnp.abs(dx), 0))
        value = jnp.zeros((cells, width), F32)
        for k in range(1, 5):
            value = jnp.where(far == k, COEFS[k], value)
        at = slice(start, start + width)
        star[0, :, at], star[1, :, at] = split(value)

    def laplace(high, low, width):
        def times(x, y):
            return jnp.dot(x, y, preferred_element_type=F32)

        total = times(high[0:cells], stencil[0]) + times(high[0:cells], stencil[1])
        total = total + times(low[0:cells], stencil[0])
        total = total + times(star[0, :, 0:width], high[0:width]) + times(star[1, :, 0:width], high[0:width])
        total = total + times(star[0, :, 0:width], low[0:width])
        lap_z[...] = total.reshape(nx, ny, depth)

    fill_star(0, cells, lambda col: (col >> bits, col & (ny - 1)))
    for load in loads[:3]:
        load.wait()

    laplace(*split(now[...].reshape(cells, depth)), cells)
    for t in range(groups):
        edges = [[], [], []]
        for x in range(4 * t, 4 * t + 4):
            center = now[x]
            factor = speed[x]
            partial = 2.0 * center - before[x] + factor * lap_z[x]
            out_next[x] = partial
            for i, v in enumerate((center, partial, factor)):
                edges[i].append(edge(v))
                if x < 4:
                    pack_x[0, x, i] = v.astype(BF16)
                if x >= nx - 4:
                    pack_x[1, x - nx + 4, i] = v.astype(BF16)
        for i in range(3):
            pack_y[0, t, i], pack_y[1, t, i] = pack_four(edges[i])

    for group in (copies_w, copies_g):
        for c in group:
            c.clear()
    pl.semaphore_wait(barrier, wanted)
    for c in copies_w:
        c.start()

    for load in loads[3:8]:
        load.wait()

    r1, r2 = ny + 4, ny + 2
    m1, m2 = 8 * r1, 8 * r2
    slots = 3 * ny + 32
    blk = 6

    def column(bias):
        wide = jnp.broadcast_to(bias[...], (8, 8))
        return jnp.sum(jnp.where(iota((8, 8), 0) == iota((8, 8), 1), wide, 0.0), axis=1, keepdims=True)

    b1, b2 = column(bias1), column(bias2)

    def place_first(shape, dim):
        col = iota(shape, dim)
        a = third(col, slots)
        slot = col - slots * a
        side = slot - 3 * ny
        q = side & 7
        e = jnp.where(slot < 3 * ny, third(slot, ny), side >> 3)
        y = jnp.where(slot < 3 * ny, slot - ny * e, jnp.where(q < 4, q + ny, q - 8))
        y = jnp.where(side >= 24, 999, y)
        return a, e, y, col

    a_in, e_in, _, _ = place_first((27, 3 * slots), 0 + 1)
    taps = [
        jnp.dot(
            raw1[...],
            one_hot(iota((27, 3 * slots), 0) == 9 * a_in + 3 * b + e_in),
            preferred_element_type=F32,
        )
        for b in range(3)
    ]
    _, _, y_in, col = place_first((8, 3 * slots), 1)
    top = b1.astype(BF16).astype(F32)
    rest = b1 - top
    middle = rest.astype(BF16).astype(F32)
    base = slots + 3 * ny + 24
    biases = jnp.where(col == base, top, jnp.where(col == base + 1, middle, jnp.where(col == base + 2, rest - middle, 0.0)))

    def rows_first(y):
        total = biases
        for b in range(3):
            total = jnp.where(y_in - y == b - 1, taps[b], total)
        return total

    for y in range(0, r1, 2):
        w1[8 * y : 8 * y + 16, :] = jnp.concatenate(
            [rows_first(y - 2), rows_first(y - 1)], axis=0
        ).astype(BF16)

    w1_rim[0:32] = w1[0:32]
    w1_rim[32:64] = w1[m1 - 32 : m1]

    def fill_mid(out, size):
        wide = 8 * (size + 2)
        same_c = (iota((64, 3 * wide), 0) >> 3) == (iota((64, 3 * wide), 1) & 7)
        a_in = third(iota((27, 3 * wide), 1), wide)
        col = iota((8, 3 * wide), 1)
        y_in = (col - wide * third(col, wide)) >> 3
        table = []
        for t in range(9):
            full = jnp.dot(
                raw2[...], one_hot(iota((27, 3 * wide), 0) == 9 * a_in + t), preferred_element_type=F32
            )
            full = jnp.where(same_c, full, 0.0)
            total = full[0:8]
            for c in range(1, 8):
                total = total + full[8 * c : 8 * c + 8]
            table.append(total)

        def rows_mid(i):
            e, y = i // size, i % size
            total = jnp.zeros((8, 3 * wide), F32)
            for b in range(3):
                total = jnp.where(y_in - y == b, table[3 * b + e], total)
            return total

        for i in range(0, 3 * size, 2):
            out[8 * i : 8 * i + 16, :] = jnp.concatenate(
                [rows_mid(i), rows_mid(i + 1)], axis=0
            ).astype(BF16)

    fill_mid(w2, blk)
    fill_mid(w2_short, 4)

    same_c = iota((8, 3 * m2), 0) == (iota((8, 3 * m2), 1) & 7)
    a_in = third(iota((27, 3 * m2), 1), m2)
    col = iota((ny, 3 * m2), 1)
    gap = ((col - m2 * third(col, m2)) >> 3) - iota((ny, 3 * m2), 0)
    for e in range(3):
        total = jnp.zeros((ny, 3 * m2), F32)
        for b in range(3):
            full = jnp.dot(
                raw3[...],
                one_hot(iota((27, 3 * m2), 0) == 9 * a_in + 3 * b + e),
                preferred_element_type=F32,
            )
            line = jnp.sum(jnp.where(same_c, full, 0.0), axis=0, keepdims=True)
            total = jnp.where(gap == b, jnp.broadcast_to(line, total.shape), total)
        w3[ny * e : ny * e + ny, :] = total.astype(BF16)

    outside = [x for x in range(-4, nx + 4) if x < 0 or x >= nx]

    def reach(x, inside):
        return [(k, x + d * k) for k in range(1, 5) for d in (-1, 1) if inside(x + d * k)]

    for i, x in enumerate(outside):
        total = jnp.zeros((ny, depth), F32)
        for k, at in reach(x, lambda v: 0 <= v < nx):
            total = total + COEFS[k] * now[at]
        from_own_x[i] = total
    for x in range(nx):
        from_own_y[x] = across(edge(now[x]))
    fill_star(
        cells,
        8 * ny,
        lambda col: ((col >> bits) + jnp.where((col >> bits) < 4, -4, nx - 4), col & (ny - 1)),
    )
    fill_star(
        cells + 8 * ny,
        8 * nx,
        lambda col: (col >> 3, (col & 7) + jnp.where((col & 7) < 4, ny, -8)),
    )
    ones = jnp.where(iota((8, depth), 0) < 3, 1.0, 0.0)
    vacant = jnp.concatenate([jnp.zeros((24, depth), F32), ones], axis=0).astype(BF16)
    for x in range(nx):
        grad[x + 3, 3 * ny : 3 * ny + 32, :] = vacant
    for load in loads[8:]:
        load.wait()

    for c in copies_w:
        c.arrive()
    def keep(start, value):
        at = slice(start, start + value.shape[0])
        wave[0, at], wave[1, at] = split(value)

    corner = {}
    for i, first in enumerate((-4, nx)):
        for j, v in enumerate(unpack_four(recv_c[i, 0], recv_c[i, 1])):
            corner[first + j] = v
    halo_x = {x: recv_x.at[i // 4, i % 4] for i, x in enumerate(outside)}
    for i, x in enumerate(outside):
        felt = from_own_x[i] + spread(across(corner[x]))
        keep(cells + ny * i, halo_x[x][1].astype(F32) + halo_x[x][2].astype(F32) * felt)
    for t in range(groups):
        sides = [unpack_four(recv_y[0, t, i], recv_y[1, t, i]) for i in range(3)]
        for j in range(4):
            x = 4 * t + j
            felt = from_own_y[x]
            for k, at in reach(x, lambda v: v in corner):
                felt = felt + COEFS[k] * corner[at]
            side = sides[1][j] + sides[2][j] * felt
            if x % 2:
                keep(cells + 8 * ny + 8 * (x - 1), jnp.concatenate([before_side, side], axis=0))
            before_side = side
            felt = spread(across(sides[0][j]))
            for k, at in reach(x, lambda v: v in corner):
                felt = felt + COEFS[k] * halo_x[at][0].astype(F32)
            value = out_next[x] + speed[x] * felt
            out_next[x] = value
            keep(ny * x, value)

    def store_own(plane, value):
        for e in range(3):
            rows = value if e == 1 else shift_z(value, e - 1)
            grad[plane, ny * e : ny * e + ny, :] = rows.astype(BF16)

    laplace(wave.at[0], wave.at[1], cells + 8 * ny + 8 * nx)

    def step_two(t):
        edges = []
        for x in range(4 * t, 4 * t + 4):
            center = out_next[x]
            value = 2.0 * center - now[x] + speed[x] * lap_z[x]
            out_after[x] = value
            gradient = prior[x] + src[0, x] * center + src[1, x] * value
            out_grad[x] = gradient
            grad[x + 3, ny : 2 * ny, :] = gradient.astype(BF16)
            edges.append(edge(gradient))
        pack_g[0, t], pack_g[1, t] = pack_four(edges)

    step_two(0)
    step_two(groups - 1)
    for c in copies_g[:4] + copies_g[6:]:
        c.start()
    for t in range(1, groups - 1):
        step_two(t)
    for c in copies_g[4:6]:
        c.start()
    for x in range(nx):
        for e in (0, 2):
            grad[x + 3, ny * e : ny * e + ny, :] = shift_z(out_grad[x], e - 1).astype(BF16)

    big = 3.0e38
    x_low = jnp.where(gx == 0, 0.0, big)
    x_high = jnp.where(gx == n_gx - 1, 0.0, big)
    y_low = jnp.where(gy == 0, 0.0, big)
    y_high = jnp.where(gy == n_gy - 1, 0.0, big)

    def limit(value, cap):
        return value if cap is None else jnp.minimum(value, cap)

    def conv_plane(weight, rhs, rows):
        res = jnp.dot(weight[...], rhs, preferred_element_type=F32)
        return (
            res[rows : 2 * rows] + shift_z(res[:rows], -1) + shift_z(res[2 * rows :], 1)
        )

    def layer_one(p, weight):
        return jnp.maximum(
            jnp.dot(weight, grad[p : p + 3].reshape(3 * slots, depth), preferred_element_type=F32), 0.0
        )

    def store_rim(p, low, high):
        h1[p, 0:16] = jnp.minimum(low[0:16], y_low).astype(BF16)
        h1[p, 16:32] = low[16:32].astype(BF16)
        h1[p, m1 - 32 : m1 - 16] = high[0:16].astype(BF16)
        h1[p, m1 - 16 : m1] = jnp.minimum(high[16:32], y_high).astype(BF16)

    def layer_two(p, y, size, weight, cap):
        rhs = h1[p : p + 3, 8 * y : 8 * y + 8 * size + 16, :].reshape(24 * size + 48, depth)
        full = jnp.concatenate([jnp.broadcast_to(b2, (8, depth))] * size, axis=0)
        res = limit(jnp.maximum(conv_plane(weight, rhs, 8 * size) + full, 0.0), cap)
        if y == 0:
            res = jnp.concatenate([jnp.minimum(res[0:8], y_low), res[8:]], axis=0)
        if y + size == r2:
            res = jnp.concatenate([res[: 8 * size - 8], jnp.minimum(res[8 * size - 8 :], y_high)], axis=0)
        h2[p, 8 * y : 8 * y + 8 * size] = res.astype(BF16)

    def fill_sides(t):
        for j, side in enumerate(unpack_four(recv_g[0, t], recv_g[1, t])):
            plane = 4 * t + j - 1
            if 0 <= plane < nx + 6:
                grad[plane, 3 * ny : 3 * ny + 32, :] = jnp.concatenate(
                    [shift_z(side, -1), side, shift_z(side, 1), ones], axis=0
                ).astype(BF16)

    core_one = range(3, nx + 1)
    core_two = range(3, nx - 1)
    for p in core_one:
        h1[p, 32 : m1 - 32] = layer_one(p, w1[32 : m1 - 32]).astype(BF16)
    for p in core_two:
        layer_two(p, 4, 6, w2, None)
        layer_two(p, 10, 4, w2_short, None)
    for c in copies_g[4:6]:
        c.arrive()
    for t in range(1, groups + 1):
        fill_sides(t)
    for p in core_one:
        res = layer_one(p, w1_rim[...])
        store_rim(p, res[0:32], res[32:64])
    for p in core_two:
        layer_two(p, 0, 4, w2_short, None)
        layer_two(p, 14, 4, w2_short, None)
    zero = jnp.zeros((ny, depth), F32)

    def layer_three(p, carry):
        gg, gd, dd = carry
        rhs = h2[p : p + 3].reshape(3 * m2, depth)
        g = out_grad[p]
        d = conv_plane(w3, rhs, ny) + g
        out_dir[p] = d
        return gg + g * g, gd + g * d, dd + d * d

    sums = (zero, zero, zero)
    core_three = range(3, nx - 3)
    for p in core_three:
        sums = layer_three(p, sums)
    for c in copies_g[:4] + copies_g[6:]:
        c.arrive()
    for t in (0, groups + 1):
        fill_sides(t)
    for i in range(3):
        store_own(i, recv_gx[0, i].astype(F32))
        store_own(nx + 3 + i, recv_gx[1, i].astype(F32))
    def rim_one(p):
        cap = x_low if p < 2 else x_high if p >= nx + 2 else None
        res = limit(layer_one(p, w1[...]), cap)
        store_rim(p, res[0:32], res[m1 - 32 : m1])
        h1[p, 32 : m1 - 32] = res[32 : m1 - 32].astype(BF16)

    def rim_two(p):
        cap = x_low if p < 1 else x_high if p >= nx + 1 else None
        for y in range(0, r2, blk):
            layer_two(p, y, blk, w2, cap)

    last = nx + 3
    for p in (2, last - 2):
        rim_one(p)
    for p, q in ((2, 1), (nx - 1, last - 1)):
        rim_two(p)
        rim_one(q)
    for p, q in ((1, 0), (nx, last)):
        rim_two(p)
        rim_one(q)
    for p, q in ((2, 0), (nx - 3, nx + 1)):
        sums = layer_three(p, sums)
        rim_two(q)
    for p in (1, nx - 2, 0, nx - 1):
        sums = layer_three(p, sums)
    row, lane = iota((8, 128), 0), iota((8, 128), 1)
    tile = jnp.zeros((8, 128), F32)
    for i, s in enumerate(sums):
        line = jnp.sum(s, axis=0, keepdims=True)
        folded = line[:, 0:128]
        for j in range(1, depth // 128):
            folded = folded + line[:, 128 * j : 128 * j + 128]
        tile = jnp.where(row == i, folded, tile)
    wide = jnp.broadcast_to(jnp.sum(tile, axis=1, keepdims=True), (8, 128))
    mine = jnp.sum(jnp.where(row == lane, wide, 0.0), axis=0, keepdims=True)
    part[...] = mine
    for i in range(1, count):
        pltpu.make_async_remote_copy(
            src_ref=part,
            dst_ref=red.at[i - 1],
            send_sem=red_send,
            recv_sem=red_recv,
            device_id=peer(i),
            device_id_type=MESH,
        ).start()
    for group in (copies_w, copies_g):
        for c in group:
            c.sent()
    every = pltpu.make_async_remote_copy(
        src_ref=red,
        dst_ref=red,
        send_sem=red_send,
        recv_sem=red_recv,
        device_id=peer(1),
        device_id_type=MESH,
    )
    every.wait_recv()
    terms = [mine] + [red[i] for i in range(count - 1)]
    while len(terms) > 1:
        pairs = [terms[i] + terms[i + 1] for i in range(0, len(terms) - 1, 2)]
        terms = pairs + terms[2 * len(pairs) :]
    total = terms[0]
    spread = jnp.where(row == lane, jnp.broadcast_to(total, (8, 128)), 0.0)
    out_sums[...] = jnp.broadcast_to(jnp.sum(spread, axis=1, keepdims=True), (8, 128))
    every.wait_send()


def hand_on(damping, sums, v_next, v_after, v_grad, v_dir, o_next, o_after, o_grad, o_step, scaled, sem):
    moves = [
        pltpu.make_async_copy(source, target, sem.at[i])
        for i, (source, target) in enumerate(((v_next, o_next), (v_after, o_after), (v_grad, o_grad)))
    ]
    for move in moves:
        move.start()
    scale = sums[1:2, 0:1] / (sums[0:1, 0:1] + sums[2:3, 0:1] + damping)
    nx = v_dir.shape[0]
    step = nx // 4
    for i in range(4):
        at = pl.ds(i * step, step)
        scaled[at] = scale.reshape(1, 1, 1) * v_dir[at]
        move = pltpu.make_async_copy(scaled.at[at], o_step.at[at], sem.at[3 + i])
        move.start()
        moves.append(move)
    for move in moves:
        move.wait()


def shards(n_gx, n_gy, speed, before, now, src, prior, w_first, b_first, w_mid, b_mid, w_last):
    nx, ny, depth = now.shape
    out = jax.ShapeDtypeStruct(now.shape, F32)
    vmem = pl.BlockSpec(memory_space=pltpu.VMEM)
    hbm = pl.BlockSpec(memory_space=pltpu.HBM)
    groups = nx // 4
    r1, r2 = ny + 4, ny + 2
    ch = b_first.shape[0]
    slots, blk = 3 * ny + 32, 6
    count = n_gx * n_gy
    held = pltpu.VMEM(now.shape, F32)
    *outs, sums = pl.pallas_call(
        functools.partial(kernel, n_gx, n_gy),
        out_shape=(held,) * 4 + (pltpu.VMEM((8, 128), F32),),
        in_specs=[hbm] * 10,
        out_specs=(vmem,) * 5,
        scratch_shapes=[
            pltpu.VMEM(now.shape, F32),
            pltpu.VMEM(now.shape, F32),
            pltpu.VMEM(src.shape, F32),
            pltpu.VMEM(now.shape, F32),
            pltpu.VMEM((ch, 27), BF16),
            pltpu.VMEM((ch * ch, 27), BF16),
            pltpu.VMEM((ch, 27), BF16),
            pltpu.VMEM((1, ch), F32),
            pltpu.VMEM((1, ch), F32),
            pltpu.SemaphoreType.DMA((10,)),
            pltpu.VMEM(now.shape, F32),
            pltpu.VMEM((2, nx * ny, nx * ny + 8 * ny + 8 * nx), BF16),
            pltpu.VMEM((2, nx * ny + 8 * ny + 8 * nx, depth), BF16),
            pltpu.VMEM((2, 4, 3, ny, depth), BF16),
            pltpu.VMEM((2, groups, 3, 16, depth), BF16),
            pltpu.VMEM((2, 4, 3, ny, depth), BF16),
            pltpu.VMEM((2, groups, 3, 16, depth), BF16),
            pltpu.VMEM((2, 2, 16, depth), BF16),
            pltpu.VMEM((8, ny, depth), F32),
            pltpu.VMEM((nx, 8, depth), F32),
            pltpu.VMEM((2, depth, depth), BF16),
            pltpu.VMEM(now.shape, F32),
            pltpu.VMEM((nx + 6, slots, depth), BF16),
            pltpu.VMEM((2, groups, 16, depth), BF16),
            pltpu.VMEM((2, 3, ny, depth), BF16),
            pltpu.VMEM((2, groups + 2, 16, depth), BF16),
            pltpu.VMEM((nx + 4, r1 * ch, depth), BF16),
            pltpu.VMEM((nx + 2, r2 * ch, depth), BF16),
            pltpu.VMEM((r1 * ch, 3 * slots), BF16),
            pltpu.VMEM((64, 3 * slots), BF16),
            pltpu.VMEM((3 * blk * ch, 3 * (blk + 2) * ch), BF16),
            pltpu.VMEM((12 * ch, 18 * ch), BF16),
            pltpu.VMEM((3 * ny, 3 * r2 * ch), BF16),
            pltpu.VMEM((1, 128), F32),
            pltpu.VMEM((count - 1, 1, 128), F32),
            pltpu.SemaphoreType.DMA((16,)),
            pltpu.SemaphoreType.DMA((16,)),
            pltpu.SemaphoreType.DMA,
            pltpu.SemaphoreType.DMA,
        ],
        compiler_params=pltpu.CompilerParams(
            collective_id=0, has_side_effects=True, vmem_limit_bytes=40 * 1024 * 1024
        ),
    )(
        *(
            pltpu.with_memory_space_constraint(v, pltpu.HBM)
            for v in (
                speed,
                before,
                now,
                src,
                prior,
                w_first.transpose(1, 2, 0).reshape(ch, 27),
                w_mid.transpose(1, 2, 0).reshape(ch * ch, 27),
                w_last.transpose(2, 1, 0).reshape(ch, 27),
                b_first.reshape(1, ch),
                b_mid.reshape(1, ch),
            )
        )
    )
    return pl.pallas_call(
        functools.partial(hand_on, 8.0 * float(nx * n_gx * ny * n_gy * depth)),
        out_shape=(out,) * 4,
        in_specs=[vmem] * 5,
        out_specs=(hbm,) * 4,
        scratch_shapes=[pltpu.VMEM(now.shape, F32), pltpu.SemaphoreType.DMA((7,))],
    )(*(pltpu.with_memory_space_constraint(v, pltpu.VMEM) for v in (sums, *outs)))


def solution(mesh):
    brick = P("gx", "gy", None)
    return jax.shard_map(
        functools.partial(shards, mesh.shape["gx"], mesh.shape["gy"]),
        mesh=mesh,
        in_specs=(brick, brick, brick, P(None, "gx", "gy", None), brick, P(), P(), P(), P(), P()),
        out_specs=(brick,) * 4,
        check_vma=False,
    )
```
